32 devices in a mesh: expert: 16 (over z, y, x), etp: 2 (over core).
Axes of the slice: x: 2, y: 2, z: 4, core: 2. Of those that a mesh axis runs over, the one named last changes fastest.
Arguments:
- hidden_in: bfloat16 [192, 4096], P('expert', 'etp'), may hold values from -6 to 6
- expert_ids: int32 [192, 8], P('expert'), may hold values from 0 to 15, all different within a row; in each aligned block of 12 rows (0 to 11, 12 to 23, ...) at most 7 rows name the same one
- gate_weights: float32 [192, 8], P('expert'), may hold values from 0.2 to 1
- out_grad: bfloat16 [192, 4096], P('expert', 'etp'), may hold values from -6 to 6
- gate_weight: bfloat16 [16, 4096, 1024], P('expert', None, 'etp'), may hold values from -0.09375 to 0.09375
- up_weight: bfloat16 [16, 4096, 1024], P('expert', None, 'etp'), may hold values from -0.09375 to 0.09375
- down_weight: bfloat16 [16, 1024, 4096], P('expert', 'etp'), may hold values from -0.1875 to 0.1875
Outputs:
- mixed_out: bfloat16 [192, 4096], P('expert', 'etp')
- input_grad: bfloat16 [192, 4096], P('expert', 'etp')
- down_grad: bfloat16 [16, 1024, 4096], P('expert', 'etp')
The draws below stay inside these ranges and needn't reach their ends.
Inputs may be any that keep to these rules, and one draw needn't show every extreme that they name: `expert_ids`: each token names 8 different experts. Within each aligned block of 12 tokens no expert is named by more than 7 tokens, and in some block an expert is named by exactly 7 tokens.
All inputs are finite; a program needn't handle non-finite values.
Results may differ from the reference program's by a relative error of at most 0.018.
Values may be sent and summed in bfloat16 or wider, within the bound.
No kernel may reach another device: no remote copies, remote signals or barrier semaphores. Data moves between devices by JAX's collectives and lax.ppermute only.
A program may use at most 64 MiB of HBM per device.

```python
import math
import jax
import jax.numpy as jnp
import numpy as np
from jax import lax

D = 4096
TOP = 8
F = 1024
TOK = 12
EXPERTS = 16
TOKENS = 192
CAP = 7
N_EXPERT = 16
N_ETP = 2


def block_levels(stream_key, extent, shards, low, top_value):
    def one(dim, blocks):
        draws = jax.random.uniform(jax.random.fold_in(jax.random.fold_in(stream_key, 6), dim), (blocks,), jnp.float32, low / len(shards), top_value / len(shards))
        return jnp.repeat(jnp.exp(draws), extent[dim] // blocks).reshape((-1,) + (1,) * (len(extent) - dim - 1))

    gain = one(*shards[0])
    for cut in shards[1:]:
        gain = gain * one(*cut)
    return gain


def assign_block(stream_key, own, number, rows, amount, top, limit, lean):
    ranking = jax.random.permutation(stream_key, amount)
    crowded, usual = portions_of(amount, rows * top, limit, lean, True), portions_of(amount, rows * top, limit, lean, False)
    places = jnp.arange(amount)

    def named(tallies, turn):
        used = int((tallies > 0).sum())
        fixed = max(1, used // 4)
        shifted = fixed + (places - fixed + turn * (used - fixed)) % max(1, amount - fixed)
        return jnp.zeros((amount,), jnp.int32).at[ranking[jnp.where(places < fixed, places, shifted)]].set(jnp.asarray(tallies, jnp.int32))

    tallies = jnp.where(number % 4 == 0, named(crowded, number // 4), named(usual, number - number // 4 - 1))
    mixed = jax.random.permutation(jax.random.fold_in(own, 3), amount)
    source_of, sink = mixed[0:amount // 2 * 2:2], mixed[1:amount // 2 * 2:2]
    margin = jnp.minimum(tallies[source_of] - 1, limit - tallies[sink]) // 2
    margin = jnp.where((source_of == ranking[0]) | (sink == ranking[0]) | (tallies[sink] == 0), 0, jnp.maximum(margin, 0))
    shifted = jax.random.randint(jax.random.fold_in(own, 4), (amount // 2,), 0, 1 << 20) % (margin + 1)
    tallies = tallies.at[source_of].add(-shifted).at[sink].add(shifted)
    items = jnp.searchsorted(jnp.cumsum(tallies), jnp.arange(rows * top), side="right").astype(jnp.int32)
    grid = items.reshape(top, rows).T
    grid = grid[jax.random.permutation(jax.random.fold_in(own, 1), rows)]
    turn = jax.random.randint(jax.random.fold_in(own, 2), (rows, 1), 0, top)
    return jnp.take_along_axis(grid, (jnp.arange(top)[None, :] + turn) % top, axis=1)


def portions_of(amount, total, bound, skew, full):
    loads = [(1 << 20) // math.isqrt(grade ** skew) + 1 for grade in range(1, amount + 1)]
    largest = bound if full else min(bound, max(-(-total // amount), total * loads[0] // sum(loads)))
    least = 1 if total - largest >= amount - 1 else 0
    holding, surplus = [largest] + [least] * (amount - 1), total - largest - least * (amount - 1)
    while surplus > 0:
        movable = [i for i in range(1, amount) if holding[i] < largest] or [i for i in range(1, amount) if holding[i] < bound]
        mass, left = sum([loads[i] for i in movable]), surplus
        for i in movable:
            extra = min(bound - holding[i], max(1, left * loads[i] // mass), surplus)
            holding[i] = holding[i] + extra
            surplus = surplus - extra
    return np.array(holding)


def gaussian(own_key, extent, scale, reach, shards=(), kind=jnp.bfloat16):
    entries = jax.random.normal(own_key, extent, jnp.float32) * scale
    if len(shards) > 0:
        entries = block_levels(own_key, extent, shards, -0.22, 0.18) * entries
    return jnp.clip(entries, min=-reach, max=reach).astype(kind)


def setup_inputs(seed: int = 0) -> dict:
    keys = jax.random.split(jax.random.key(seed), 8)
    hidden_in = gaussian(keys[0], (TOKENS, D), 1.0, 6.0, ((0, 16), (1, 2)))
    expert_ids_keys = jax.random.split(jax.random.fold_in(keys[1], 1), TOKENS // TOK)
    expert_ids_turns = jax.random.permutation(jax.random.fold_in(keys[1], 3), TOKENS // TOK)
    expert_ids = jax.vmap(lambda own, number: assign_block(jax.random.fold_in(keys[1], 2), own, number, TOK, EXPERTS, TOP, CAP, 2))(expert_ids_keys, expert_ids_turns).reshape((TOKENS, TOP))
    gate_weights = jnp.clip(0.2 + 0.8 * jax.random.uniform(keys[2], (TOKENS, TOP), jnp.float32) ** block_levels(keys[2], (TOKENS, TOP), ((0, 16),), -0.2, 0.2), 0.2, 1.0)
    out_grad = gaussian(keys[3], (TOKENS, D), 1.0, 6.0, ((0, 16), (1, 2)))
    gate_weight = gaussian(keys[4], (EXPERTS, D, F), D ** -0.5, 0.09375, ((0, 16), (2, 2)))
    up_weight = gaussian(keys[5], (EXPERTS, D, F), D ** -0.5, 0.09375, ((0, 16), (2, 2)))
    down_weight = gaussian(keys[6], (EXPERTS, F, D), F ** -0.5, 0.1875, ((0, 16), (1, 2)))
    return dict(hidden_in=hidden_in, expert_ids=expert_ids, gate_weights=gate_weights, out_grad=out_grad, gate_weight=gate_weight, up_weight=up_weight, down_weight=down_weight)


def group_terms(left, right):
    row_count = left.shape[0]
    width = right.shape[0]
    left_groups = left.astype(jnp.float32).reshape(row_count, N_ETP, F // N_ETP)
    right_groups = right.astype(jnp.float32).reshape(width, N_ETP, F // N_ETP)
    return jnp.einsum("rgf,dgf->grd", left_groups, right_groups, precision=lax.Precision.HIGHEST)


def summed_groups(terms):
    rounded = lax.optimization_barrier(terms.astype(jnp.bfloat16))
    return jnp.sum(rounded.astype(jnp.float32), axis=0).astype(jnp.bfloat16)


def reference(hidden_in, expert_ids, gate_weights, out_grad, gate_weight, up_weight, down_weight):
    row_count = N_EXPERT * CAP
    blocks = expert_ids.reshape(N_EXPERT, TOK * TOP)
    onehot = (blocks[:, :, None] == jnp.arange(EXPERTS, dtype=jnp.int32)[None, None, :]).astype(jnp.int32)
    slot_rank = jnp.sum((jnp.cumsum(onehot, axis=1) - onehot) * onehot, axis=2)
    source = jnp.arange(N_EXPERT, dtype=jnp.int32)[:, None]
    position = (blocks * row_count + source * CAP + slot_rank).reshape(-1).astype(jnp.int32)
    filler = jnp.arange(TOKENS * TOP, dtype=jnp.int32) + 1
    table = jnp.zeros((EXPERTS * row_count,), jnp.int32).at[position].set(filler)
    table = table.reshape(EXPERTS, row_count)
    gate_flat = gate_weights.reshape(-1)

    def one_expert(operands):
        entry_code, gate_matrix, up_matrix, down_matrix = operands
        is_live = entry_code > 0
        slot_index = jnp.maximum(entry_code - 1, 0)
        token_index = slot_index // TOP
        rows_in = jnp.where(is_live[:, None], hidden_in[token_index], jnp.zeros((), jnp.bfloat16))
        scaled = (out_grad[token_index].astype(jnp.float32) * gate_flat[slot_index][:, None]).astype(jnp.bfloat16)
        grad_in = jnp.where(is_live[:, None], scaled, jnp.zeros((), jnp.bfloat16))
        gate_pre = jnp.dot(rows_in, gate_matrix, preferred_element_type=jnp.float32)
        up_pre = jnp.dot(rows_in, up_matrix, preferred_element_type=jnp.float32)
        sigmoid_gate = jax.nn.sigmoid(gate_pre)
        swish_gate = gate_pre * sigmoid_gate
        hidden_act = (swish_gate * up_pre).astype(jnp.bfloat16)
        expert_out = summed_groups(group_terms(hidden_act, down_matrix.T))
        act_grad = jnp.dot(grad_in, down_matrix.T, preferred_element_type=jnp.float32)
        down_grad = jnp.dot(hidden_act.T, grad_in, preferred_element_type=jnp.float32).astype(jnp.bfloat16)
        gate_grad = (act_grad * up_pre * sigmoid_gate * (1.0 + gate_pre * (1.0 - sigmoid_gate))).astype(jnp.bfloat16)
        up_grad = (act_grad * swish_gate).astype(jnp.bfloat16)
        slot_dx = summed_groups(group_terms(gate_grad, gate_matrix) + group_terms(up_grad, up_matrix))
        return expert_out, slot_dx, down_grad

    expert_out, slot_dx, down_grad = lax.map(one_expert, (table, gate_weight, up_weight, down_weight))
    picked = expert_out.reshape(-1, D)[position].astype(jnp.float32).reshape(TOKENS, TOP, D)
    mixed_out = jnp.sum(picked * gate_weights[:, :, None], axis=1).astype(jnp.bfloat16)
    returned = slot_dx.reshape(-1, D)[position].astype(jnp.float32).reshape(TOKENS, TOP, D)
    input_grad = jnp.sum(returned, axis=1).astype(jnp.bfloat16)
    return mixed_out, input_grad, down_grad
```

```python
import functools
import jax
import jax.numpy as jnp
from jax import lax
from jax.experimental import pallas as pl
from jax.experimental.pallas import tpu as pltpu
from jax.sharding import PartitionSpec as P

BF16 = jnp.bfloat16
F32 = jnp.float32
META = 128
VMEM_LIMIT = 48 * 1024 * 1024


def group_sizes(experts):
    inner = 1
    while inner * inner * 4 <= experts and experts % (inner * 2) == 0:
        inner *= 2
    return experts // inner, inner


def partner(index, step, size):
    return index ^ step if size & (size - 1) == 0 else (index + step) % size


def origin(index, step, size):
    return index ^ step if size & (size - 1) == 0 else (index - step) % size


def traced_partner(index, step, size):
    return index ^ step if size & (size - 1) == 0 else lax.rem(index + step, size)


def traced_origin(index, step, size):
    return index ^ step if size & (size - 1) == 0 else lax.rem(index + size - step, size)


def send_outer(x, step, outer, inner, back=False):
    move = origin if back else partner
    pairs = [
        (a * inner + b, move(a, step, outer) * inner + b) for a in range(outer) for b in range(inner)
    ]
    return lax.ppermute(x, "expert", pairs)


def send_inner(x, step, outer, inner, back=False):
    move = origin if back else partner
    pairs = [
        (a * inner + b, a * inner + move(b, step, inner)) for a in range(outer) for b in range(inner)
    ]
    return lax.ppermute(x, "expert", pairs)


def send_core(x, step, cores, back=False):
    move = origin if back else partner
    return lax.ppermute(x, "etp", [(i, move(i, step, cores)) for i in range(cores)])


def contract(left, right, left_dim, right_dim):
    return lax.dot_general(
        left, right, (((left_dim,), (right_dim,)), ((), ())), preferred_element_type=F32
    )


def whole_specs(count):
    return [pl.BlockSpec(memory_space=pltpu.VMEM)] * count


def any_specs(count):
    return [pl.BlockSpec(memory_space=pl.ANY)] * count


def params():
    return pltpu.CompilerParams(vmem_limit_bytes=VMEM_LIMIT)


def fold(x):
    half = x.shape[1] // 2
    return jnp.concatenate([x[:, :half], x[:, half:]], axis=0)


def stacked(refs, columns=None):
    parts = [r[...] if columns is None else r[:, columns] for r in refs]
    if len(parts) == 1:
        return parts[0]
    return jnp.concatenate([p.astype(F32) for p in parts], axis=0).astype(BF16)


def count_above(index, unit, total):
    value = jnp.zeros_like(index)
    for m in range(unit, total, unit):
        value = value + (index >= m).astype(jnp.int32)
    return value


def route_kernel(dims, *refs):
    outer, inner, tokens, top, cap, reach, half = dims
    blocks = refs[:outer]
    sends = refs[outer : outer + inner]
    pick_ref, gate_hi_ref, gate_lo_ref, gate_col_ref = refs[outer + inner :]
    rows = outer * 2 * tokens
    slots = inner * reach
    me = lax.axis_index("expert")
    my_inner = lax.rem(me, inner)
    my_base = me - my_inner
    meta = jnp.concatenate([r[:, half:].astype(F32) for r in blocks], axis=0)
    lane = lax.broadcasted_iota(jnp.int32, (rows, slots), 1)
    row = lax.broadcasted_iota(jnp.int32, (rows, slots), 0)
    step = count_above(lane, reach, slots)
    dest = jnp.zeros((rows, slots), F32)
    for q in range(inner):
        expert = (my_base + traced_partner(my_inner, q, inner)).astype(F32)
        dest = jnp.where(step == q, expert, dest)
    slot = lane - step * reach
    named = jnp.zeros((rows, slots), F32)
    gate = jnp.zeros((rows, slots), F32)
    for k in range(top):
        hit = meta[:, k : k + 1] == dest
        value = (
            meta[:, top + k : top + k + 1]
            + meta[:, 2 * top + k : 2 * top + k + 1]
            + meta[:, 3 * top + k : 3 * top + k + 1]
        )
        named = named + hit.astype(F32)
        gate = gate + jnp.where(hit, value, 0.0)
    left = lax.broadcasted_iota(jnp.int32, (rows, rows), 1)
    down = lax.broadcasted_iota(jnp.int32, (rows, rows), 0)
    same = count_above(left, tokens, rows) == count_above(down, tokens, rows)
    before = (same & (left < down)).astype(F32).astype(BF16)
    rank = jnp.dot(before, named.astype(BF16), preferred_element_type=F32)
    position = count_above(row, 2 * tokens, rows) * cap + rank.astype(jnp.int32)
    pick = jnp.where(position == slot, named, 0.0)
    gate = pick * gate
    gate_hi = gate.astype(BF16)
    rest = gate - gate_hi.astype(F32)
    gate_mid = rest.astype(BF16)
    gate_lo = (rest - gate_mid.astype(F32)).astype(BF16)
    part = count_above(row, tokens, rows)
    even = part - 2 * count_above(row, 2 * tokens, rows) == 0
    pick_left = jnp.where(even, pick, 0.0).astype(BF16)
    pick_right = jnp.where(even, 0.0, pick).astype(BF16)
    pick_ref[...] = jnp.concatenate([pick_left, pick_right], axis=1)
    gate_hi_ref[...] = jnp.concatenate(
        [jnp.where(even, gate_hi.astype(F32), 0.0), jnp.where(even, 0.0, gate_hi.astype(F32))], axis=1
    ).astype(BF16)
    gate_lo_ref[...] = jnp.concatenate(
        [jnp.where(even, gate_mid.astype(F32), 0.0), jnp.where(even, 0.0, gate_mid.astype(F32))], axis=1
    ).astype(BF16)
    ones = jnp.ones((rows, META), BF16)
    column = contract(gate_hi, ones, 0, 0) + contract(gate_mid, ones, 0, 0) + contract(gate_lo, ones, 0, 0)
    gate_col_ref[...] = 0.5 * column
    table = stacked(blocks, pl.ds(0, half))
    for side, chosen in enumerate((pick_left, pick_right)):
        out = contract(chosen, table, 0, 0).astype(BF16)
        for q in range(inner):
            sends[q][:, side * half : (side + 1) * half] = out[q * reach : (q + 1) * reach]


def pick_kernel(dims, *refs):
    outer, inner, reach, half = dims
    blocks = refs[:outer]
    pick_ref, gate_col_ref = refs[outer : outer + 2]
    sends = refs[outer + 2 :]
    slots = inner * reach
    table = stacked(blocks)
    scale = gate_col_ref[:, :1]
    for side in range(2):
        out = contract(pick_ref[:, side * slots : (side + 1) * slots], table, 0, 0)
        out = (out * scale).astype(BF16)
        for q in range(inner):
            sends[q][:, side * half : (side + 1) * half] = out[q * reach : (q + 1) * reach]


def start_pieces(pieces, stack, sems):
    reach = pieces[0].shape[0]
    copies = []
    for i, piece in enumerate(pieces):
        copy = pltpu.make_async_copy(piece, stack.at[pl.ds(i * reach, reach), :], sems.at[i])
        copy.start()
        copies.append(copy)
    return copies


def forward_kernel(dims, *refs):
    cores, inner, reach, width = dims
    pieces = refs[: cores * inner]
    gate_hbm, up_hbm, down_hbm = refs[cores * inner : cores * inner + 3]
    outs = refs[cores * inner + 3 :]
    gate_ref, up_ref, act_ref = outs[:3]
    parts = outs[3 : 3 + cores]
    gate_w, up_w, down_w, stack, piece_sems, weight_sems = outs[3 + cores :]
    core = lax.axis_index("etp")
    starts = [traced_partner(core, d, cores) * width for d in range(cores)]
    origins = [traced_origin(core, d, cores) * width for d in range(cores)]
    weights = []
    for d in range(cores):
        for n, (source, target) in enumerate(((gate_hbm, gate_w), (up_hbm, up_w))):
            span = pl.ds(pl.multiple_of(origins[d], width), width)
            copy = pltpu.make_async_copy(source.at[0, span, :], target.at[d], weight_sems.at[2 * d + n])
            copy.start()
            weights.append(copy)
    waits = start_pieces(pieces, stack, piece_sems)
    for d in reversed(range(cores)):
        span = pl.ds(pl.multiple_of(starts[d], width), width)
        copy = pltpu.make_async_copy(down_hbm.at[0, :, span], down_w.at[d], weight_sems.at[2 * cores + d])
        copy.start()
        weights.append(copy)
    gate_pre = None
    up_pre = None
    for d in range(cores):
        for copy in waits[d * inner : (d + 1) * inner]:
            copy.wait()
        rows = stack[d * inner * reach : (d + 1) * inner * reach, :]
        weights[2 * d].wait()
        term = jnp.dot(rows, gate_w[d], preferred_element_type=F32)
        gate_pre = term if gate_pre is None else gate_pre + term
        weights[2 * d + 1].wait()
        term = jnp.dot(rows, up_w[d], preferred_element_type=F32)
        up_pre = term if up_pre is None else up_pre + term
    act = (gate_pre * jax.nn.sigmoid(gate_pre) * up_pre).astype(BF16)
    gate_ref[...] = gate_pre
    up_ref[...] = up_pre
    act_ref[...] = act
    for n, d in enumerate(reversed(range(cores))):
        weights[2 * cores + n].wait()
        parts[d][...] = jnp.dot(act, down_w[d], preferred_element_type=F32).astype(BF16)


def backward_kernel(dims, *refs):
    cores, inner, reach, width = dims
    pieces = refs[: cores * inner]
    gate_hbm, up_hbm, down_hbm, gate_ref, up_ref = refs[cores * inner : cores * inner + 5]
    outs = refs[cores * inner + 5 :]
    parts = outs[:cores]
    gate_w, up_w, down_w, stack, piece_sems, weight_sems = outs[cores:]
    core = lax.axis_index("etp")
    starts = [traced_partner(core, d, cores) * width for d in range(cores)]
    origins = [traced_origin(core, d, cores) * width for d in range(cores)]
    weights = []
    for d in range(cores):
        span = pl.ds(pl.multiple_of(origins[d], width), width)
        copy = pltpu.make_async_copy(down_hbm.at[0, :, span], down_w.at[d], weight_sems.at[2 * cores + d])
        copy.start()
        weights.append(copy)
    waits = start_pieces(pieces, stack, piece_sems)
    for d in reversed(range(cores)):
        for n, (source, target) in enumerate(((gate_hbm, gate_w), (up_hbm, up_w))):
            span = pl.ds(pl.multiple_of(starts[d], width), width)
            copy = pltpu.make_async_copy(source.at[0, span, :], target.at[d], weight_sems.at[2 * d + n])
            copy.start()
            weights.append(copy)
    act_grad = None
    for d in range(cores):
        for copy in waits[d * inner : (d + 1) * inner]:
            copy.wait()
        rows = stack[d * inner * reach : (d + 1) * inner * reach, :]
        weights[d].wait()
        term = contract(rows, down_w[d], 1, 1)
        act_grad = term if act_grad is None else act_grad + term
    gate_pre = gate_ref[...]
    sigmoid = jax.nn.sigmoid(gate_pre)
    gate_grad = (act_grad * up_ref[...] * sigmoid * (1.0 + gate_pre * (1.0 - sigmoid))).astype(BF16)
    up_grad = (act_grad * (gate_pre * sigmoid)).astype(BF16)
    for n, d in enumerate(reversed(range(cores))):
        weights[cores + 2 * n].wait()
        weights[cores + 2 * n + 1].wait()
        part = contract(gate_grad, gate_w[d], 1, 1) + contract(up_grad, up_w[d], 1, 1)
        parts[d][...] = part.astype(BF16)


def down_kernel(dims, *refs):
    cores, inner, reach, width = dims
    pieces = refs[: cores * inner]
    act_ref, out_hbm, stack, result, piece_sems, out_sems = refs[cores * inner :]
    core = lax.axis_index("etp")
    waits = start_pieces(pieces, stack, piece_sems)
    act = act_ref[...]
    copies = []
    for d in range(cores):
        for copy in waits[d * inner : (d + 1) * inner]:
            copy.wait()
        rows = stack[d * inner * reach : (d + 1) * inner * reach, :]
        result[d] = contract(act, rows, 0, 0).astype(BF16)
        span = pl.ds(pl.multiple_of(traced_origin(core, d, cores) * width, width), width)
        copy = pltpu.make_async_copy(result.at[d], out_hbm.at[0, :, span], out_sems.at[d])
        copy.start()
        copies.append(copy)
    for copy in copies:
        copy.wait()


def split_kernel(dims, *refs):
    cores, inner, reach = dims
    total = refs[0][...].astype(F32)
    for part in refs[1:cores]:
        total = total + part[...].astype(F32)
    total = total.astype(BF16)
    for q in range(inner):
        refs[cores + q][...] = total[q * reach : (q + 1) * reach]


def combine_kernel(dims, weighted, *refs):
    outer, inner, unit, half = dims
    pieces = refs[:inner]
    tables = refs[inner : inner + weighted]
    outs = refs[inner + weighted :]
    rows = jnp.concatenate([p[...] for p in pieces], axis=0)
    slots = rows.shape[0]
    total = None
    for table in tables:
        term = jnp.dot(table[:, :slots], rows[:, :half], preferred_element_type=F32)
        term = term + jnp.dot(table[:, slots:], rows[:, half:], preferred_element_type=F32)
        total = term if total is None else total + term
    for b in range(outer):
        outs[b][...] = total[b * unit : (b + 1) * unit].astype(BF16)


def final_kernel(dims, *refs):
    tokens, half = dims
    total = refs[0][...].astype(F32)
    for part in refs[1:-1]:
        total = total + part[...].astype(F32)
    refs[-1][:, :half] = total[:tokens].astype(BF16)
    refs[-1][:, half:] = total[tokens:].astype(BF16)


def shape(rows, columns, kind=BF16):
    return jax.ShapeDtypeStruct((rows, columns), kind)


def on_device(hidden_in, expert_ids, gate_weights, out_grad, gate_weight, up_weight, down_weight):
    tokens, top = expert_ids.shape
    experts = lax.axis_size("expert")
    cores = lax.axis_size("etp")
    outer, inner = group_sizes(experts)
    cap = min(tokens, tokens * top // experts + 1)
    width = hidden_in.shape[1]
    half = width // 2
    hidden = gate_weight.shape[2]
    reach = -(-(outer * cap) // 16) * 16
    rows = inner * reach
    unit = 2 * tokens

    with jax.named_scope("prepare"):
        gate_hi = lax.reduce_precision(gate_weights, 8, 7)
        rest = gate_weights - gate_hi
        gate_mid = lax.reduce_precision(rest, 8, 7)
        meta = jnp.concatenate(
            [expert_ids.astype(F32), gate_hi, gate_mid, rest - gate_mid], axis=1
        ).astype(BF16)
        meta = jnp.pad(meta, ((0, 0), (0, META - 4 * top)))
        packed_in = jnp.concatenate([fold(hidden_in), jnp.concatenate([meta, meta], axis=0)], axis=1)
        packed_grad = fold(out_grad)

    with jax.named_scope("gather_blocks"):
        in_blocks = [packed_in] + [send_outer(packed_in, s, outer, inner) for s in range(1, outer)]
        grad_blocks = [packed_grad] + [send_outer(packed_grad, s, outer, inner) for s in range(1, outer)]

    send_shapes = [shape(reach, width)] * inner
    table_shape = shape(outer * unit, 2 * rows)
    with jax.named_scope("route"):
        routed = pl.pallas_call(
            functools.partial(route_kernel, (outer, inner, tokens, top, cap, reach, half)),
            out_shape=send_shapes + [table_shape] * 3 + [shape(rows, META, F32)],
            in_specs=whole_specs(outer),
            out_specs=whole_specs(inner + 4),
            compiler_params=params(),
            name="route",
        )(*in_blocks)
        in_sends, (pick, gate_hi, gate_lo, gate_col) = routed[:inner], routed[inner:]

    def exchange(sends):
        own = [sends[0]] + [send_inner(sends[q], q, outer, inner) for q in range(1, inner)]
        groups = [own]
        for d in range(1, cores):
            groups.append([send_core(piece, d, cores) for piece in own])
        return [piece for group in groups for piece in group]

    in_pieces = exchange(in_sends)

    with jax.named_scope("scale"):
        grad_sends = pl.pallas_call(
            functools.partial(pick_kernel, (outer, inner, reach, half)),
            out_shape=send_shapes,
            in_specs=whole_specs(outer + 2),
            out_specs=whole_specs(inner),
            compiler_params=params(),
            name="scale",
        )(*grad_blocks, pick, gate_col)
    grad_pieces = exchange(grad_sends)

    dims = (cores, inner, reach, width)
    weight_scratch = [
        pltpu.VMEM((cores, width, hidden), BF16),
        pltpu.VMEM((cores, width, hidden), BF16),
        pltpu.VMEM((cores, hidden, width), BF16),
        pltpu.VMEM((cores * rows, width), BF16),
        pltpu.SemaphoreType.DMA((cores * inner,)),
        pltpu.SemaphoreType.DMA((3 * cores,)),
    ]
    weight_bytes = 2 * (gate_weight.size + up_weight.size + down_weight.size)
    flops = 2 * rows * cores * width * hidden
    with jax.named_scope("forward"):
        gate_pre, up_pre, act, *out_parts = pl.pallas_call(
            functools.partial(forward_kernel, dims),
            out_shape=[shape(rows, hidden, F32)] * 2 + [shape(rows, hidden)] + [shape(rows, width)] * cores,
            in_specs=any_specs(cores * inner + 3),
            out_specs=whole_specs(3 + cores),
            scratch_shapes=weight_scratch,
            compiler_params=params(),
            cost_estimate=pl.CostEstimate(
                flops=3 * flops, bytes_accessed=weight_bytes, transcendentals=rows * hidden
            ),
            name="forward",
        )(*in_pieces, gate_weight, up_weight, down_weight)

    def give_back(parts):
        got = [parts[0]] + [send_core(parts[d], d, cores) for d in range(1, cores)]
        sends = pl.pallas_call(
            functools.partial(split_kernel, (cores, inner, reach)),
            out_shape=send_shapes,
            in_specs=whole_specs(cores),
            out_specs=whole_specs(inner),
            compiler_params=params(),
            name="split",
        )(*got)
        return [sends[0]] + [send_inner(sends[q], q, outer, inner, back=True) for q in range(1, inner)]

    def combine(pieces, tables):
        blocks = pl.pallas_call(
            functools.partial(combine_kernel, (outer, inner, unit, half), len(tables)),
            out_shape=[shape(unit, half)] * outer,
            in_specs=whole_specs(inner + len(tables)),
            out_specs=whole_specs(outer),
            compiler_params=params(),
            name="combine",
        )(*pieces, *tables)
        blocks = [blocks[0]] + [send_outer(blocks[s], s, outer, inner, back=True) for s in range(1, outer)]
        return pl.pallas_call(
            functools.partial(final_kernel, (tokens, half)),
            out_shape=shape(tokens, width),
            in_specs=whole_specs(outer),
            out_specs=pl.BlockSpec(memory_space=pltpu.VMEM),
            compiler_params=params(),
            name="final",
        )(*blocks)

    with jax.named_scope("return_out"):
        mixed_out = combine(give_back(out_parts), (gate_hi, gate_lo))

    with jax.named_scope("backward"):
        grad_parts = pl.pallas_call(
            functools.partial(backward_kernel, dims),
            out_shape=[shape(rows, width)] * cores,
            in_specs=any_specs(cores * inner + 3) + whole_specs(2),
            out_specs=whole_specs(cores),
            scratch_shapes=weight_scratch,
            compiler_params=params(),
            cost_estimate=pl.CostEstimate(
                flops=3 * flops, bytes_accessed=weight_bytes, transcendentals=rows * hidden
            ),
            name="backward",
        )(*grad_pieces, gate_weight, up_weight, down_weight, gate_pre, up_pre)

    with jax.named_scope("return_grad"):
        input_grad = combine(give_back(grad_parts), (pick,))

    with jax.named_scope("down_grad"):
        down_grad = pl.pallas_call(
            functools.partial(down_kernel, dims),
            out_shape=jax.ShapeDtypeStruct(down_weight.shape, BF16),
            in_specs=any_specs(cores * inner) + whole_specs(1),
            out_specs=pl.BlockSpec(memory_space=pl.ANY),
            scratch_shapes=[
                pltpu.VMEM((cores * rows, width), BF16),
                pltpu.VMEM((cores, hidden, width), BF16),
                pltpu.SemaphoreType.DMA((cores * inner,)),
                pltpu.SemaphoreType.DMA((cores,)),
            ],
            compiler_params=params(),
            cost_estimate=pl.CostEstimate(
                flops=flops, bytes_accessed=2 * down_weight.size, transcendentals=0
            ),
            name="down_grad",
        )(*grad_pieces, act)
    return (mixed_out, input_grad, down_grad)


def solution(mesh):
    return jax.shard_map(
        on_device,
        mesh=mesh,
        in_specs=(
            P("expert", "etp"),
            P("expert", None),
            P("expert", None),
            P("expert", "etp"),
            P("expert", None, "etp"),
            P("expert", None, "etp"),
            P("expert", "etp", None),
        ),
        out_specs=(P("expert", "etp"), P("expert", "etp"), P("expert", "etp", None)),
        check_vma=False,
    )
```

```python
import functools
import jax
import jax.numpy as jnp
from jax import lax
from jax.experimental import pallas as pl
from jax.experimental.pallas import tpu as pltpu
from jax.sharding import PartitionSpec as P

BF16 = jnp.bfloat16
F32 = jnp.float32
META = 128
VMEM_LIMIT = 20 * 1024 * 1024


def group_sizes(experts):
    inner = 1
    while inner * inner * 4 <= experts and experts % (inner * 2) == 0:
        inner *= 2
    return experts // inner, inner


def partner(index, step, size):
    return index ^ step if size & (size - 1) == 0 else (index + step) % size


def origin(index, step, size):
    return index ^ step if size & (size - 1) == 0 else (index - step) % size


def traced_partner(index, step, size):
    return index ^ step if size & (size - 1) == 0 else lax.rem(index + step, size)


def traced_origin(index, step, size):
    return index ^ step if size & (size - 1) == 0 else lax.rem(index + size - step, size)


def send_outer(x, step, outer, inner, back=False):
    move = origin if back else partner
    pairs = [
        (a * inner + b, move(a, step, outer) * inner + b) for a in range(outer) for b in range(inner)
    ]
    return lax.ppermute(x, "expert", pairs)


def send_inner(x, step, outer, inner, back=False):
    move = origin if back else partner
    pairs = [
        (a * inner + b, a * inner + move(b, step, inner)) for a in range(outer) for b in range(inner)
    ]
    return lax.ppermute(x, "expert", pairs)


def send_core(x, step, cores, back=False):
    move = origin if back else partner
    return lax.ppermute(x, "etp", [(i, move(i, step, cores)) for i in range(cores)])


def send_order(count):
    return range(1, count)


def gather_outer(x, outer, inner):
    sent = {s: send_outer(x, s, outer, inner) for s in send_order(outer)}
    return [x] + [sent[s] for s in range(1, outer)]


def contract(left, right, left_dim, right_dim):
    return lax.dot_general(
        left, right, (((left_dim,), (right_dim,)), ((), ())), preferred_element_type=F32
    )


def whole_specs(count):
    return [pl.BlockSpec(memory_space=pltpu.VMEM)] * count


def any_specs(count):
    return [pl.BlockSpec(memory_space=pl.ANY)] * count


def params():
    return pltpu.CompilerParams(vmem_limit_bytes=VMEM_LIMIT)


def in_hbm(x):
    return pltpu.with_memory_space_constraint(x, pltpu.HBM)


def hbm_specs(count):
    return [pl.BlockSpec(memory_space=pltpu.HBM)] * count


def prepare_kernel(dims, *refs):
    tokens, top, half = dims
    sources, out_ref, held, sems = refs[:4], refs[4], refs[5:9], refs[9]
    copies = [pltpu.make_async_copy(a, b, sems.at[n]) for n, (a, b) in enumerate(zip(sources, held))]
    for copy in copies:
        copy.start()
    for copy in copies:
        copy.wait()
    ids_ref, gates_ref, hidden_ref, grad_ref = held
    gates = gates_ref[...]
    gate_hi = gates.astype(BF16)
    rest = gates - gate_hi.astype(F32)
    gate_mid = rest.astype(BF16)
    gate_lo = (rest - gate_mid.astype(F32)).astype(BF16)
    meta = jnp.zeros((tokens, META), F32)
    entry = lax.broadcasted_iota(jnp.int32, (top, META), 0)
    lane = lax.broadcasted_iota(jnp.int32, (top, META), 1)
    for n, value in enumerate((ids_ref[...].astype(F32).astype(BF16), gate_hi, gate_mid, gate_lo)):
        spread = (lane == entry + n * top).astype(F32).astype(BF16)
        meta = meta + contract(value, spread, 0, 0)
    unit = 2 * tokens
    row = lax.broadcasted_iota(jnp.int32, (unit, tokens), 0)
    token = lax.broadcasted_iota(jnp.int32, (unit, tokens), 1)
    upper = (row == token).astype(F32).astype(BF16)
    lower = (row == token + tokens).astype(F32).astype(BF16)
    for n, source in enumerate((hidden_ref, grad_ref)):
        value = jnp.dot(upper, source[:, :half], preferred_element_type=F32)
        value = value + jnp.dot(lower, source[:, half:], preferred_element_type=F32)
        out_ref[:, n * half : (n + 1) * half] = value.astype(BF16)
    out_ref[:, 2 * half :] = jnp.dot(upper + lower, meta.astype(BF16), preferred_element_type=F32).astype(BF16)


def stacked(refs, columns=None):
    parts = [r[...] if columns is None else r[:, columns] for r in refs]
    if len(parts) == 1:
        return parts[0]
    return jnp.concatenate([p.astype(F32) for p in parts], axis=0).astype(BF16)


def count_above(index, unit, total):
    value = jnp.zeros_like(index)
    for m in range(unit, total, unit):
        value = value + (index >= m).astype(jnp.int32)
    return value


def route_kernel(dims, *refs):
    outer, inner, tokens, top, cap, reach, half = dims
    blocks = refs[:outer]
    sends = refs[outer + 1 : outer + 1 + inner]
    pick_ref, gate_hi_ref, gate_lo_ref = refs[outer + 1 + inner :]
    rows = outer * 2 * tokens
    slots = inner * reach
    me = lax.axis_index("expert")
    my_inner = lax.rem(me, inner)
    my_base = me - my_inner
    meta = jnp.concatenate([r[:, 2 * half :].astype(F32) for r in blocks], axis=0)
    lane = lax.broadcasted_iota(jnp.int32, (rows, slots), 1)
    row = lax.broadcasted_iota(jnp.int32, (rows, slots), 0)
    step = count_above(lane, reach, slots)
    dest = jnp.zeros((rows, slots), F32)
    for q in range(inner):
        expert = (my_base + traced_partner(my_inner, q, inner)).astype(F32)
        dest = jnp.where(step == q, expert, dest)
    slot = lane - step * reach
    named = jnp.zeros((rows, slots), F32)
    gate = jnp.zeros((rows, slots), F32)
    for k in range(top):
        hit = meta[:, k : k + 1] == dest
        value = (
            meta[:, top + k : top + k + 1]
            + meta[:, 2 * top + k : 2 * top + k + 1]
            + meta[:, 3 * top + k : 3 * top + k + 1]
        )
        named = named + hit.astype(F32)
        gate = gate + jnp.where(hit, value, 0.0)
    left = lax.broadcasted_iota(jnp.int32, (rows, rows), 1)
    down = lax.broadcasted_iota(jnp.int32, (rows, rows), 0)
    same = count_above(left, tokens, rows) == count_above(down, tokens, rows)
    before = (same & (left < down)).astype(F32).astype(BF16)
    rank = jnp.dot(before, named.astype(BF16), preferred_element_type=F32)
    position = count_above(row, 2 * tokens, rows) * cap + rank.astype(jnp.int32)
    pick = jnp.where(position == slot, named, 0.0)
    gate = pick * gate
    gate_hi = gate.astype(BF16)
    rest = gate - gate_hi.astype(F32)
    gate_mid = rest.astype(BF16)
    gate_lo = (rest - gate_mid.astype(F32)).astype(BF16)
    part = count_above(row, tokens, rows)
    even = part - 2 * count_above(row, 2 * tokens, rows) == 0
    pick_left = jnp.where(even, pick, 0.0).astype(BF16)
    pick_right = jnp.where(even, 0.0, pick).astype(BF16)
    pick_ref[...] = jnp.concatenate([pick_left, pick_right], axis=1)
    gate_hi_ref[...] = jnp.concatenate(
        [jnp.where(even, gate_hi.astype(F32), 0.0), jnp.where(even, 0.0, gate_hi.astype(F32))], axis=1
    ).astype(BF16)
    gate_lo_ref[...] = jnp.concatenate(
        [jnp.where(even, gate_mid.astype(F32), 0.0), jnp.where(even, 0.0, gate_mid.astype(F32))], axis=1
    ).astype(BF16)
    ones = jnp.ones((rows, META), BF16)
    column = contract(gate_hi, ones, 0, 0) + contract(gate_mid, ones, 0, 0) + contract(gate_lo, ones, 0, 0)
    scale = 0.5 * column[:, :1]
    for array in range(2):
        table = stacked(blocks, pl.ds(array * half, half))
        for side, chosen in enumerate((pick_left, pick_right)):
            out = contract(chosen, table, 0, 0)
            out = (out * scale if array else out).astype(BF16)
            for q in range(inner):
                start = (2 * array + side) * half
                sends[q][:, start : start + half] = out[q * reach : (q + 1) * reach]


def load_kernel(parts, *refs):
    sources, targets, turned, sems = refs[:3], refs[4:7], refs[7:10], refs[11]
    copies = []
    for n in range(3):
        step = sources[n].shape[1] // parts
        for m in range(parts):
            index = (0, pl.ds(m * step, step))
            copy = pltpu.make_async_copy(sources[n].at[index], targets[n].at[index], sems.at[n * parts + m])
            copy.start()
            copies.append(copy)
    for n in range(3):
        step = sources[n].shape[1] // parts
        for m in range(parts):
            copies[n * parts + m].wait()
            turned[n][:, m * step : (m + 1) * step] = targets[n][0, m * step : (m + 1) * step, :].T


def piece_rows(pieces, d, inner, columns):
    return jnp.concatenate([p[:, columns] for p in pieces[d * inner : (d + 1) * inner]], axis=0)


def core_spans(cores, width, move):
    core = lax.axis_index("etp")
    return [pl.ds(pl.multiple_of(move(core, d, cores) * width, width), width) for d in range(cores)]


def forward_kernel(dims, *refs):
    cores, inner, width = dims
    pieces = refs[: cores * inner]
    gate_w, up_w, down_w = refs[cores * inner : cores * inner + 3]
    gate_ref, up_ref, act_ref, *parts = refs[cores * inner + 3 :]
    spans = core_spans(cores, width, traced_origin)
    gate_pre = None
    up_pre = None
    for d in range(cores):
        rows = piece_rows(pieces, d, inner, pl.ds(0, width))
        term = jnp.dot(rows, gate_w[0, spans[d], :], preferred_element_type=F32)
        gate_pre = term if gate_pre is None else gate_pre + term
        term = jnp.dot(rows, up_w[0, spans[d], :], preferred_element_type=F32)
        up_pre = term if up_pre is None else up_pre + term
    act = (gate_pre * jax.nn.sigmoid(gate_pre) * up_pre).astype(BF16)
    gate_ref[...] = gate_pre
    up_ref[...] = up_pre
    act_ref[...] = act
    spans = core_spans(cores, width, traced_partner)
    for d in reversed(range(cores)):
        parts[d][...] = jnp.dot(act, down_w[0, :, spans[d]], preferred_element_type=F32).astype(BF16)


def backward_kernel(dims, *refs):
    cores, inner, width = dims
    pieces = refs[: cores * inner]
    gate_t, up_t, down_t, gate_ref, up_ref = refs[cores * inner : cores * inner + 5]
    parts = refs[-cores:]
    spans = core_spans(cores, width, traced_origin)
    act_grad = None
    for d in range(cores):
        rows = piece_rows(pieces, d, inner, pl.ds(width, width))
        term = jnp.dot(rows, down_t[spans[d], :], preferred_element_type=F32)
        act_grad = term if act_grad is None else act_grad + term
    gate_pre = gate_ref[...]
    sigmoid = jax.nn.sigmoid(gate_pre)
    gate_grad = (act_grad * up_ref[...] * sigmoid * (1.0 + gate_pre * (1.0 - sigmoid))).astype(BF16)
    up_grad = (act_grad * (gate_pre * sigmoid)).astype(BF16)
    spans = core_spans(cores, width, traced_partner)
    for d in reversed(range(cores)):
        part = jnp.dot(gate_grad, gate_t[:, spans[d]], preferred_element_type=F32)
        part = part + jnp.dot(up_grad, up_t[:, spans[d]], preferred_element_type=F32)
        parts[d][...] = part.astype(BF16)


def down_kernel(dims, chunks, *refs):
    cores, inner, width = dims
    pieces = refs[: cores * inner]
    act_ref = refs[cores * inner]
    out_hbm, result, out_sems = refs[-3:]
    core = lax.axis_index("etp")
    act = act_ref[...]
    chunk = width // chunks
    copies = []
    for d in range(cores):
        rows = piece_rows(pieces, d, inner, pl.ds(width, width))
        base = traced_origin(core, d, cores) * width
        for n in range(chunks):
            result[d * chunks + n] = contract(act, rows[:, n * chunk : (n + 1) * chunk], 0, 0).astype(BF16)
            span = pl.ds(pl.multiple_of(base + n * chunk, chunk), chunk)
            copy = pltpu.make_async_copy(
                result.at[d * chunks + n], out_hbm.at[0, :, span], out_sems.at[d * chunks + n]
            )
            copy.start()
            copies.append(copy)
    for copy in copies:
        copy.wait()


def split_kernel(dims, *refs):
    cores, inner, reach = dims
    total = refs[0][...].astype(F32)
    for part in refs[1:cores]:
        total = total + part[...].astype(F32)
    total = total.astype(BF16)
    for q in range(inner):
        refs[q - inner][...] = total[q * reach : (q + 1) * reach]


def combine_kernel(dims, weighted, *refs):
    outer, inner, unit, half = dims
    pieces = refs[:inner]
    tables = refs[inner : inner + weighted]
    outs = refs[-outer:]
    rows = jnp.concatenate([p[...] for p in pieces], axis=0)
    slots = rows.shape[0]
    total = None
    for table in tables:
        term = jnp.dot(table[:, :slots], rows[:, :half], preferred_element_type=F32)
        term = term + jnp.dot(table[:, slots:], rows[:, half:], preferred_element_type=F32)
        total = term if total is None else total + term
    for b in range(outer):
        outs[b][...] = total[b * unit : (b + 1) * unit].astype(BF16)


def final_kernel(dims, *refs):
    outer, tokens, half = dims
    out_ref = refs[-2]
    total = refs[0][...].astype(F32)
    for part in refs[1:outer]:
        total = total + part[...].astype(F32)
    out_ref[:, :half] = total[:tokens].astype(BF16)
    out_ref[:, half:] = total[tokens:].astype(BF16)


def shape(rows, columns, kind=BF16):
    return jax.ShapeDtypeStruct((rows, columns), kind)


def on_device(hidden_in, expert_ids, gate_weights, out_grad, gate_weight, up_weight, down_weight):
    tokens, top = expert_ids.shape
    experts = lax.axis_size("expert")
    cores = lax.axis_size("etp")
    outer, inner = group_sizes(experts)
    cap = min(tokens, tokens * top // experts + 1)
    width = hidden_in.shape[1]
    half = width // 2
    hidden = gate_weight.shape[2]
    reach = -(-(outer * cap) // 16) * 16
    rows = inner * reach
    unit = 2 * tokens

    with jax.named_scope("prepare"):
        packed = pl.pallas_call(
            functools.partial(prepare_kernel, (tokens, top, half)),
            out_shape=shape(unit, 2 * half + META),
            in_specs=hbm_specs(4),
            out_specs=pl.BlockSpec(memory_space=pltpu.VMEM),
            scratch_shapes=[
                pltpu.VMEM((top, tokens), jnp.int32),
                pltpu.VMEM((top, tokens), F32),
                pltpu.VMEM((tokens, width), BF16),
                pltpu.VMEM((tokens, width), BF16),
                pltpu.SemaphoreType.DMA((4,)),
            ],
            compiler_params=params(),
            name="prepare",
        )(in_hbm(expert_ids.T), in_hbm(gate_weights.T), in_hbm(hidden_in), in_hbm(out_grad))

    with jax.named_scope("gather_blocks"):
        blocks = gather_outer(packed, outer, inner)

    table_shape = shape(outer * unit, 2 * rows)
    with jax.named_scope("load_weights"):
        weights = (gate_weight, up_weight, down_weight)
        weight_parts = 4
        held = pl.pallas_call(
            functools.partial(load_kernel, weight_parts),
            out_shape=[pltpu.VMEM(w.shape, BF16) for w in weights]
            + [pltpu.VMEM((w.shape[2], w.shape[1]), BF16) for w in weights]
            + [shape(8, META, F32)],
            in_specs=hbm_specs(3) + whole_specs(1),
            out_specs=whole_specs(7),
            scratch_shapes=[pltpu.SemaphoreType.DMA((3 * weight_parts,))],
            compiler_params=params(),
            cost_estimate=pl.CostEstimate(
                flops=0, bytes_accessed=6 * sum(w.size for w in weights), transcendentals=0
            ),
            name="load_weights",
        )(*[in_hbm(w) for w in weights], packed)
        weights, turned = held[:3], held[3:6]

    with jax.named_scope("route"):
        routed = pl.pallas_call(
            functools.partial(route_kernel, (outer, inner, tokens, top, cap, reach, half)),
            out_shape=[shape(reach, 2 * width)] * inner + [table_shape] * 3,
            in_specs=whole_specs(outer + 1),
            out_specs=whole_specs(inner + 3),
            compiler_params=params(),
            name="route",
        )(*blocks, held[6])
        sends, (pick, gate_hi, gate_lo) = routed[:inner], routed[inner:]

    with jax.named_scope("exchange"):
        pieces = [sends[0]] + [send_inner(sends[q], q, outer, inner) for q in range(1, inner)]
        pieces = pieces + [send_core(piece, d, cores) for d in range(1, cores) for piece in pieces]

    dims = (cores, inner, width)
    with jax.named_scope("forward"):
        gate_pre, up_pre, act, *out_parts = pl.pallas_call(
            functools.partial(forward_kernel, dims),
            out_shape=[shape(rows, hidden, F32)] * 2 + [shape(rows, hidden)] + [shape(rows, width)] * cores,
            in_specs=whole_specs(cores * inner + 3),
            out_specs=whole_specs(3 + cores),
            compiler_params=params(),
            name="forward",
        )(*pieces, *weights)

    def give_back(parts, after=()):
        got = [parts[0]] + [send_core(parts[d], d, cores) for d in range(1, cores)]
        sends = pl.pallas_call(
            functools.partial(split_kernel, (cores, inner, reach)),
            out_shape=[shape(reach, width)] * inner,
            in_specs=whole_specs(cores) + any_specs(len(after)),
            out_specs=whole_specs(inner),
            compiler_params=params(),
            name="split",
        )(*got, *after)
        return [sends[0]] + [send_inner(sends[q], q, outer, inner, back=True) for q in range(1, inner)]

    def combine(pieces, tables):
        blocks = pl.pallas_call(
            functools.partial(combine_kernel, (outer, inner, unit, half), len(tables)),
            out_shape=[shape(unit, half)] * outer,
            in_specs=whole_specs(inner + len(tables)),
            out_specs=whole_specs(outer),
            compiler_params=params(),
            name="combine",
        )(*pieces, *tables)
        return [blocks[0]] + [send_outer(blocks[s], s, outer, inner, back=True) for s in send_order(outer)]

    def finish(blocks, after=()):
        return pl.pallas_call(
            functools.partial(final_kernel, (outer, tokens, half)),
            out_shape=[shape(tokens, width), shape(8, META, F32)],
            in_specs=whole_specs(outer + len(after)),
            out_specs=whole_specs(2),
            compiler_params=params(),
            name="final",
        )(*blocks, *after)

    with jax.named_scope("return_out"):
        out_back = give_back(out_parts)
        out_blocks = combine(out_back, (gate_hi, gate_lo))

    with jax.named_scope("backward"):
        grad_parts = pl.pallas_call(
            functools.partial(backward_kernel, dims),
            out_shape=[shape(rows, width)] * cores,
            in_specs=whole_specs(cores * inner + 5),
            out_specs=whole_specs(cores),
            compiler_params=params(),
            name="backward",
        )(*pieces, *turned, gate_pre, up_pre)

    with jax.named_scope("return_grad"):
        back_blocks = combine(give_back(grad_parts, out_back[:1]), (pick,))

    with jax.named_scope("down_grad"):
        chunks = max(1, width // 512)
        down_grad = pl.pallas_call(
            functools.partial(down_kernel, dims, chunks),
            out_shape=pltpu.HBM(down_weight.shape, BF16),
            in_specs=whole_specs(cores * inner + 1) + any_specs(1),
            out_specs=pl.BlockSpec(memory_space=pltpu.HBM),
            scratch_shapes=[
                pltpu.VMEM((cores * chunks, hidden, width // chunks), BF16),
                pltpu.SemaphoreType.DMA((cores * chunks,)),
            ],
            compiler_params=params(),
            name="down_grad",
        )(*pieces, act, back_blocks[0])

    mixed_out, done = finish(out_blocks)
    input_grad, done = finish(back_blocks, (done,))
    return (mixed_out, input_grad, down_grad)


def solution(mesh):
    return jax.shard_map(
        on_device,
        mesh=mesh,
        in_specs=(
            P("expert", "etp"),
            P("expert", None),
            P("expert", None),
            P("expert", "etp"),
            P("expert", None, "etp"),
            P("expert", None, "etp"),
            P("expert", "etp", None),
        ),
        out_specs=(P("expert", "etp"), P("expert", "etp"), P("expert", "etp", None)),
        check_vma=False,
    )
```

```python
import functools
import jax
import jax.numpy as jnp
from jax import lax
from jax.experimental import pallas as pl
from jax.experimental.pallas import tpu as pltpu
from jax.sharding import PartitionSpec as P

BF16 = jnp.bfloat16
F32 = jnp.float32
META = 128
VMEM_LIMIT = 20 * 1024 * 1024


def group_sizes(experts):
    inner = 1
    while inner * inner * 4 <= experts and experts % (inner * 2) == 0:
        inner *= 2
    return experts // inner, inner


def partner(index, step, size):
    return index ^ step if size & (size - 1) == 0 else (index + step) % size


def origin(index, step, size):
    return index ^ step if size & (size - 1) == 0 else (index - step) % size


def traced_partner(index, step, size):
    return index ^ step if size & (size - 1) == 0 else lax.rem(index + step, size)


def traced_origin(index, step, size):
    return index ^ step if size & (size - 1) == 0 else lax.rem(index + size - step, size)


def send_outer(x, step, outer, inner, back=False):
    move = origin if back else partner
    pairs = [
        (a * inner + b, move(a, step, outer) * inner + b) for a in range(outer) for b in range(inner)
    ]
    return lax.ppermute(x, "expert", pairs)


def send_inner(x, step, outer, inner, back=False):
    move = origin if back else partner
    pairs = [
        (a * inner + b, a * inner + move(b, step, inner)) for a in range(outer) for b in range(inner)
    ]
    return lax.ppermute(x, "expert", pairs)


def send_core(x, step, cores, back=False):
    move = origin if back else partner
    return lax.ppermute(x, "etp", [(i, move(i, step, cores)) for i in range(cores)])


def send_order(count):
    return range(1, count)


def gather_outer(x, outer, inner):
    sent = {s: send_outer(x, s, outer, inner) for s in send_order(outer)}
    return [x] + [sent[s] for s in range(1, outer)]


def contract(left, right, left_dim, right_dim):
    return lax.dot_general(
        left, right, (((left_dim,), (right_dim,)), ((), ())), preferred_element_type=F32
    )


def whole_specs(count):
    return [pl.BlockSpec(memory_space=pltpu.VMEM)] * count


def any_specs(count):
    return [pl.BlockSpec(memory_space=pl.ANY)] * count


def params():
    return pltpu.CompilerParams(vmem_limit_bytes=VMEM_LIMIT)


def in_hbm(x):
    return pltpu.with_memory_space_constraint(x, pltpu.HBM)


def hbm_specs(count):
    return [pl.BlockSpec(memory_space=pltpu.HBM)] * count


def prepare_kernel(dims, *refs):
    tokens, top, half = dims
    sources, out_ref, held, sems = refs[:4], refs[4], refs[5:9], refs[9]
    copies = [pltpu.make_async_copy(a, b, sems.at[n]) for n, (a, b) in enumerate(zip(sources, held))]
    for copy in copies:
        copy.start()
    for copy in copies:
        copy.wait()
    ids_ref, gates_ref, hidden_ref, grad_ref = held
    gates = gates_ref[...]
    gate_hi = gates.astype(BF16)
    rest = gates - gate_hi.astype(F32)
    gate_mid = rest.astype(BF16)
    gate_lo = (rest - gate_mid.astype(F32)).astype(BF16)
    meta = jnp.zeros((tokens, META), F32)
    entry = lax.broadcasted_iota(jnp.int32, (top, META), 0)
    lane = lax.broadcasted_iota(jnp.int32, (top, META), 1)
    for n, value in enumerate((ids_ref[...].astype(F32).astype(BF16), gate_hi, gate_mid, gate_lo)):
        spread = (lane == entry + n * top).astype(F32).astype(BF16)
        meta = meta + contract(value, spread, 0, 0)
    unit = 2 * tokens
    row = lax.broadcasted_iota(jnp.int32, (unit, tokens), 0)
    token = lax.broadcasted_iota(jnp.int32, (unit, tokens), 1)
    upper = (row == token).astype(F32).astype(BF16)
    lower = (row == token + tokens).astype(F32).astype(BF16)
    for n, source in enumerate((hidden_ref, grad_ref)):
        value = jnp.dot(upper, source[:, :half], preferred_element_type=F32)
        value = value + jnp.dot(lower, source[:, half:], preferred_element_type=F32)
        out_ref[:, n * half : (n + 1) * half] = value.astype(BF16)
    out_ref[:, 2 * half :] = jnp.dot(upper + lower, meta.astype(BF16), preferred_element_type=F32).astype(BF16)


def stacked(refs, columns=None):
    parts = [r[...] if columns is None else r[:, columns] for r in refs]
    if len(parts) == 1:
        return parts[0]
    return jnp.concatenate([p.astype(F32) for p in parts], axis=0).astype(BF16)


def count_above(index, unit, total):
    value = jnp.zeros_like(index)
    for m in range(unit, total, unit):
        value = value + (index >= m).astype(jnp.int32)
    return value


def route_kernel(dims, *refs):
    outer, inner, tokens, top, cap, reach, half = dims
    blocks = refs[:outer]
    sends = refs[outer + 1 : outer + 1 + inner]
    pick_ref, gate_hi_ref, gate_lo_ref, gate_col_ref = refs[outer + 1 + inner :]
    rows = outer * 2 * tokens
    slots = inner * reach
    me = lax.axis_index("expert")
    my_inner = lax.rem(me, inner)
    my_base = me - my_inner
    meta = jnp.concatenate([r[:, 2 * half :].astype(F32) for r in blocks], axis=0)
    lane = lax.broadcasted_iota(jnp.int32, (rows, slots), 1)
    row = lax.broadcasted_iota(jnp.int32, (rows, slots), 0)
    step = count_above(lane, reach, slots)
    dest = jnp.zeros((rows, slots), F32)
    for q in range(inner):
        expert = (my_base + traced_partner(my_inner, q, inner)).astype(F32)
        dest = jnp.where(step == q, expert, dest)
    slot = lane - step * reach
    named = jnp.zeros((rows, slots), F32)
    gate = jnp.zeros((rows, slots), F32)
    for k in range(top):
        hit = meta[:, k : k + 1] == dest
        value = (
            meta[:, top + k : top + k + 1]
            + meta[:, 2 * top + k : 2 * top + k + 1]
            + meta[:, 3 * top + k : 3 * top + k + 1]
        )
        named = named + hit.astype(F32)
        gate = gate + jnp.where(hit, value, 0.0)
    left = lax.broadcasted_iota(jnp.int32, (rows, rows), 1)
    down = lax.broadcasted_iota(jnp.int32, (rows, rows), 0)
    same = count_above(left, tokens, rows) == count_above(down, tokens, rows)
    before = (same & (left < down)).astype(F32).astype(BF16)
    rank = jnp.dot(before, named.astype(BF16), preferred_element_type=F32)
    position = count_above(row, 2 * tokens, rows) * cap + rank.astype(jnp.int32)
    pick = jnp.where(position == slot, named, 0.0)
    gate = pick * gate
    gate_hi = gate.astype(BF16)
    rest = gate - gate_hi.astype(F32)
    gate_mid = rest.astype(BF16)
    gate_lo = (rest - gate_mid.astype(F32)).astype(BF16)
    part = count_above(row, tokens, rows)
    even = part - 2 * count_above(row, 2 * tokens, rows) == 0
    pick_left = jnp.where(even, pick, 0.0).astype(BF16)
    pick_right = jnp.where(even, 0.0, pick).astype(BF16)
    pick_ref[...] = jnp.concatenate([pick_left, pick_right], axis=1)
    gate_hi_ref[...] = jnp.concatenate(
        [jnp.where(even, gate_hi.astype(F32), 0.0), jnp.where(even, 0.0, gate_hi.astype(F32))], axis=1
    ).astype(BF16)
    gate_lo_ref[...] = jnp.concatenate(
        [jnp.where(even, gate_mid.astype(F32), 0.0), jnp.where(even, 0.0, gate_mid.astype(F32))], axis=1
    ).astype(BF16)
    ones = jnp.ones((rows, META), BF16)
    column = contract(gate_hi, ones, 0, 0) + contract(gate_mid, ones, 0, 0) + contract(gate_lo, ones, 0, 0)
    gate_col_ref[...] = 0.5 * column
    select_rows(blocks, 0, pick_ref, None, sends)


def select_rows(blocks, array, pick_ref, scale, sends):
    inner = len(sends)
    reach, width = sends[0].shape
    half = width // 2
    slots = inner * reach
    table = stacked(blocks, pl.ds(array * half, half))
    for side in range(2):
        out = contract(pick_ref[:, side * slots : (side + 1) * slots], table, 0, 0)
        out = (out if scale is None else out * scale).astype(BF16)
        for q in range(inner):
            sends[q][:, side * half : (side + 1) * half] = out[q * reach : (q + 1) * reach]


def scale_kernel(outer, inner, *refs):
    pick_ref, gate_col_ref = refs[outer : outer + 2]
    select_rows(refs[:outer], 1, pick_ref, gate_col_ref[:, :1], refs[-inner:])


def stack_kernel(inner, *refs):
    reach = refs[0].shape[0]
    for q in range(inner):
        refs[-1][q * reach : (q + 1) * reach, :] = refs[q][...]


def load_kernel(parts, *refs):
    sources, targets, turned, sems = refs[:3], refs[4:7], refs[7:10], refs[11]
    copies = []
    for n in range(3):
        step = sources[n].shape[1] // parts
        for m in range(parts):
            index = (0, pl.ds(m * step, step))
            copy = pltpu.make_async_copy(sources[n].at[index], targets[n].at[index], sems.at[n * parts + m])
            copy.start()
            copies.append(copy)
    for n in range(3):
        step = sources[n].shape[1] // parts
        for m in range(parts):
            copies[n * parts + m].wait()
            turned[n][:, m * step : (m + 1) * step] = targets[n][0, m * step : (m + 1) * step, :].T


def core_spans(cores, width, move):
    core = lax.axis_index("etp")
    return [pl.ds(pl.multiple_of(move(core, d, cores) * width, width), width) for d in range(cores)]


def forward_kernel(dims, *refs):
    cores, width = dims
    pieces = refs[:cores]
    gate_w, up_w, down_w = refs[cores : cores + 3]
    gate_ref, up_ref, act_ref, *parts = refs[-(3 + cores) :]
    spans = core_spans(cores, width, traced_origin)
    gate_pre = None
    up_pre = None
    for d in range(cores):
        rows = pieces[d][...]
        term = jnp.dot(rows, gate_w[0, spans[d], :], preferred_element_type=F32)
        gate_pre = term if gate_pre is None else gate_pre + term
        term = jnp.dot(rows, up_w[0, spans[d], :], preferred_element_type=F32)
        up_pre = term if up_pre is None else up_pre + term
    act = (gate_pre * jax.nn.sigmoid(gate_pre) * up_pre).astype(BF16)
    gate_ref[...] = gate_pre
    up_ref[...] = up_pre
    act_ref[...] = act
    spans = core_spans(cores, width, traced_partner)
    for d in reversed(range(cores)):
        parts[d][...] = jnp.dot(act, down_w[0, :, spans[d]], preferred_element_type=F32).astype(BF16)


def backward_kernel(dims, *refs):
    cores, width = dims
    pieces = refs[:cores]
    gate_t, up_t, down_t, gate_ref, up_ref = refs[cores : cores + 5]
    parts = refs[-cores:]
    spans = core_spans(cores, width, traced_origin)
    act_grad = None
    for d in range(cores):
        rows = pieces[d][...]
        term = jnp.dot(rows, down_t[spans[d], :], preferred_element_type=F32)
        act_grad = term if act_grad is None else act_grad + term
    gate_pre = gate_ref[...]
    sigmoid = jax.nn.sigmoid(gate_pre)
    gate_grad = (act_grad * up_ref[...] * sigmoid * (1.0 + gate_pre * (1.0 - sigmoid))).astype(BF16)
    up_grad = (act_grad * (gate_pre * sigmoid)).astype(BF16)
    spans = core_spans(cores, width, traced_partner)
    for d in reversed(range(cores)):
        part = jnp.dot(gate_grad, gate_t[:, spans[d]], preferred_element_type=F32)
        part = part + jnp.dot(up_grad, up_t[:, spans[d]], preferred_element_type=F32)
        parts[d][...] = part.astype(BF16)


def down_kernel(dims, chunks, *refs):
    cores, width = dims
    pieces = refs[:cores]
    act_ref = refs[cores]
    out_hbm, result, out_sems = refs[-3:]
    core = lax.axis_index("etp")
    act = act_ref[...]
    chunk = width // chunks
    copies = []
    for d in range(cores):
        rows = pieces[d][...]
        base = traced_origin(core, d, cores) * width
        for n in range(chunks):
            result[d * chunks + n] = contract(act, rows[:, n * chunk : (n + 1) * chunk], 0, 0).astype(BF16)
            span = pl.ds(pl.multiple_of(base + n * chunk, chunk), chunk)
            copy = pltpu.make_async_copy(
                result.at[d * chunks + n], out_hbm.at[0, :, span], out_sems.at[d * chunks + n]
            )
            copy.start()
            copies.append(copy)
    for copy in copies:
        copy.wait()


def split_kernel(dims, *refs):
    cores, inner, reach = dims
    total = refs[0][...].astype(F32)
    for part in refs[1:cores]:
        total = total + part[...].astype(F32)
    total = total.astype(BF16)
    for q in range(inner):
        refs[q - inner][...] = total[q * reach : (q + 1) * reach]


def combine_kernel(dims, weighted, *refs):
    outer, inner, unit, half = dims
    pieces = refs[:inner]
    tables = refs[inner : inner + weighted]
    outs = refs[-outer:]
    rows = jnp.concatenate([p[...] for p in pieces], axis=0)
    slots = rows.shape[0]
    total = None
    for table in tables:
        term = jnp.dot(table[:, :slots], rows[:, :half], preferred_element_type=F32)
        term = term + jnp.dot(table[:, slots:], rows[:, half:], preferred_element_type=F32)
        total = term if total is None else total + term
    for b in range(outer):
        outs[b][...] = total[b * unit : (b + 1) * unit].astype(BF16)


def final_kernel(dims, *refs):
    outer, tokens, half = dims
    out_ref = refs[-2]
    total = refs[0][...].astype(F32)
    for part in refs[1:outer]:
        total = total + part[...].astype(F32)
    out_ref[:, :half] = total[:tokens].astype(BF16)
    out_ref[:, half:] = total[tokens:].astype(BF16)


def shape(rows, columns, kind=BF16):
    return jax.ShapeDtypeStruct((rows, columns), kind)


def on_device(hidden_in, expert_ids, gate_weights, out_grad, gate_weight, up_weight, down_weight):
    tokens, top = expert_ids.shape
    experts = lax.axis_size("expert")
    cores = lax.axis_size("etp")
    outer, inner = group_sizes(experts)
    cap = min(tokens, tokens * top // experts + 1)
    width = hidden_in.shape[1]
    half = width // 2
    hidden = gate_weight.shape[2]
    reach = -(-(outer * cap) // 16) * 16
    rows = inner * reach
    unit = 2 * tokens

    with jax.named_scope("prepare"):
        packed = pl.pallas_call(
            functools.partial(prepare_kernel, (tokens, top, half)),
            out_shape=shape(unit, 2 * half + META),
            in_specs=hbm_specs(4),
            out_specs=pl.BlockSpec(memory_space=pltpu.VMEM),
            scratch_shapes=[
                pltpu.VMEM((top, tokens), jnp.int32),
                pltpu.VMEM((top, tokens), F32),
                pltpu.VMEM((tokens, width), BF16),
                pltpu.VMEM((tokens, width), BF16),
                pltpu.SemaphoreType.DMA((4,)),
            ],
            compiler_params=params(),
            cost_estimate=pl.CostEstimate(flops=1, bytes_accessed=1, transcendentals=0),
            name="prepare",
        )(in_hbm(expert_ids.T), in_hbm(gate_weights.T), in_hbm(hidden_in), in_hbm(out_grad))

    with jax.named_scope("gather_blocks"):
        blocks = gather_outer(packed, outer, inner)

    table_shape = shape(outer * unit, 2 * rows)
    with jax.named_scope("load_weights"):
        weights = (gate_weight, up_weight, down_weight)
        weight_parts = 4
        held = pl.pallas_call(
            functools.partial(load_kernel, weight_parts),
            out_shape=[pltpu.VMEM(w.shape, BF16) for w in weights]
            + [pltpu.VMEM((w.shape[2], w.shape[1]), BF16) for w in weights]
            + [shape(8, META, F32)],
            in_specs=hbm_specs(3) + whole_specs(1),
            out_specs=whole_specs(7),
            scratch_shapes=[pltpu.SemaphoreType.DMA((3 * weight_parts,))],
            compiler_params=params(),
            cost_estimate=pl.CostEstimate(flops=1, bytes_accessed=1, transcendentals=0),
            name="load_weights",
        )(*[in_hbm(w) for w in weights], packed)
        weights, turned = held[:3], held[3:6]

    with jax.named_scope("route"):
        routed = pl.pallas_call(
            functools.partial(route_kernel, (outer, inner, tokens, top, cap, reach, half)),
            out_shape=[shape(reach, width)] * inner + [table_shape] * 3 + [shape(rows, META, F32)],
            in_specs=whole_specs(outer + 1),
            out_specs=whole_specs(inner + 4),
            compiler_params=params(),
            cost_estimate=pl.CostEstimate(flops=1, bytes_accessed=1, transcendentals=0),
            name="route",
        )(*blocks, held[6])
        in_sends, (pick, gate_hi, gate_lo, gate_col) = routed[:inner], routed[inner:]

    def spread(sends):
        return [sends[0]] + [send_inner(sends[q], q, outer, inner) for q in range(1, inner)]

    def gather_cores(pieces, after=()):
        stack = pl.pallas_call(
            functools.partial(stack_kernel, inner),
            out_shape=shape(rows, width),
            in_specs=whole_specs(inner) + any_specs(len(after)),
            out_specs=pl.BlockSpec(memory_space=pltpu.VMEM),
            compiler_params=params(),
            cost_estimate=pl.CostEstimate(flops=1, bytes_accessed=1, transcendentals=0),
            name="stack",
        )(*pieces, *after)
        return [stack] + [send_core(stack, d, cores) for d in range(1, cores)]

    with jax.named_scope("exchange_in"):
        in_pieces = spread(in_sends)
    with jax.named_scope("scale"):
        grad_sends = pl.pallas_call(
            functools.partial(scale_kernel, outer, inner),
            out_shape=[shape(reach, width)] * inner,
            in_specs=whole_specs(outer + 2),
            out_specs=whole_specs(inner),
            compiler_params=params(),
            cost_estimate=pl.CostEstimate(flops=1, bytes_accessed=1, transcendentals=0),
            name="scale",
        )(*blocks, pick, gate_col)
    with jax.named_scope("exchange_grad"):
        grad_pieces = spread(grad_sends)
    with jax.named_scope("gather_in"):
        in_rows = gather_cores(in_pieces)
        grad_rows = gather_cores(grad_pieces)

    dims = (cores, width)
    with jax.named_scope("forward"):
        gate_pre, up_pre, act, *out_parts = pl.pallas_call(
            functools.partial(forward_kernel, dims),
            out_shape=[shape(rows, hidden, F32)] * 2 + [shape(rows, hidden)] + [shape(rows, width)] * cores,
            in_specs=whole_specs(cores + 3) + any_specs(1),
            out_specs=whole_specs(3 + cores),
            compiler_params=params(),
            cost_estimate=pl.CostEstimate(flops=1, bytes_accessed=1, transcendentals=0),
            name="forward",
        )(*in_rows, *weights, grad_rows[0])

    def give_back(parts, after=()):
        got = [parts[0]] + [send_core(parts[d], d, cores) for d in range(1, cores)]
        sends = pl.pallas_call(
            functools.partial(split_kernel, (cores, inner, reach)),
            out_shape=[shape(reach, width)] * inner,
            in_specs=whole_specs(cores) + any_specs(len(after)),
            out_specs=whole_specs(inner),
            compiler_params=params(),
            cost_estimate=pl.CostEstimate(flops=1, bytes_accessed=1, transcendentals=0),
            name="split",
        )(*got, *after)
        return [sends[0]] + [send_inner(sends[q], q, outer, inner, back=True) for q in range(1, inner)]

    def combine(pieces, tables):
        blocks = pl.pallas_call(
            functools.partial(combine_kernel, (outer, inner, unit, half), len(tables)),
            out_shape=[shape(unit, half)] * outer,
            in_specs=whole_specs(inner + len(tables)),
            out_specs=whole_specs(outer),
            compiler_params=params(),
            cost_estimate=pl.CostEstimate(flops=1, bytes_accessed=1, transcendentals=0),
            name="combine",
        )(*pieces, *tables)
        return [blocks[0]] + [send_outer(blocks[s], s, outer, inner, back=True) for s in send_order(outer)]

    def finish(blocks, after=()):
        return pl.pallas_call(
            functools.partial(final_kernel, (outer, tokens, half)),
            out_shape=[shape(tokens, width), shape(8, META, F32)],
            in_specs=whole_specs(outer + len(after)),
            out_specs=whole_specs(2),
            compiler_params=params(),
            cost_estimate=pl.CostEstimate(flops=1, bytes_accessed=1, transcendentals=0),
            name="final",
        )(*blocks, *after)

    with jax.named_scope("return_out"):
        out_back = give_back(out_parts)
        out_blocks = combine(out_back, (gate_hi, gate_lo))

    with jax.named_scope("backward"):
        grad_parts = pl.pallas_call(
            functools.partial(backward_kernel, dims),
            out_shape=[shape(rows, width)] * cores,
            in_specs=whole_specs(cores + 5),
            out_specs=whole_specs(cores),
            compiler_params=params(),
            cost_estimate=pl.CostEstimate(flops=1, bytes_accessed=1, transcendentals=0),
            name="backward",
        )(*grad_rows, *turned, gate_pre, up_pre)

    with jax.named_scope("return_grad"):
        back_blocks = combine(give_back(grad_parts, out_back[:1]), (pick,))

    with jax.named_scope("down_grad"):
        chunks = max(1, width // 512)
        down_grad = pl.pallas_call(
            functools.partial(down_kernel, dims, chunks),
            out_shape=pltpu.HBM(down_weight.shape, BF16),
            in_specs=whole_specs(cores + 1) + any_specs(1),
            out_specs=pl.BlockSpec(memory_space=pltpu.HBM),
            scratch_shapes=[
                pltpu.VMEM((cores * chunks, hidden, width // chunks), BF16),
                pltpu.SemaphoreType.DMA((cores * chunks,)),
            ],
            compiler_params=params(),
            cost_estimate=pl.CostEstimate(flops=1, bytes_accessed=1, transcendentals=0),
            name="down_grad",
        )(*grad_rows, act, back_blocks[0])

    mixed_out, done = finish(out_blocks)
    input_grad, done = finish(back_blocks, (done,))
    return (mixed_out, input_grad, down_grad)


def solution(mesh):
    return jax.shard_map(
        on_device,
        mesh=mesh,
        in_specs=(
            P("expert", "etp"),
            P("expert", None),
            P("expert", None),
            P("expert", "etp"),
            P("expert", None, "etp"),
            P("expert", None, "etp"),
            P("expert", "etp", None),
        ),
        out_specs=(P("expert", "etp"), P("expert", "etp"), P("expert", "etp", None)),
        check_vma=False,
    )
```

```python
import functools
import jax
import jax.numpy as jnp
from jax import lax
from jax.experimental import pallas as pl
from jax.experimental.pallas import tpu as pltpu
from jax.sharding import PartitionSpec as P

BF16 = jnp.bfloat16
F32 = jnp.float32
META = 128
VMEM_LIMIT = 20 * 1024 * 1024


def group_sizes(experts):
    inner = 1
    while inner * inner * 4 <= experts and experts % (inner * 2) == 0:
        inner *= 2
    return experts // inner, inner


def partner(index, step, size):
    return index ^ step if size & (size - 1) == 0 else (index + step) % size


def origin(index, step, size):
    return index ^ step if size & (size - 1) == 0 else (index - step) % size


def traced_partner(index, step, size):
    return index ^ step if size & (size - 1) == 0 else lax.rem(index + step, size)


def traced_origin(index, step, size):
    return index ^ step if size & (size - 1) == 0 else lax.rem(index + size - step, size)


def send_outer(x, step, outer, inner, back=False):
    move = origin if back else partner
    pairs = [
        (a * inner + b, move(a, step, outer) * inner + b) for a in range(outer) for b in range(inner)
    ]
    return lax.ppermute(x, "expert", pairs)


def send_inner(x, step, outer, inner, back=False):
    move = origin if back else partner
    pairs = [
        (a * inner + b, a * inner + move(b, step, inner)) for a in range(outer) for b in range(inner)
    ]
    return lax.ppermute(x, "expert", pairs)


def send_core(x, step, cores, back=False):
    move = origin if back else partner
    return lax.ppermute(x, "etp", [(i, move(i, step, cores)) for i in range(cores)])


def flipped(parts):
    return [parts[0], *parts[:0:-1]]


def contract(left, right, left_dim, right_dim):
    return lax.dot_general(
        left, right, (((left_dim,), (right_dim,)), ((), ())), preferred_element_type=F32
    )


def whole_specs(count):
    return [pl.BlockSpec(memory_space=pltpu.VMEM)] * count


def any_specs(count):
    return [pl.BlockSpec(memory_space=pl.ANY)] * count


def params():
    return pltpu.CompilerParams(vmem_limit_bytes=VMEM_LIMIT)


def in_hbm(x):
    return pltpu.with_memory_space_constraint(x, pltpu.HBM)


def hbm_specs(count):
    return [pl.BlockSpec(memory_space=pltpu.HBM)] * count


def prepare_kernel(dims, *refs):
    tokens, top, half = dims
    sources, out_ref, held, sems = refs[:4], refs[4], refs[5:9], refs[9]
    copies = [pltpu.make_async_copy(a, b, sems.at[n]) for n, (a, b) in enumerate(zip(sources, held))]
    for copy in copies:
        copy.start()
    for copy in copies:
        copy.wait()
    ids_ref, gates_ref, hidden_ref, grad_ref = held
    gates = gates_ref[...]
    gate_hi = gates.astype(BF16)
    rest = gates - gate_hi.astype(F32)
    gate_mid = rest.astype(BF16)
    gate_lo = (rest - gate_mid.astype(F32)).astype(BF16)
    meta = jnp.zeros((tokens, META), F32)
    entry = lax.broadcasted_iota(jnp.int32, (top, META), 0)
    lane = lax.broadcasted_iota(jnp.int32, (top, META), 1)
    for n, value in enumerate((ids_ref[...].astype(F32).astype(BF16), gate_hi, gate_mid, gate_lo)):
        spread = (lane == entry + n * top).astype(F32).astype(BF16)
        meta = meta + contract(value, spread, 0, 0)
    unit = 2 * tokens
    row = lax.broadcasted_iota(jnp.int32, (unit, tokens), 0)
    token = lax.broadcasted_iota(jnp.int32, (unit, tokens), 1)
    upper = (row == token).astype(F32).astype(BF16)
    lower = (row == token + tokens).astype(F32).astype(BF16)
    for n, source in enumerate((hidden_ref, grad_ref)):
        value = jnp.dot(upper, source[:, :half], preferred_element_type=F32)
        value = value + jnp.dot(lower, source[:, half:], preferred_element_type=F32)
        out_ref[:, n * half : (n + 1) * half] = value.astype(BF16)
    out_ref[:, 2 * half :] = jnp.dot(upper + lower, meta.astype(BF16), preferred_element_type=F32).astype(BF16)


def stacked(refs, columns=None):
    parts = [r[...] if columns is None else r[:, columns] for r in refs]
    if len(parts) == 1:
        return parts[0]
    return jnp.concatenate([p.astype(F32) for p in parts], axis=0).astype(BF16)


def count_above(index, unit, total):
    value = jnp.zeros_like(index)
    for m in range(unit, total, unit):
        value = value + (index >= m).astype(jnp.int32)
    return value


def route_kernel(dims, *refs):
    outer, inner, tokens, top, cap, reach, half = dims
    blocks = refs[:outer]
    sends = refs[outer + 1 : outer + 1 + inner]
    pick_ref, gate_hi_ref, gate_mid_ref, gate_col_ref = refs[outer + 1 + inner :]
    rows = outer * 2 * tokens
    fold = 2 * reach
    slots = inner * fold
    me = lax.axis_index("expert")
    my_inner = lax.rem(me, inner)
    my_base = me - my_inner
    meta = jnp.concatenate([r[:, 2 * half :].astype(F32) for r in blocks], axis=0)
    lane = lax.broadcasted_iota(jnp.int32, (rows, slots), 1)
    row = lax.broadcasted_iota(jnp.int32, (rows, slots), 0)
    step = count_above(lane, fold, slots)
    dest = jnp.zeros((rows, slots), F32)
    for q in range(inner):
        expert = (my_base + traced_partner(my_inner, q, inner)).astype(F32)
        dest = jnp.where(step == q, expert, dest)
    slot = lane - step * fold
    side = (slot >= reach).astype(jnp.int32)
    slot = slot - side * reach
    named = jnp.zeros((rows, slots), F32)
    gate = jnp.zeros((rows, slots), F32)
    for k in range(top):
        hit = meta[:, k : k + 1] == dest
        value = (
            meta[:, top + k : top + k + 1]
            + meta[:, 2 * top + k : 2 * top + k + 1]
            + meta[:, 3 * top + k : 3 * top + k + 1]
        )
        named = named + hit.astype(F32)
        gate = gate + jnp.where(hit, value, 0.0)
    left = lax.broadcasted_iota(jnp.int32, (rows, rows), 1)
    down = lax.broadcasted_iota(jnp.int32, (rows, rows), 0)
    same = count_above(left, tokens, rows) == count_above(down, tokens, rows)
    before = (same & (left < down)).astype(F32).astype(BF16)
    rank = jnp.dot(before, named.astype(BF16), preferred_element_type=F32)
    position = count_above(row, 2 * tokens, rows) * cap + rank.astype(jnp.int32)
    row_side = count_above(row, tokens, rows) - 2 * count_above(row, 2 * tokens, rows)
    pick = jnp.where((position == slot) & (row_side == side), named, 0.0)
    gate = pick * gate
    gate_hi = gate.astype(BF16)
    rest = gate - gate_hi.astype(F32)
    gate_mid = rest.astype(BF16)
    gate_lo = (rest - gate_mid.astype(F32)).astype(BF16)
    pick_ref[...] = pick.astype(BF16)
    gate_hi_ref[...] = gate_hi
    gate_mid_ref[...] = gate_mid
    ones = jnp.ones((rows, META), BF16)
    column = contract(gate_hi, ones, 0, 0) + contract(gate_mid, ones, 0, 0) + contract(gate_lo, ones, 0, 0)
    gate_col_ref[...] = column
    select_rows(blocks, 0, pick_ref, None, sends)


def select_rows(blocks, array, pick_ref, scale, sends):
    fold, half = sends[0].shape
    table = stacked(blocks, pl.ds(array * half, half))
    out = contract(pick_ref[...], table, 0, 0)
    out = (out if scale is None else out * scale).astype(F32)
    for q, send in enumerate(sends):
        send[...] = out[q * fold : (q + 1) * fold].astype(BF16)


def scale_kernel(outer, inner, *refs):
    pick_ref, gate_col_ref = refs[outer : outer + 2]
    select_rows(refs[:outer], 1, pick_ref, gate_col_ref[:, :1], refs[-inner:])


def stack_kernel(dims, *refs):
    inner, reach, held = dims
    fold, half = refs[0].shape
    live = lax.broadcasted_iota(jnp.int32, (held, half), 0) < reach
    for q, piece in enumerate(flipped(refs[:inner])):
        value = piece[...].astype(F32)
        sides = (value[:held], pltpu.roll(value[fold - held :], fold - reach, 0))
        for n, side in enumerate(sides):
            target = refs[-1].at[q * held : (q + 1) * held, n * half : (n + 1) * half]
            target[...] = jnp.where(live, side, 0.0).astype(BF16)


def load_kernel(parts, *refs):
    sources, targets, turned, sems = refs[:3], refs[4:7], refs[7:10], refs[11]
    copies = []
    for n in range(3):
        step = sources[n].shape[1] // parts
        for m in range(parts):
            index = (0, pl.ds(m * step, step))
            copy = pltpu.make_async_copy(sources[n].at[index], targets[n].at[index], sems.at[n * parts + m])
            copy.start()
            copies.append(copy)
    for n in range(3):
        step = sources[n].shape[1] // parts
        for m in range(parts):
            copies[n * parts + m].wait()
            turned[n][:, m * step : (m + 1) * step] = targets[n][0, m * step : (m + 1) * step, :].T


def core_spans(cores, width, move):
    core = lax.axis_index("etp")
    return [pl.ds(pl.multiple_of(move(core, d, cores) * width, width), width) for d in range(cores)]


def forward_kernel(dims, *refs):
    cores, width = dims
    pieces = refs[:cores]
    gate_w, up_w, down_w = refs[cores : cores + 3]
    gate_ref, up_ref, act_ref, *parts = refs[-(3 + cores) :]
    spans = core_spans(cores, width, traced_origin)
    gate_pre = None
    up_pre = None
    for d in range(cores):
        rows = pieces[d][...]
        term = jnp.dot(rows, gate_w[0, spans[d], :], preferred_element_type=F32)
        gate_pre = term if gate_pre is None else gate_pre + term
        term = jnp.dot(rows, up_w[0, spans[d], :], preferred_element_type=F32)
        up_pre = term if up_pre is None else up_pre + term
    act = (gate_pre * jax.nn.sigmoid(gate_pre) * up_pre).astype(BF16)
    gate_ref[...] = gate_pre
    up_ref[...] = up_pre
    act_ref[...] = act
    spans = core_spans(cores, width, traced_partner)
    for d in reversed(range(cores)):
        parts[d][...] = jnp.dot(act, down_w[0, :, spans[d]], preferred_element_type=F32).astype(BF16)


def backward_kernel(dims, *refs):
    cores, width = dims
    pieces = refs[:cores]
    gate_t, up_t, down_t, gate_ref, up_ref = refs[cores : cores + 5]
    parts = refs[-cores:]
    spans = core_spans(cores, width, traced_origin)
    act_grad = None
    for d in range(cores):
        rows = pieces[d][...]
        term = jnp.dot(rows, down_t[spans[d], :], preferred_element_type=F32)
        act_grad = term if act_grad is None else act_grad + term
    gate_pre = gate_ref[...]
    sigmoid = jax.nn.sigmoid(gate_pre)
    gate_grad = (act_grad * up_ref[...] * sigmoid * (1.0 + gate_pre * (1.0 - sigmoid))).astype(BF16)
    up_grad = (act_grad * (gate_pre * sigmoid)).astype(BF16)
    spans = core_spans(cores, width, traced_partner)
    for d in reversed(range(cores)):
        part = jnp.dot(gate_grad, gate_t[:, spans[d]], preferred_element_type=F32)
        part = part + jnp.dot(up_grad, up_t[:, spans[d]], preferred_element_type=F32)
        parts[d][...] = part.astype(BF16)


def down_kernel(dims, chunks, *refs):
    cores, width = dims
    pieces = refs[:cores]
    act_ref = refs[cores]
    out_hbm, result, out_sems = refs[-3:]
    core = lax.axis_index("etp")
    act = act_ref[...]
    chunk = width // chunks
    copies = []
    for d in range(cores):
        rows = pieces[d][...]
        base = traced_origin(core, d, cores) * width
        for n in range(chunks):
            result[d * chunks + n] = contract(act, rows[:, n * chunk : (n + 1) * chunk], 0, 0).astype(BF16)
            span = pl.ds(pl.multiple_of(base + n * chunk, chunk), chunk)
            copy = pltpu.make_async_copy(
                result.at[d * chunks + n], out_hbm.at[0, :, span], out_sems.at[d * chunks + n]
            )
            copy.start()
            copies.append(copy)
    for copy in copies:
        copy.wait()


def split_kernel(dims, *refs):
    cores, inner, reach, held = dims
    total = refs[0][...].astype(F32)
    for part in refs[1:cores]:
        total = total + part[...].astype(F32)
    half = total.shape[1] // 2
    rest = jnp.zeros((2 * reach - held, half), F32)
    for q in range(inner):
        rows = total[q * held : (q + 1) * held]
        right = pltpu.roll(rows[:, half:], held - reach, 0)
        value = jnp.concatenate([rows[:, :half], rest], axis=0) + jnp.concatenate([rest, right], axis=0)
        refs[q - inner][...] = value.astype(BF16)


def combine_kernel(dims, weighted, *refs):
    outer, inner, unit = dims
    tables = refs[inner : inner + weighted]
    outs = refs[-outer:]
    rows = stacked(flipped(refs[:inner]))
    total = None
    for table in tables:
        term = jnp.dot(table[...], rows, preferred_element_type=F32)
        total = term if total is None else total + term
    for b in range(outer):
        outs[b][...] = total[b * unit : (b + 1) * unit].astype(BF16)


def final_kernel(dims, *refs):
    outer, tokens, half = dims
    out_ref = refs[-2]
    total = refs[0][...].astype(F32)
    for part in refs[1:outer]:
        total = total + part[...].astype(F32)
    out_ref[:, :half] = total[:tokens].astype(BF16)
    out_ref[:, half:] = total[tokens:].astype(BF16)


def shape(rows, columns, kind=BF16):
    return jax.ShapeDtypeStruct((rows, columns), kind)


def on_device(hidden_in, expert_ids, gate_weights, out_grad, gate_weight, up_weight, down_weight):
    tokens, top = expert_ids.shape
    experts = lax.axis_size("expert")
    cores = lax.axis_size("etp")
    outer, inner = group_sizes(experts)
    cap = min(tokens, tokens * top // experts + 1)
    width = hidden_in.shape[1]
    half = width // 2
    hidden = gate_weight.shape[2]
    reach = outer * cap
    held = -(-reach // 16) * 16
    rows = inner * held
    unit = 2 * tokens

    with jax.named_scope("prepare"):
        packed = pl.pallas_call(
            functools.partial(prepare_kernel, (tokens, top, half)),
            out_shape=shape(unit, 2 * half + META),
            in_specs=hbm_specs(4),
            out_specs=pl.BlockSpec(memory_space=pltpu.VMEM),
            scratch_shapes=[
                pltpu.VMEM((top, tokens), jnp.int32),
                pltpu.VMEM((top, tokens), F32),
                pltpu.VMEM((tokens, width), BF16),
                pltpu.VMEM((tokens, width), BF16),
                pltpu.SemaphoreType.DMA((4,)),
            ],
            compiler_params=params(),
            cost_estimate=pl.CostEstimate(flops=1, bytes_accessed=1, transcendentals=0),
            name="prepare",
        )(in_hbm(expert_ids.T), in_hbm(gate_weights.T), in_hbm(hidden_in), in_hbm(out_grad))

    with jax.named_scope("gather_blocks"):
        blocks = [packed] + [send_outer(packed, s, outer, inner) for s in range(1, outer)]

    piece_shapes = [shape(2 * reach, half)] * inner
    table_shape = shape(outer * unit, inner * 2 * reach)
    with jax.named_scope("load_weights"):
        weights = (gate_weight, up_weight, down_weight)
        weight_parts = 4
        loaded = pl.pallas_call(
            functools.partial(load_kernel, weight_parts),
            out_shape=[pltpu.VMEM(w.shape, BF16) for w in weights]
            + [pltpu.VMEM((w.shape[2], w.shape[1]), BF16) for w in weights]
            + [shape(8, META, F32)],
            in_specs=hbm_specs(3) + whole_specs(1),
            out_specs=whole_specs(7),
            scratch_shapes=[pltpu.SemaphoreType.DMA((3 * weight_parts,))],
            compiler_params=params(),
            cost_estimate=pl.CostEstimate(flops=1, bytes_accessed=1, transcendentals=0),
            name="load_weights",
        )(*[in_hbm(w) for w in weights], packed)
        weights, turned = loaded[:3], loaded[3:6]

    with jax.named_scope("route"):
        routed = pl.pallas_call(
            functools.partial(route_kernel, (outer, inner, tokens, top, cap, reach, half)),
            out_shape=piece_shapes + [table_shape] * 3 + [shape(inner * 2 * reach, META, F32)],
            in_specs=whole_specs(outer + 1),
            out_specs=whole_specs(inner + 4),
            compiler_params=params(),
            cost_estimate=pl.CostEstimate(flops=1, bytes_accessed=1, transcendentals=0),
            name="route",
        )(*blocks, loaded[6])
        in_sends, (pick, gate_hi, gate_lo, gate_col) = routed[:inner], routed[inner:]

    def spread(sends):
        return [sends[0]] + [send_inner(sends[q], q, outer, inner) for q in range(1, inner)]

    def gather_cores(pieces, after=()):
        stack = pl.pallas_call(
            functools.partial(stack_kernel, (inner, reach, held)),
            out_shape=shape(rows, width),
            in_specs=whole_specs(inner) + any_specs(len(after)),
            out_specs=pl.BlockSpec(memory_space=pltpu.VMEM),
            compiler_params=params(),
            cost_estimate=pl.CostEstimate(flops=1, bytes_accessed=1, transcendentals=0),
            name="stack",
        )(*flipped(pieces), *after)
        return [stack] + [send_core(stack, d, cores) for d in range(1, cores)]

    with jax.named_scope("exchange_in"):
        in_pieces = spread(in_sends)
    with jax.named_scope("scale"):
        grad_sends = pl.pallas_call(
            functools.partial(scale_kernel, outer, inner),
            out_shape=piece_shapes,
            in_specs=whole_specs(outer + 2),
            out_specs=whole_specs(inner),
            compiler_params=params(),
            cost_estimate=pl.CostEstimate(flops=1, bytes_accessed=1, transcendentals=0),
            name="scale",
        )(*blocks, pick, gate_col)
    with jax.named_scope("exchange_grad"):
        grad_pieces = spread(grad_sends)
    with jax.named_scope("gather_in"):
        in_rows = gather_cores(in_pieces)
        grad_rows = gather_cores(grad_pieces)

    dims = (cores, width)
    with jax.named_scope("forward"):
        gate_pre, up_pre, act, *out_parts = pl.pallas_call(
            functools.partial(forward_kernel, dims),
            out_shape=[shape(rows, hidden, F32)] * 2 + [shape(rows, hidden)] + [shape(rows, width)] * cores,
            in_specs=whole_specs(cores + 3) + any_specs(1),
            out_specs=whole_specs(3 + cores),
            compiler_params=params(),
            cost_estimate=pl.CostEstimate(flops=1, bytes_accessed=1, transcendentals=0),
            name="forward",
        )(*in_rows, *weights, grad_pieces[-1])

    def give_back(parts, after=()):
        got = [parts[0]] + [send_core(parts[d], d, cores) for d in range(1, cores)]
        sends = pl.pallas_call(
            functools.partial(split_kernel, (cores, inner, reach, held)),
            out_shape=piece_shapes,
            in_specs=whole_specs(cores) + any_specs(len(after)),
            out_specs=whole_specs(inner),
            compiler_params=params(),
            cost_estimate=pl.CostEstimate(flops=1, bytes_accessed=1, transcendentals=0),
            name="split",
        )(*got, *after)
        return [sends[0]] + [send_inner(sends[q], q, outer, inner, back=True) for q in range(1, inner)]

    def combine(pieces, tables):
        blocks = pl.pallas_call(
            functools.partial(combine_kernel, (outer, inner, unit), len(tables)),
            out_shape=[shape(unit, half)] * outer,
            in_specs=whole_specs(inner + len(tables)),
            out_specs=whole_specs(outer),
            compiler_params=params(),
            cost_estimate=pl.CostEstimate(flops=1, bytes_accessed=1, transcendentals=0),
            name="combine",
        )(*flipped(pieces), *tables)
        return [blocks[0]] + [send_outer(blocks[s], s, outer, inner, back=True) for s in range(1, outer)]

    def finish(blocks, after=()):
        return pl.pallas_call(
            functools.partial(final_kernel, (outer, tokens, half)),
            out_shape=[shape(tokens, width), shape(8, META, F32)],
            in_specs=whole_specs(outer + len(after)),
            out_specs=whole_specs(2),
            compiler_params=params(),
            cost_estimate=pl.CostEstimate(flops=1, bytes_accessed=1, transcendentals=0),
            name="final",
        )(*flipped(blocks), *after)

    with jax.named_scope("return_out"):
        out_back = give_back(out_parts)
        out_blocks = combine(out_back, (gate_hi, gate_lo))

    with jax.named_scope("backward"):
        grad_parts = pl.pallas_call(
            functools.partial(backward_kernel, dims),
            out_shape=[shape(rows, width)] * cores,
            in_specs=whole_specs(cores + 5),
            out_specs=whole_specs(cores),
            compiler_params=params(),
            cost_estimate=pl.CostEstimate(flops=1, bytes_accessed=1, transcendentals=0),
            name="backward",
        )(*grad_rows, *turned, gate_pre, up_pre)

    with jax.named_scope("return_grad"):
        back_blocks = combine(give_back(grad_parts, out_back[:1]), (pick,))

    with jax.named_scope("down_grad"):
        chunks = max(1, width // 512)
        down_grad = pl.pallas_call(
            functools.partial(down_kernel, dims, chunks),
            out_shape=pltpu.HBM(down_weight.shape, BF16),
            in_specs=whole_specs(cores + 1) + any_specs(1),
            out_specs=pl.BlockSpec(memory_space=pltpu.HBM),
            scratch_shapes=[
                pltpu.VMEM((cores * chunks, hidden, width // chunks), BF16),
                pltpu.SemaphoreType.DMA((cores * chunks,)),
            ],
            compiler_params=params(),
            cost_estimate=pl.CostEstimate(flops=1, bytes_accessed=1, transcendentals=0),
            name="down_grad",
        )(*grad_rows, act, back_blocks[0])

    mixed_out, done = finish(out_blocks)
    input_grad, done = finish(back_blocks, (done,))
    return (mixed_out, input_grad, down_grad)


def solution(mesh):
    return jax.shard_map(
        on_device,
        mesh=mesh,
        in_specs=(
            P("expert", "etp"),
            P("expert", None),
            P("expert", None),
            P("expert", "etp"),
            P("expert", None, "etp"),
            P("expert", None, "etp"),
            P("expert", "etp", None),
        ),
        out_specs=(P("expert", "etp"), P("expert", "etp"), P("expert", "etp", None)),
        check_vma=False,
    )
```

```python
import functools
import jax
import jax.numpy as jnp
from jax import lax
from jax.experimental import pallas as pl
from jax.experimental.pallas import tpu as pltpu
from jax.sharding import PartitionSpec as P

BF16 = jnp.bfloat16
F32 = jnp.float32
META = 128
VMEM_LIMIT = 20 * 1024 * 1024


def group_sizes(experts):
    inner = 1
    while inner * inner * 4 <= experts and experts % (inner * 2) == 0:
        inner *= 2
    return experts // inner, inner


def partner(index, step, size):
    return index ^ step if size & (size - 1) == 0 else (index + step) % size


def origin(index, step, size):
    return index ^ step if size & (size - 1) == 0 else (index - step) % size


def traced_partner(index, step, size):
    return index ^ step if size & (size - 1) == 0 else lax.rem(index + step, size)


def traced_origin(index, step, size):
    return index ^ step if size & (size - 1) == 0 else lax.rem(index + size - step, size)


def send_outer(x, step, outer, inner, back=False):
    move = origin if back else partner
    pairs = [
        (a * inner + b, move(a, step, outer) * inner + b) for a in range(outer) for b in range(inner)
    ]
    return lax.ppermute(x, "expert", pairs)


def send_inner(x, step, outer, inner, back=False):
    move = origin if back else partner
    pairs = [
        (a * inner + b, a * inner + move(b, step, inner)) for a in range(outer) for b in range(inner)
    ]
    return lax.ppermute(x, "expert", pairs)


def send_core(x, step, cores, back=False):
    move = origin if back else partner
    return lax.ppermute(x, "etp", [(i, move(i, step, cores)) for i in range(cores)])


def flipped(parts):
    return [parts[0], *parts[:0:-1]]


def contract(left, right, left_dim, right_dim):
    return lax.dot_general(
        left, right, (((left_dim,), (right_dim,)), ((), ())), preferred_element_type=F32
    )


def whole_specs(count):
    return [pl.BlockSpec(memory_space=pltpu.VMEM)] * count


def any_specs(count):
    return [pl.BlockSpec(memory_space=pl.ANY)] * count


def params():
    return pltpu.CompilerParams(vmem_limit_bytes=VMEM_LIMIT)


def in_hbm(x):
    return pltpu.with_memory_space_constraint(x, pltpu.HBM)


def hbm_specs(count):
    return [pl.BlockSpec(memory_space=pltpu.HBM)] * count


def prepare_kernel(dims, *refs):
    tokens, top, half = dims
    sources, out_ref, held, sems = refs[:4], refs[4], refs[5:9], refs[9]
    copies = [pltpu.make_async_copy(a, b, sems.at[n]) for n, (a, b) in enumerate(zip(sources, held))]
    for copy in copies:
        copy.start()
    for copy in copies:
        copy.wait()
    ids_ref, gates_ref, hidden_ref, grad_ref = held
    gates = gates_ref[...]
    gate_hi = gates.astype(BF16)
    rest = gates - gate_hi.astype(F32)
    gate_mid = rest.astype(BF16)
    gate_lo = (rest - gate_mid.astype(F32)).astype(BF16)
    meta = jnp.zeros((tokens, META), F32)
    entry = lax.broadcasted_iota(jnp.int32, (top, META), 0)
    lane = lax.broadcasted_iota(jnp.int32, (top, META), 1)
    for n, value in enumerate((ids_ref[...].astype(F32).astype(BF16), gate_hi, gate_mid, gate_lo)):
        spread = (lane == entry + n * top).astype(F32).astype(BF16)
        meta = meta + contract(value, spread, 0, 0)
    unit = 2 * tokens
    row = lax.broadcasted_iota(jnp.int32, (unit, tokens), 0)
    token = lax.broadcasted_iota(jnp.int32, (unit, tokens), 1)
    upper = (row == token).astype(F32).astype(BF16)
    lower = (row == token + tokens).astype(F32).astype(BF16)
    for n, source in enumerate((hidden_ref, grad_ref)):
        value = jnp.dot(upper, source[:, :half], preferred_element_type=F32)
        value = value + jnp.dot(lower, source[:, half:], preferred_element_type=F32)
        out_ref[:, n * half : (n + 1) * half] = value.astype(BF16)
    out_ref[:, 2 * half :] = jnp.dot(upper + lower, meta.astype(BF16), preferred_element_type=F32).astype(BF16)


def stacked(refs, columns=None):
    parts = [r[...] if columns is None else r[:, columns] for r in refs]
    if len(parts) == 1:
        return parts[0]
    return jnp.concatenate([p.astype(F32) for p in parts], axis=0).astype(BF16)


def count_above(index, unit, total):
    value = jnp.zeros_like(index)
    for m in range(unit, total, unit):
        value = value + (index >= m).astype(jnp.int32)
    return value


def slot_lanes(dims):
    outer, inner, tokens, top, cap, reach = dims
    fold = 2 * reach
    shape = (outer * 2 * tokens, inner * fold)
    me = lax.axis_index("expert")
    my_inner = lax.rem(me, inner)
    my_base = me - my_inner
    lane = lax.broadcasted_iota(jnp.int32, shape, 1)
    step = count_above(lane, fold, shape[1])
    dest = jnp.zeros(shape, F32)
    for q in range(inner):
        expert = (my_base + traced_partner(my_inner, q, inner)).astype(F32)
        dest = jnp.where(step == q, expert, dest)
    return lane - step * fold, dest


def route_kernel(dims, *refs):
    outer, inner, tokens, top, cap, reach = dims
    blocks = refs[:outer]
    sends = refs[outer + 1 : outer + 1 + inner]
    pick_ref = refs[outer + 1 + inner]
    half = sends[0].shape[1]
    rows = outer * 2 * tokens
    slot, dest = slot_lanes(dims)
    side = (slot >= reach).astype(jnp.int32)
    slot = slot - side * reach
    meta = jnp.concatenate([r[:, 2 * half :].astype(F32) for r in blocks], axis=0)
    named = jnp.zeros(dest.shape, F32)
    for k in range(top):
        named = jnp.where(meta[:, k : k + 1] == dest, 1.0, named)
    left = lax.broadcasted_iota(jnp.int32, (rows, rows), 1)
    down = lax.broadcasted_iota(jnp.int32, (rows, rows), 0)
    same = count_above(left, tokens, rows) == count_above(down, tokens, rows)
    before = (same & (left < down)).astype(F32).astype(BF16)
    rank = jnp.dot(before, named.astype(BF16), preferred_element_type=F32)
    row = lax.broadcasted_iota(jnp.int32, (rows, 1), 0)
    block = count_above(row, 2 * tokens, rows)
    row_side = count_above(row, tokens, rows) - 2 * block
    position = block * cap + rank.astype(jnp.int32)
    pick = jnp.where((position == slot) & (row_side == side), named, 0.0)
    pick_ref[...] = pick.astype(BF16)
    select_rows(blocks, 0, pick_ref, None, sends)


def select_rows(blocks, array, pick_ref, scale, sends):
    fold, half = sends[0].shape
    table = stacked(blocks, pl.ds(array * half, half))
    out = contract(pick_ref[...], table, 0, 0)
    out = (out if scale is None else out * scale).astype(F32)
    for q, send in enumerate(sends):
        send[...] = out[q * fold : (q + 1) * fold].astype(BF16)


def scale_kernel(dims, *refs):
    outer, inner, tokens, top, cap, reach = dims
    blocks = refs[:outer]
    pick_ref = refs[outer]
    gate_hi_ref, gate_mid_ref, *sends = refs[outer + 1 :]
    half = sends[0].shape[1]
    _, dest = slot_lanes(dims)
    meta = jnp.concatenate([r[:, 2 * half :].astype(F32) for r in blocks], axis=0)
    gate = jnp.zeros(dest.shape, F32)
    for k in range(top):
        value = sum(meta[:, n * top + k : n * top + k + 1] for n in range(1, 4))
        gate = jnp.where(meta[:, k : k + 1] == dest, value, gate)
    gate = pick_ref[...].astype(F32) * gate
    gate_hi = gate.astype(BF16)
    rest = gate - gate_hi.astype(F32)
    gate_mid = rest.astype(BF16)
    gate_lo = (rest - gate_mid.astype(F32)).astype(BF16)
    gate_hi_ref[...] = gate_hi
    gate_mid_ref[...] = gate_mid
    ones = jnp.ones((dest.shape[0], META), BF16)
    column = contract(gate_hi, ones, 0, 0) + contract(gate_mid, ones, 0, 0) + contract(gate_lo, ones, 0, 0)
    select_rows(blocks, 1, pick_ref, column[:, :1], sends)


def stack_kernel(dims, *refs):
    inner, reach, held = dims
    fold, half = refs[0].shape
    live = lax.broadcasted_iota(jnp.int32, (held, half), 0) < reach
    for q, piece in enumerate(flipped(refs[:inner])):
        value = piece[...].astype(F32)
        sides = (value[:held], pltpu.roll(value[fold - held :], fold - reach, 0))
        for n, side in enumerate(sides):
            target = refs[-1].at[q * held : (q + 1) * held, n * half : (n + 1) * half]
            target[...] = jnp.where(live, side, 0.0).astype(BF16)


def load_kernel(parts, *refs):
    sources, targets, turned, sems = refs[:3], refs[4:7], refs[7:10], refs[11]
    copies = []
    for n in range(3):
        step = sources[n].shape[1] // parts
        for m in range(parts):
            index = (0, pl.ds(m * step, step))
            copy = pltpu.make_async_copy(sources[n].at[index], targets[n].at[index], sems.at[n * parts + m])
            copy.start()
            copies.append(copy)
    for n in range(3):
        step = sources[n].shape[1] // parts
        for m in range(parts):
            copies[n * parts + m].wait()
            turned[n][:, m * step : (m + 1) * step] = targets[n][0, m * step : (m + 1) * step, :].T


def core_spans(cores, width, move):
    core = lax.axis_index("etp")
    return [pl.ds(pl.multiple_of(move(core, d, cores) * width, width), width) for d in range(cores)]


def forward_own_kernel(dims, *refs):
    rows, gate_w, up_w, gate_ref, up_ref, _ = refs
    span = core_spans(*dims, traced_origin)[0]
    gate_ref[...] = jnp.dot(rows[...], gate_w[0, span, :], preferred_element_type=F32)
    up_ref[...] = jnp.dot(rows[...], up_w[0, span, :], preferred_element_type=F32)


def forward_kernel(dims, *refs):
    cores, width = dims
    gate_own, up_own, *pieces = refs[: cores + 1]
    gate_w, up_w, down_w = refs[cores + 1 : cores + 4]
    gate_ref, up_ref, act_ref, *parts = refs[-(3 + cores) :]
    spans = core_spans(cores, width, traced_origin)
    gate_pre = gate_own[...]
    up_pre = up_own[...]
    for piece, span in zip(pieces, spans[1:]):
        rows = piece[...]
        gate_pre = gate_pre + jnp.dot(rows, gate_w[0, span, :], preferred_element_type=F32)
        up_pre = up_pre + jnp.dot(rows, up_w[0, span, :], preferred_element_type=F32)
    act = (gate_pre * jax.nn.sigmoid(gate_pre) * up_pre).astype(BF16)
    gate_ref[...] = gate_pre
    up_ref[...] = up_pre
    act_ref[...] = act
    spans = core_spans(cores, width, traced_partner)
    for d in reversed(range(cores)):
        parts[d][...] = jnp.dot(act, down_w[0, :, spans[d]], preferred_element_type=F32).astype(BF16)


def backward_own_kernel(dims, rows, down_t, out_ref):
    span = core_spans(*dims, traced_origin)[0]
    out_ref[...] = jnp.dot(rows[...], down_t[span, :], preferred_element_type=F32)


def backward_kernel(dims, *refs):
    cores, width = dims
    act_own, *pieces = refs[:cores]
    gate_t, up_t, down_t, gate_ref, up_ref = refs[cores : cores + 5]
    gate_out, up_out, *parts = refs[cores + 5 :]
    spans = core_spans(cores, width, traced_origin)
    act_grad = act_own[...]
    for piece, span in zip(pieces, spans[1:]):
        act_grad = act_grad + jnp.dot(piece[...], down_t[span, :], preferred_element_type=F32)
    gate_pre = gate_ref[...]
    sigmoid = jax.nn.sigmoid(gate_pre)
    gate_grad = (act_grad * up_ref[...] * sigmoid * (1.0 + gate_pre * (1.0 - sigmoid))).astype(BF16)
    up_grad = (act_grad * (gate_pre * sigmoid)).astype(BF16)
    gate_out[...] = gate_grad
    up_out[...] = up_grad
    spans = core_spans(cores, width, traced_partner)
    for part, span in zip(parts, spans[1:]):
        value = jnp.dot(gate_grad, gate_t[:, span], preferred_element_type=F32)
        value = value + jnp.dot(up_grad, up_t[:, span], preferred_element_type=F32)
        part[...] = value.astype(BF16)


def input_own_kernel(dims, *refs):
    gate_grad, up_grad, gate_t, up_t = refs[:4]
    span = core_spans(*dims, traced_partner)[0]
    value = jnp.dot(gate_grad[...], gate_t[:, span], preferred_element_type=F32)
    value = value + jnp.dot(up_grad[...], up_t[:, span], preferred_element_type=F32)
    refs[-1][...] = value.astype(BF16)


def down_kernel(dims, chunks, *refs):
    cores, width = dims
    pieces = refs[:cores]
    act_ref = refs[cores]
    out_hbm, result, out_sems = refs[-3:]
    core = lax.axis_index("etp")
    act = act_ref[...]
    chunk = width // chunks
    copies = []
    for d in range(cores):
        rows = pieces[d][...]
        base = traced_origin(core, d, cores) * width
        for n in range(chunks):
            result[d * chunks + n] = contract(act, rows[:, n * chunk : (n + 1) * chunk], 0, 0).astype(BF16)
            span = pl.ds(pl.multiple_of(base + n * chunk, chunk), chunk)
            copy = pltpu.make_async_copy(
                result.at[d * chunks + n], out_hbm.at[0, :, span], out_sems.at[d * chunks + n]
            )
            copy.start()
            copies.append(copy)
    for copy in copies:
        copy.wait()


def split_kernel(dims, *refs):
    cores, inner, reach, held = dims
    total = refs[0][...].astype(F32)
    for part in refs[1:cores]:
        total = total + part[...].astype(F32)
    half = total.shape[1] // 2
    rest = jnp.zeros((2 * reach - held, half), F32)
    for q in range(inner):
        rows = total[q * held : (q + 1) * held]
        right = pltpu.roll(rows[:, half:], held - reach, 0)
        value = jnp.concatenate([rows[:, :half], rest], axis=0) + jnp.concatenate([rest, right], axis=0)
        refs[q - inner][...] = value.astype(BF16)


def combine_kernel(dims, weighted, *refs):
    outer, inner, unit = dims
    tables = refs[inner : inner + weighted]
    outs = refs[-outer:]
    rows = stacked(flipped(refs[:inner]))
    total = None
    for table in tables:
        term = jnp.dot(table[...], rows, preferred_element_type=F32)
        total = term if total is None else total + term
    for b in range(outer):
        outs[b][...] = total[b * unit : (b + 1) * unit].astype(BF16)


def final_kernel(dims, *refs):
    outer, tokens, half = dims
    out_ref = refs[-2]
    total = refs[0][...].astype(F32)
    for part in refs[1:outer]:
        total = total + part[...].astype(F32)
    out_ref[:, :half] = total[:tokens].astype(BF16)
    out_ref[:, half:] = total[tokens:].astype(BF16)


def shape(rows, columns, kind=BF16):
    return jax.ShapeDtypeStruct((rows, columns), kind)


def on_device(hidden_in, expert_ids, gate_weights, out_grad, gate_weight, up_weight, down_weight):
    tokens, top = expert_ids.shape
    experts = lax.axis_size("expert")
    cores = lax.axis_size("etp")
    outer, inner = group_sizes(experts)
    cap = min(tokens, tokens * top // experts + 1)
    width = hidden_in.shape[1]
    half = width // 2
    hidden = gate_weight.shape[2]
    reach = outer * cap
    held = -(-reach // 16) * 16
    rows = inner * held
    unit = 2 * tokens

    with jax.named_scope("prepare"):
        packed = pl.pallas_call(
            functools.partial(prepare_kernel, (tokens, top, half)),
            out_shape=shape(unit, 2 * half + META),
            in_specs=hbm_specs(4),
            out_specs=pl.BlockSpec(memory_space=pltpu.VMEM),
            scratch_shapes=[
                pltpu.VMEM((top, tokens), jnp.int32),
                pltpu.VMEM((top, tokens), F32),
                pltpu.VMEM((tokens, width), BF16),
                pltpu.VMEM((tokens, width), BF16),
                pltpu.SemaphoreType.DMA((4,)),
            ],
            compiler_params=params(),
            name="prepare",
        )(in_hbm(expert_ids.T), in_hbm(gate_weights.T), in_hbm(hidden_in), in_hbm(out_grad))

    with jax.named_scope("gather_blocks"):
        blocks = [packed] + [send_outer(packed, s, outer, inner) for s in range(1, outer)]

    piece_shapes = [shape(2 * reach, half)] * inner
    table_shape = shape(outer * unit, inner * 2 * reach)
    with jax.named_scope("load_weights"):
        weights = (gate_weight, up_weight, down_weight)
        weight_parts = 4
        loaded = pl.pallas_call(
            functools.partial(load_kernel, weight_parts),
            out_shape=[pltpu.VMEM(w.shape, BF16) for w in weights]
            + [pltpu.VMEM((w.shape[2], w.shape[1]), BF16) for w in weights]
            + [shape(8, META, F32)],
            in_specs=hbm_specs(3) + whole_specs(1),
            out_specs=whole_specs(7),
            scratch_shapes=[pltpu.SemaphoreType.DMA((3 * weight_parts,))],
            compiler_params=params(),
            name="load_weights",
        )(*[in_hbm(w) for w in weights], packed)
        weights, turned = loaded[:3], loaded[3:6]

    with jax.named_scope("route"):
        dims = (outer, inner, tokens, top, cap, reach)
        *in_sends, pick = pl.pallas_call(
            functools.partial(route_kernel, dims),
            out_shape=piece_shapes + [table_shape],
            in_specs=whole_specs(outer + 1),
            out_specs=whole_specs(inner + 1),
            compiler_params=params(),
            name="route",
        )(*blocks, loaded[6])

    def spread(sends):
        return [sends[0]] + [send_inner(sends[q], q, outer, inner) for q in range(1, inner)]

    def gather_cores(pieces, after=()):
        stack = pl.pallas_call(
            functools.partial(stack_kernel, (inner, reach, held)),
            out_shape=shape(rows, width),
            in_specs=whole_specs(inner) + any_specs(len(after)),
            out_specs=pl.BlockSpec(memory_space=pltpu.VMEM),
            compiler_params=params(),
            name="stack",
        )(*flipped(pieces), *after)
        return [stack] + [send_core(stack, d, cores) for d in range(1, cores)]

    with jax.named_scope("exchange_in"):
        in_pieces = spread(in_sends)
    with jax.named_scope("scale"):
        gate_hi, gate_lo, *grad_sends = pl.pallas_call(
            functools.partial(scale_kernel, dims),
            out_shape=[table_shape] * 2 + piece_shapes,
            in_specs=whole_specs(outer + 1),
            out_specs=whole_specs(inner + 2),
            compiler_params=params(),
            name="scale",
        )(*blocks, pick)
    with jax.named_scope("exchange_grad"):
        grad_pieces = spread(grad_sends)
    with jax.named_scope("gather_in"):
        in_rows = gather_cores(in_pieces)
        with jax.named_scope("forward_own"):
            gate_own, up_own, started = pl.pallas_call(
                functools.partial(forward_own_kernel, (cores, width)),
                out_shape=[shape(rows, hidden, F32)] * 2 + [shape(8, META, F32)],
                in_specs=whole_specs(3),
                out_specs=whole_specs(3),
                compiler_params=params(),
                name="forward_own",
            )(in_rows[0], *weights[:2])
        grad_rows = gather_cores(grad_pieces, (started,))

    dims = (cores, width)
    with jax.named_scope("forward"):
        gate_pre, up_pre, act, *out_parts = pl.pallas_call(
            functools.partial(forward_kernel, dims),
            out_shape=[shape(rows, hidden, F32)] * 2 + [shape(rows, hidden)] + [shape(rows, width)] * cores,
            in_specs=whole_specs(cores + 4) + any_specs(1),
            out_specs=whole_specs(3 + cores),
            compiler_params=params(),
            name="forward",
        )(gate_own, up_own, *in_rows[1:], *weights, grad_pieces[-1])

    def give_back(parts, after=()):
        got = [parts[0]] + [send_core(parts[d], d, cores) for d in range(1, cores)]
        sends = pl.pallas_call(
            functools.partial(split_kernel, (cores, inner, reach, held)),
            out_shape=piece_shapes,
            in_specs=whole_specs(cores) + any_specs(len(after)),
            out_specs=whole_specs(inner),
            compiler_params=params(),
            name="split",
        )(*got, *after)
        return [sends[0]] + [send_inner(sends[q], q, outer, inner, back=True) for q in range(1, inner)]

    def combine(pieces, tables):
        blocks = pl.pallas_call(
            functools.partial(combine_kernel, (outer, inner, unit), len(tables)),
            out_shape=[shape(unit, half)] * outer,
            in_specs=whole_specs(inner + len(tables)),
            out_specs=whole_specs(outer),
            compiler_params=params(),
            name="combine",
        )(*flipped(pieces), *tables)
        return [blocks[0]] + [send_outer(blocks[s], s, outer, inner, back=True) for s in range(1, outer)]

    def finish(blocks, after=()):
        return pl.pallas_call(
            functools.partial(final_kernel, (outer, tokens, half)),
            out_shape=[shape(tokens, width), shape(8, META, F32)],
            in_specs=whole_specs(outer + len(after)),
            out_specs=whole_specs(2),
            compiler_params=params(),
            name="final",
        )(*flipped(blocks), *after)

    with jax.named_scope("return_out"):
        out_back = give_back(out_parts)
        out_blocks = combine(out_back, (gate_hi, gate_lo))

    with jax.named_scope("backward"):
        gate_t, up_t, down_t = turned
        act_own = pl.pallas_call(
            functools.partial(backward_own_kernel, dims),
            out_shape=shape(rows, hidden, F32),
            in_specs=whole_specs(2),
            out_specs=pl.BlockSpec(memory_space=pltpu.VMEM),
            compiler_params=params(),
            name="backward_own",
        )(grad_rows[0], down_t)
        gate_grad, up_grad, *grad_parts = pl.pallas_call(
            functools.partial(backward_kernel, dims),
            out_shape=[shape(rows, hidden)] * 2 + [shape(rows, width)] * (cores - 1),
            in_specs=whole_specs(cores + 5),
            out_specs=whole_specs(cores + 1),
            compiler_params=params(),
            name="backward",
        )(act_own, *grad_rows[1:], gate_t, up_t, down_t, gate_pre, up_pre)
        own_part = pl.pallas_call(
            functools.partial(input_own_kernel, dims),
            out_shape=shape(rows, width),
            in_specs=whole_specs(4) + any_specs(1),
            out_specs=pl.BlockSpec(memory_space=pltpu.VMEM),
            compiler_params=params(),
            name="input_own",
        )(gate_grad, up_grad, gate_t, up_t, out_back[0])
        grad_parts = [own_part, *grad_parts]

    with jax.named_scope("return_grad"):
        back_blocks = combine(give_back(grad_parts, out_back[:1]), (pick,))

    with jax.named_scope("down_grad"):
        chunks = max(1, width // 512)
        down_grad = pl.pallas_call(
            functools.partial(down_kernel, dims, chunks),
            out_shape=pltpu.HBM(down_weight.shape, BF16),
            in_specs=whole_specs(cores + 1) + any_specs(1),
            out_specs=pl.BlockSpec(memory_space=pltpu.HBM),
            scratch_shapes=[
                pltpu.VMEM((cores * chunks, hidden, width // chunks), BF16),
                pltpu.SemaphoreType.DMA((cores * chunks,)),
            ],
            compiler_params=params(),
            name="down_grad",
        )(*grad_rows, act, back_blocks[0])

    mixed_out, done = finish(out_blocks)
    input_grad, done = finish(back_blocks, (done,))
    return (mixed_out, input_grad, down_grad)


def solution(mesh):
    return jax.shard_map(
        on_device,
        mesh=mesh,
        in_specs=(
            P("expert", "etp"),
            P("expert", None),
            P("expert", None),
            P("expert", "etp"),
            P("expert", None, "etp"),
            P("expert", None, "etp"),
            P("expert", "etp", None),
        ),
        out_specs=(P("expert", "etp"), P("expert", "etp"), P("expert", "etp", None)),
        check_vma=False,
    )
```

```python
import functools
import jax
import jax.numpy as jnp
from jax import lax
from jax.experimental import pallas as pl
from jax.experimental.pallas import tpu as pltpu
from jax.sharding import PartitionSpec as P

BF16 = jnp.bfloat16
F32 = jnp.float32
META = 128
SUBLANES = 8
VMEM_LIMIT = 20 * 1024 * 1024


def group_sizes(experts):
    inner = 1
    while inner * inner * 4 <= experts and experts % (inner * 2) == 0:
        inner *= 2
    return experts // inner, inner


def partner(index, step, size):
    return index ^ step if size & (size - 1) == 0 else (index + step) % size


def origin(index, step, size):
    return index ^ step if size & (size - 1) == 0 else (index - step) % size


def traced_partner(index, step, size):
    return index ^ step if size & (size - 1) == 0 else lax.rem(index + step, size)


def traced_origin(index, step, size):
    return index ^ step if size & (size - 1) == 0 else lax.rem(index + size - step, size)


def send_outer(x, step, outer, inner, back=False):
    move = origin if back else partner
    pairs = [
        (a * inner + b, move(a, step, outer) * inner + b) for a in range(outer) for b in range(inner)
    ]
    return lax.ppermute(x, "expert", pairs)


def send_inner(x, step, outer, inner, back=False):
    move = origin if back else partner
    pairs = [
        (a * inner + b, a * inner + move(b, step, inner)) for a in range(outer) for b in range(inner)
    ]
    return lax.ppermute(x, "expert", pairs)


def send_core(x, step, cores, back=False):
    move = origin if back else partner
    return lax.ppermute(x, "etp", [(i, move(i, step, cores)) for i in range(cores)])


def flipped(parts):
    return [parts[0], *parts[:0:-1]]


def contract(left, right, left_dim, right_dim):
    return lax.dot_general(
        left, right, (((left_dim,), (right_dim,)), ((), ())), preferred_element_type=F32
    )


def whole_specs(count):
    return [pl.BlockSpec(memory_space=pltpu.VMEM)] * count


def any_specs(count):
    return [pl.BlockSpec(memory_space=pl.ANY)] * count


def params():
    return pltpu.CompilerParams(vmem_limit_bytes=VMEM_LIMIT)


def in_hbm(x):
    return pltpu.with_memory_space_constraint(x, pltpu.HBM)


def hbm_specs(count):
    return [pl.BlockSpec(memory_space=pltpu.HBM)] * count


def prepare_kernel(dims, *refs):
    tokens, top, half = dims
    sources, out_ref, held, sems = refs[:4], refs[4], refs[5:9], refs[9]
    copies = [pltpu.make_async_copy(a, b, sems.at[n]) for n, (a, b) in enumerate(zip(sources, held))]
    for copy in copies:
        copy.start()
    for copy in copies:
        copy.wait()
    ids_ref, gates_ref, hidden_ref, grad_ref = held
    gates = gates_ref[...]
    gate_hi = gates.astype(BF16)
    rest = gates - gate_hi.astype(F32)
    gate_mid = rest.astype(BF16)
    gate_lo = rest - gate_mid.astype(F32)
    values = [ids_ref[...].astype(F32), gate_hi.astype(F32), gate_mid.astype(F32), gate_lo]
    values = jnp.concatenate(values, axis=0).astype(BF16)
    entry = lax.broadcasted_iota(jnp.int32, (4 * top, META), 0)
    lane = lax.broadcasted_iota(jnp.int32, (4 * top, META), 1)
    meta = contract(values, (lane == entry).astype(F32).astype(BF16), 0, 0)
    meta = jnp.concatenate([meta, meta], axis=0)
    tiles = 2 * tokens // SUBLANES
    for n, source in enumerate((hidden_ref, grad_ref)):
        value = source[...].astype(F32)
        value = jnp.concatenate([value[:, :half], value[:, half:]], axis=0)
        for i in range(tiles):
            start = (n * tiles + i) * half
            out_ref[:, start : start + half] = value[i * SUBLANES : (i + 1) * SUBLANES].astype(BF16)
    packed = meta[:SUBLANES]
    for i in range(1, tiles):
        packed = packed + pltpu.roll(meta[i * SUBLANES : (i + 1) * SUBLANES], i * 4 * top, 1)
    out_ref[:, 2 * tiles * half :] = packed.astype(BF16)


def block_rows(blocks, start, width, tiles, shift=0):
    parts = []
    for block in blocks:
        for i in range(tiles):
            if shift:
                part = block[:, start : start + width].astype(F32)
                parts.append(pltpu.roll(part, width - i * shift, 1) if i else part)
            else:
                parts.append(block[:, start + i * width : start + (i + 1) * width].astype(F32))
    return jnp.concatenate(parts, axis=0)


def stacked(refs):
    return jnp.concatenate([r[...].astype(F32) for r in refs], axis=0).astype(BF16)


def count_above(index, unit, total):
    value = jnp.zeros_like(index)
    for m in range(unit, total, unit):
        value = value + (index >= m).astype(jnp.int32)
    return value


def slot_lanes(dims):
    outer, inner, tokens, top, cap, reach = dims
    fold = 2 * reach
    shape = (outer * 2 * tokens, inner * fold)
    me = lax.axis_index("expert")
    my_inner = lax.rem(me, inner)
    my_base = me - my_inner
    lane = lax.broadcasted_iota(jnp.int32, shape, 1)
    step = count_above(lane, fold, shape[1])
    dest = jnp.zeros(shape, F32)
    for q in range(inner):
        expert = (my_base + traced_partner(my_inner, q, inner)).astype(F32)
        dest = jnp.where(step == q, expert, dest)
    return lane - step * fold, dest


def route_kernel(dims, *refs):
    outer, inner, tokens, top, cap, reach = dims
    blocks = flipped(refs[:outer])
    sends = refs[outer + 1 : outer + 1 + inner]
    pick_ref = refs[outer + 1 + inner]
    half = sends[0].shape[1]
    rows = outer * 2 * tokens
    slot, dest = slot_lanes(dims)
    side = (slot >= reach).astype(jnp.int32)
    slot = slot - side * reach
    tiles = 2 * tokens // SUBLANES
    meta = block_rows(blocks, 2 * tiles * half, META, tiles, 4 * top)
    named = jnp.zeros(dest.shape, F32)
    for k in range(top):
        named = jnp.where(meta[:, k : k + 1] == dest, 1.0, named)
    left = lax.broadcasted_iota(jnp.int32, (rows, rows), 1)
    down = lax.broadcasted_iota(jnp.int32, (rows, rows), 0)
    same = count_above(left, tokens, rows) == count_above(down, tokens, rows)
    before = (same & (left < down)).astype(F32).astype(BF16)
    rank = jnp.dot(before, named.astype(BF16), preferred_element_type=F32)
    row = lax.broadcasted_iota(jnp.int32, (rows, 1), 0)
    block = count_above(row, 2 * tokens, rows)
    row_side = count_above(row, tokens, rows) - 2 * block
    position = block * cap + rank.astype(jnp.int32)
    pick = jnp.where((position == slot) & (row_side == side), named, 0.0)
    pick_ref[...] = pick.astype(BF16)
    select_rows(blocks, 0, pick_ref, None, sends)


def select_rows(blocks, array, pick_ref, scale, sends):
    fold, half = sends[0].shape
    tiles = pick_ref.shape[0] // (len(blocks) * SUBLANES)
    table = block_rows(blocks, array * tiles * half, half, tiles).astype(BF16)
    out = contract(pick_ref[...], table, 0, 0)
    out = (out if scale is None else out * scale).astype(F32)
    for q, send in enumerate(sends):
        send[...] = out[q * fold : (q + 1) * fold].astype(BF16)


def scale_kernel(dims, *refs):
    outer, inner, tokens, top, cap, reach = dims
    blocks = flipped(refs[:outer])
    pick_ref = refs[outer]
    gate_hi_ref, gate_mid_ref, *sends = refs[outer + 1 :]
    half = sends[0].shape[1]
    _, dest = slot_lanes(dims)
    tiles = 2 * tokens // SUBLANES
    meta = block_rows(blocks, 2 * tiles * half, META, tiles, 4 * top)
    gate = jnp.zeros(dest.shape, F32)
    for k in range(top):
        value = sum(meta[:, n * top + k : n * top + k + 1] for n in range(1, 4))
        gate = jnp.where(meta[:, k : k + 1] == dest, value, gate)
    gate = pick_ref[...].astype(F32) * gate
    gate_hi = gate.astype(BF16)
    rest = gate - gate_hi.astype(F32)
    gate_mid = rest.astype(BF16)
    gate_lo = (rest - gate_mid.astype(F32)).astype(BF16)
    gate_hi_ref[...] = gate_hi
    gate_mid_ref[...] = gate_mid
    ones = jnp.ones((dest.shape[0], META), BF16)
    column = contract(gate_hi, ones, 0, 0) + contract(gate_mid, ones, 0, 0) + contract(gate_lo, ones, 0, 0)
    select_rows(blocks, 1, pick_ref, column[:, :1], sends)


def stack_kernel(dims, *refs):
    inner, reach, held = dims
    fold, half = refs[0].shape
    live = lax.broadcasted_iota(jnp.int32, (held, half), 0) < reach
    for q, piece in enumerate(flipped(refs[:inner])):
        value = piece[...].astype(F32)
        sides = (value[:held], pltpu.roll(value[fold - held :], fold - reach, 0))
        for n, side in enumerate(sides):
            target = refs[-1].at[q * held : (q + 1) * held, n * half : (n + 1) * half]
            target[...] = jnp.where(live, side, 0.0).astype(BF16)


def load_kernel(parts, *refs):
    sources, targets, turned, sems = refs[:3], refs[4:7], refs[7:10], refs[11]
    copies = []
    for n in range(3):
        step = sources[n].shape[1] // parts
        for m in range(parts):
            index = (0, pl.ds(m * step, step))
            copy = pltpu.make_async_copy(sources[n].at[index], targets[n].at[index], sems.at[n * parts + m])
            copy.start()
            copies.append(copy)
    for n in range(3):
        step = sources[n].shape[1] // parts
        for m in range(parts):
            copies[n * parts + m].wait()
            turned[n][:, m * step : (m + 1) * step] = targets[n][0, m * step : (m + 1) * step, :].T


def core_spans(cores, width, move):
    core = lax.axis_index("etp")
    return [pl.ds(pl.multiple_of(move(core, d, cores) * width, width), width) for d in range(cores)]


def forward_own_kernel(dims, *refs):
    rows, gate_w, up_w, gate_ref, up_ref, _ = refs
    span = core_spans(*dims, traced_origin)[0]
    gate_ref[...] = jnp.dot(rows[...], gate_w[0, span, :], preferred_element_type=F32)
    up_ref[...] = jnp.dot(rows[...], up_w[0, span, :], preferred_element_type=F32)


def forward_kernel(dims, *refs):
    cores, width = dims
    gate_own, up_own, *pieces = refs[: cores + 1]
    gate_w, up_w, down_w = refs[cores + 1 : cores + 4]
    gate_ref, up_ref, act_ref, *parts = refs[-(3 + cores) :]
    spans = core_spans(cores, width, traced_origin)
    gate_pre = gate_own[...]
    up_pre = up_own[...]
    for piece, span in zip(pieces, spans[1:]):
        rows = piece[...]
        gate_pre = gate_pre + jnp.dot(rows, gate_w[0, span, :], preferred_element_type=F32)
        up_pre = up_pre + jnp.dot(rows, up_w[0, span, :], preferred_element_type=F32)
    act = (gate_pre * jax.nn.sigmoid(gate_pre) * up_pre).astype(BF16)
    gate_ref[...] = gate_pre
    up_ref[...] = up_pre
    act_ref[...] = act
    spans = core_spans(cores, width, traced_partner)
    for d in reversed(range(cores)):
        parts[d][...] = jnp.dot(act, down_w[0, :, spans[d]], preferred_element_type=F32).astype(BF16)


def backward_own_kernel(dims, rows, down_t, out_ref):
    span = core_spans(*dims, traced_origin)[0]
    out_ref[...] = jnp.dot(rows[...], down_t[span, :], preferred_element_type=F32)


def backward_kernel(dims, *refs):
    cores, width = dims
    act_own, *pieces = refs[:cores]
    gate_t, up_t, down_t, gate_ref, up_ref = refs[cores : cores + 5]
    gate_out, up_out, *parts = refs[cores + 5 :]
    spans = core_spans(cores, width, traced_origin)
    act_grad = act_own[...]
    for piece, span in zip(pieces, spans[1:]):
        act_grad = act_grad + jnp.dot(piece[...], down_t[span, :], preferred_element_type=F32)
    gate_pre = gate_ref[...]
    sigmoid = jax.nn.sigmoid(gate_pre)
    gate_grad = (act_grad * up_ref[...] * sigmoid * (1.0 + gate_pre * (1.0 - sigmoid))).astype(BF16)
    up_grad = (act_grad * (gate_pre * sigmoid)).astype(BF16)
    gate_out[...] = gate_grad
    up_out[...] = up_grad
    spans = core_spans(cores, width, traced_partner)
    for part, span in zip(parts, spans[1:]):
        value = jnp.dot(gate_grad, gate_t[:, span], preferred_element_type=F32)
        value = value + jnp.dot(up_grad, up_t[:, span], preferred_element_type=F32)
        part[...] = value.astype(BF16)


def input_own_kernel(dims, *refs):
    gate_grad, up_grad, gate_t, up_t = refs[:4]
    span = core_spans(*dims, traced_partner)[0]
    value = jnp.dot(gate_grad[...], gate_t[:, span], preferred_element_type=F32)
    value = value + jnp.dot(up_grad[...], up_t[:, span], preferred_element_type=F32)
    refs[-1][...] = value.astype(BF16)


def down_kernel(dims, chunks, *refs):
    cores, width = dims
    pieces = refs[:cores]
    act_ref = refs[cores]
    out_hbm, result, out_sems = refs[-3:]
    core = lax.axis_index("etp")
    act = act_ref[...]
    chunk = width // chunks
    copies = []
    for d in range(cores):
        rows = pieces[d][...]
        base = traced_origin(core, d, cores) * width
        for n in range(chunks):
            result[d * chunks + n] = contract(act, rows[:, n * chunk : (n + 1) * chunk], 0, 0).astype(BF16)
            span = pl.ds(pl.multiple_of(base + n * chunk, chunk), chunk)
            copy = pltpu.make_async_copy(
                result.at[d * chunks + n], out_hbm.at[0, :, span], out_sems.at[d * chunks + n]
            )
            copy.start()
            copies.append(copy)
    for copy in copies:
        copy.wait()


def split_kernel(dims, *refs):
    cores, inner, reach, held = dims
    total = refs[0][...].astype(F32)
    for part in refs[1:cores]:
        total = total + part[...].astype(F32)
    half = total.shape[1] // 2
    rest = jnp.zeros((2 * reach - held, half), F32)
    for q in range(inner):
        rows = total[q * held : (q + 1) * held]
        right = pltpu.roll(rows[:, half:], held - reach, 0)
        value = jnp.concatenate([rows[:, :half], rest], axis=0) + jnp.concatenate([rest, right], axis=0)
        refs[q - inner][...] = value.astype(BF16)


def combine_kernel(dims, weighted, *refs):
    outer, inner, unit = dims
    tables = refs[inner : inner + weighted]
    outs = refs[-outer:]
    rows = stacked(flipped(refs[:inner]))
    total = None
    for table in tables:
        term = jnp.dot(table[...], rows, preferred_element_type=F32)
        total = term if total is None else total + term
    for b in range(outer):
        outs[b][...] = total[b * unit : (b + 1) * unit].astype(BF16)


def final_kernel(dims, *refs):
    outer, tokens, half = dims
    out_ref = refs[-2]
    total = refs[0][...].astype(F32)
    for part in refs[1:outer]:
        total = total + part[...].astype(F32)
    out_ref[:, :half] = total[:tokens].astype(BF16)
    out_ref[:, half:] = total[tokens:].astype(BF16)


def shape(rows, columns, kind=BF16):
    return jax.ShapeDtypeStruct((rows, columns), kind)


def on_device(hidden_in, expert_ids, gate_weights, out_grad, gate_weight, up_weight, down_weight):
    tokens, top = expert_ids.shape
    experts = lax.axis_size("expert")
    cores = lax.axis_size("etp")
    outer, inner = group_sizes(experts)
    cap = min(tokens, tokens * top // experts + 1)
    width = hidden_in.shape[1]
    half = width // 2
    hidden = gate_weight.shape[2]
    reach = outer * cap
    held = -(-reach // 16) * 16
    rows = inner * held
    unit = 2 * tokens

    with jax.named_scope("prepare"):
        packed = pl.pallas_call(
            functools.partial(prepare_kernel, (tokens, top, half)),
            out_shape=shape(SUBLANES, 2 * unit // SUBLANES * half + META),
            in_specs=hbm_specs(4),
            out_specs=pl.BlockSpec(memory_space=pltpu.VMEM),
            scratch_shapes=[
                pltpu.VMEM((top, tokens), jnp.int32),
                pltpu.VMEM((top, tokens), F32),
                pltpu.VMEM((tokens, width), BF16),
                pltpu.VMEM((tokens, width), BF16),
                pltpu.SemaphoreType.DMA((4,)),
            ],
            compiler_params=params(),
            name="prepare",
        )(in_hbm(expert_ids.T), in_hbm(gate_weights.T), in_hbm(hidden_in), in_hbm(out_grad))

    with jax.named_scope("gather_blocks"):
        blocks = [packed] + [send_outer(packed, s, outer, inner) for s in range(1, outer)]

    piece_shapes = [shape(2 * reach, half)] * inner
    table_shape = shape(outer * unit, inner * 2 * reach)
    with jax.named_scope("load_weights"):
        weights = (gate_weight, up_weight, down_weight)
        weight_parts = 4
        loaded = pl.pallas_call(
            functools.partial(load_kernel, weight_parts),
            out_shape=[pltpu.VMEM(w.shape, BF16) for w in weights]
            + [pltpu.VMEM((w.shape[2], w.shape[1]), BF16) for w in weights]
            + [shape(8, META, F32)],
            in_specs=hbm_specs(3) + whole_specs(1),
            out_specs=whole_specs(7),
            scratch_shapes=[pltpu.SemaphoreType.DMA((3 * weight_parts,))],
            compiler_params=params(),
            name="load_weights",
        )(*[in_hbm(w) for w in weights], packed)
        weights, turned = loaded[:3], loaded[3:6]

    with jax.named_scope("route"):
        dims = (outer, inner, tokens, top, cap, reach)
        *in_sends, pick = pl.pallas_call(
            functools.partial(route_kernel, dims),
            out_shape=piece_shapes + [table_shape],
            in_specs=whole_specs(outer + 1),
            out_specs=whole_specs(inner + 1),
            compiler_params=params(),
            name="route",
        )(*flipped(blocks), loaded[6])

    def spread(sends):
        return [sends[0]] + [send_inner(sends[q], q, outer, inner) for q in range(1, inner)]

    def gather_cores(pieces, after=()):
        stack = pl.pallas_call(
            functools.partial(stack_kernel, (inner, reach, held)),
            out_shape=shape(rows, width),
            in_specs=whole_specs(inner) + any_specs(len(after)),
            out_specs=pl.BlockSpec(memory_space=pltpu.VMEM),
            compiler_params=params(),
            name="stack",
        )(*flipped(pieces), *after)
        return [stack] + [send_core(stack, d, cores) for d in range(1, cores)]

    with jax.named_scope("exchange_in"):
        in_pieces = spread(in_sends)
    with jax.named_scope("scale"):
        gate_hi, gate_lo, *grad_sends = pl.pallas_call(
            functools.partial(scale_kernel, dims),
            out_shape=[table_shape] * 2 + piece_shapes,
            in_specs=whole_specs(outer + 1),
            out_specs=whole_specs(inner + 2),
            compiler_params=params(),
            name="scale",
        )(*flipped(blocks), pick)
    with jax.named_scope("exchange_grad"):
        grad_pieces = spread(grad_sends)
    with jax.named_scope("gather_in"):
        in_rows = gather_cores(in_pieces)
        with jax.named_scope("forward_own"):
            gate_own, up_own, started = pl.pallas_call(
                functools.partial(forward_own_kernel, (cores, width)),
                out_shape=[shape(rows, hidden, F32)] * 2 + [shape(8, META, F32)],
                in_specs=whole_specs(3),
                out_specs=whole_specs(3),
                compiler_params=params(),
                name="forward_own",
            )(in_rows[0], *weights[:2])
        grad_rows = gather_cores(grad_pieces, (started,))

    dims = (cores, width)
    with jax.named_scope("forward"):
        gate_pre, up_pre, act, *out_parts = pl.pallas_call(
            functools.partial(forward_kernel, dims),
            out_shape=[shape(rows, hidden, F32)] * 2 + [shape(rows, hidden)] + [shape(rows, width)] * cores,
            in_specs=whole_specs(cores + 4) + any_specs(1),
            out_specs=whole_specs(3 + cores),
            compiler_params=params(),
            name="forward",
        )(gate_own, up_own, *in_rows[1:], *weights, grad_pieces[-1])

    def give_back(parts, after=()):
        got = [parts[0]] + [send_core(parts[d], d, cores) for d in range(1, cores)]
        sends = pl.pallas_call(
            functools.partial(split_kernel, (cores, inner, reach, held)),
            out_shape=piece_shapes,
            in_specs=whole_specs(cores) + any_specs(len(after)),
            out_specs=whole_specs(inner),
            compiler_params=params(),
            name="split",
        )(*got, *after)
        return [sends[0]] + [send_inner(sends[q], q, outer, inner, back=True) for q in range(1, inner)]

    def combine(pieces, tables):
        blocks = pl.pallas_call(
            functools.partial(combine_kernel, (outer, inner, unit), len(tables)),
            out_shape=[shape(unit, half)] * outer,
            in_specs=whole_specs(inner + len(tables)),
            out_specs=whole_specs(outer),
            compiler_params=params(),
            name="combine",
        )(*flipped(pieces), *tables)
        return [blocks[0]] + [send_outer(blocks[s], s, outer, inner, back=True) for s in range(1, outer)]

    def finish(blocks, after=()):
        return pl.pallas_call(
            functools.partial(final_kernel, (outer, tokens, half)),
            out_shape=[shape(tokens, width), shape(8, META, F32)],
            in_specs=whole_specs(outer + len(after)),
            out_specs=whole_specs(2),
            compiler_params=params(),
            name="final",
        )(*flipped(blocks), *after)

    with jax.named_scope("return_out"):
        out_back = give_back(out_parts)
        out_blocks = combine(out_back, (gate_hi, gate_lo))

    with jax.named_scope("backward"):
        gate_t, up_t, down_t = turned
        act_own = pl.pallas_call(
            functools.partial(backward_own_kernel, dims),
            out_shape=shape(rows, hidden, F32),
            in_specs=whole_specs(2),
            out_specs=pl.BlockSpec(memory_space=pltpu.VMEM),
            compiler_params=params(),
            name="backward_own",
        )(grad_rows[0], down_t)
        gate_grad, up_grad, *grad_parts = pl.pallas_call(
            functools.partial(backward_kernel, dims),
            out_shape=[shape(rows, hidden)] * 2 + [shape(rows, width)] * (cores - 1),
            in_specs=whole_specs(cores + 5),
            out_specs=whole_specs(cores + 1),
            compiler_params=params(),
            name="backward",
        )(act_own, *grad_rows[1:], gate_t, up_t, down_t, gate_pre, up_pre)
        own_part = pl.pallas_call(
            functools.partial(input_own_kernel, dims),
            out_shape=shape(rows, width),
            in_specs=whole_specs(4) + any_specs(1),
            out_specs=pl.BlockSpec(memory_space=pltpu.VMEM),
            compiler_params=params(),
            name="input_own",
        )(gate_grad, up_grad, gate_t, up_t, out_back[0])
        grad_parts = [own_part, *grad_parts]

    with jax.named_scope("return_grad"):
        back_blocks = combine(give_back(grad_parts, out_back[:1]), (pick,))

    with jax.named_scope("down_grad"):
        chunks = max(1, width // 512)
        down_grad = pl.pallas_call(
            functools.partial(down_kernel, dims, chunks),
            out_shape=pltpu.HBM(down_weight.shape, BF16),
            in_specs=whole_specs(cores + 1) + any_specs(1),
            out_specs=pl.BlockSpec(memory_space=pltpu.HBM),
            scratch_shapes=[
                pltpu.VMEM((cores * chunks, hidden, width // chunks), BF16),
                pltpu.SemaphoreType.DMA((cores * chunks,)),
            ],
            compiler_params=params(),
            name="down_grad",
        )(*grad_rows, act, back_blocks[0])

    mixed_out, done = finish(out_blocks)
    input_grad, done = finish(back_blocks, (done,))
    return (mixed_out, input_grad, down_grad)


def solution(mesh):
    return jax.shard_map(
        on_device,
        mesh=mesh,
        in_specs=(
            P("expert", "etp"),
            P("expert", None),
            P("expert", None),
            P("expert", "etp"),
            P("expert", None, "etp"),
            P("expert", None, "etp"),
            P("expert", "etp", None),
        ),
        out_specs=(P("expert", "etp"), P("expert", "etp"), P("expert", "etp", None)),
        check_vma=False,
    )
```

```python
import functools
import jax
import jax.numpy as jnp
from jax import lax
from jax.experimental import pallas as pl
from jax.experimental.pallas import tpu as pltpu
from jax.sharding import PartitionSpec as P

BF16 = jnp.bfloat16
F32 = jnp.float32
META = 128
COSTS = {"PREPARE": 20, "ROUTE0": 9, "ROUTE1": 9}
SUBLANES = 8
VMEM_LIMIT = 20 * 1024 * 1024


def group_sizes(experts):
    inner = 1
    while inner * inner * 4 <= experts and experts % (inner * 2) == 0:
        inner *= 2
    return experts // inner, inner


def partner(index, step, size):
    return index ^ step if size & (size - 1) == 0 else (index + step) % size


def origin(index, step, size):
    return index ^ step if size & (size - 1) == 0 else (index - step) % size


def traced_partner(index, step, size):
    return index ^ step if size & (size - 1) == 0 else lax.rem(index + step, size)


def traced_origin(index, step, size):
    return index ^ step if size & (size - 1) == 0 else lax.rem(index + size - step, size)


def send_outer(x, step, outer, inner, back=False):
    move = origin if back else partner
    pairs = [
        (a * inner + b, move(a, step, outer) * inner + b) for a in range(outer) for b in range(inner)
    ]
    return lax.ppermute(x, "expert", pairs)


def send_inner(x, step, outer, inner, back=False):
    move = origin if back else partner
    pairs = [
        (a * inner + b, a * inner + move(b, step, inner)) for a in range(outer) for b in range(inner)
    ]
    return lax.ppermute(x, "expert", pairs)


def send_core(x, step, cores, back=False):
    move = origin if back else partner
    return lax.ppermute(x, "etp", [(i, move(i, step, cores)) for i in range(cores)])


def flipped(parts):
    return [parts[0], *parts[:0:-1]]


def contract(left, right, left_dim, right_dim):
    return lax.dot_general(
        left, right, (((left_dim,), (right_dim,)), ((), ())), preferred_element_type=F32
    )


def whole_specs(count):
    return [pl.BlockSpec(memory_space=pltpu.VMEM)] * count


def any_specs(count):
    return [pl.BlockSpec(memory_space=pl.ANY)] * count


def cost(name):
    return pl.CostEstimate(flops=int(COSTS.get(name, 0) * 1e9) + 1, bytes_accessed=1, transcendentals=0)


def params():
    return pltpu.CompilerParams(vmem_limit_bytes=VMEM_LIMIT)


def in_hbm(x):
    return pltpu.with_memory_space_constraint(x, pltpu.HBM)


def hbm_specs(count):
    return [pl.BlockSpec(memory_space=pltpu.HBM)] * count


def prepare_kernel(dims, *refs):
    tokens, top, half = dims
    sources, out_ref, held, sems = refs[:4], refs[4], refs[5:9], refs[9]
    copies = [pltpu.make_async_copy(a, b, sems.at[n]) for n, (a, b) in enumerate(zip(sources, held))]
    for copy in copies:
        copy.start()
    for copy in copies:
        copy.wait()
    ids_ref, gates_ref, hidden_ref, grad_ref = held
    gates = gates_ref[...]
    gate_hi = gates.astype(BF16)
    rest = gates - gate_hi.astype(F32)
    gate_mid = rest.astype(BF16)
    gate_lo = rest - gate_mid.astype(F32)
    values = [ids_ref[...].astype(F32), gate_hi.astype(F32), gate_mid.astype(F32), gate_lo]
    values = jnp.concatenate(values, axis=0).astype(BF16)
    entry = lax.broadcasted_iota(jnp.int32, (4 * top, META), 0)
    lane = lax.broadcasted_iota(jnp.int32, (4 * top, META), 1)
    meta = contract(values, (lane == entry).astype(F32).astype(BF16), 0, 0)
    meta = jnp.concatenate([meta, meta], axis=0)
    tiles = 2 * tokens // SUBLANES
    for n, source in enumerate((hidden_ref, grad_ref)):
        value = source[...].astype(F32)
        value = jnp.concatenate([value[:, :half], value[:, half:]], axis=0)
        for i in range(tiles):
            start = (n * tiles + i) * half
            out_ref[:, start : start + half] = value[i * SUBLANES : (i + 1) * SUBLANES].astype(BF16)
    packed = meta[:SUBLANES]
    for i in range(1, tiles):
        packed = packed + pltpu.roll(meta[i * SUBLANES : (i + 1) * SUBLANES], i * 4 * top, 1)
    out_ref[:, 2 * tiles * half :] = packed.astype(BF16)


def block_rows(blocks, start, width, tiles, shift=0):
    parts = []
    for block in blocks:
        for i in range(tiles):
            if shift:
                part = block[:, start : start + width].astype(F32)
                parts.append(pltpu.roll(part, width - i * shift, 1) if i else part)
            else:
                parts.append(block[:, start + i * width : start + (i + 1) * width].astype(F32))
    return jnp.concatenate(parts, axis=0)


def stacked(refs):
    return jnp.concatenate([r[...].astype(F32) for r in refs], axis=0).astype(BF16)


def count_above(index, unit, total):
    value = jnp.zeros_like(index)
    for m in range(unit, total, unit):
        value = value + (index >= m).astype(jnp.int32)
    return value


def routing(blocks, fold, dims):
    inner, tokens, top, cap, half = dims
    tiles = 2 * tokens // SUBLANES
    rows = len(blocks) * 2 * tokens
    shape = (rows, inner * fold)
    me = lax.axis_index("expert")
    my_inner = lax.rem(me, inner)
    my_base = me - my_inner
    lane = lax.broadcasted_iota(jnp.int32, shape, 1)
    step = count_above(lane, fold, shape[1])
    dest = jnp.zeros(shape, F32)
    for q in range(inner):
        expert = (my_base + traced_partner(my_inner, q, inner)).astype(F32)
        dest = jnp.where(step == q, expert, dest)
    meta = block_rows(blocks, 2 * tiles * half, META, tiles, 4 * top)
    named = jnp.zeros(shape, F32)
    gate = jnp.zeros(shape, F32)
    for k in range(top):
        hit = meta[:, k : k + 1] == dest
        value = sum(meta[:, n * top + k : n * top + k + 1] for n in range(1, 4))
        named = jnp.where(hit, 1.0, named)
        gate = jnp.where(hit, value, gate)
    left = lax.broadcasted_iota(jnp.int32, (rows, rows), 1)
    down = lax.broadcasted_iota(jnp.int32, (rows, rows), 0)
    same = count_above(left, tokens, rows) == count_above(down, tokens, rows)
    before = (same & (left < down)).astype(F32).astype(BF16)
    rank = jnp.dot(before, named.astype(BF16), preferred_element_type=F32)
    row = lax.broadcasted_iota(jnp.int32, (rows, 1), 0)
    block = count_above(row, 2 * tokens, rows)
    row_side = count_above(row, tokens, rows) - 2 * block
    position = block * cap + rank.astype(jnp.int32)
    return lane - step * fold, named, gate, position, row_side


def gate_parts(gate):
    gate_hi = gate.astype(BF16)
    rest = gate - gate_hi.astype(F32)
    gate_mid = rest.astype(BF16)
    return gate_hi, gate_mid, (rest - gate_mid.astype(F32)).astype(BF16)


def route_kernel(dims, count, reach, *refs):
    inner, tokens, top, cap, half = dims
    blocks = refs[:count]
    sends = refs[-inner:]
    fold = 4 * reach
    tiles = 2 * tokens // SUBLANES
    lane, named, gate, position, row_side = routing(blocks, fold, dims)
    segment = count_above(lane, reach, fold)
    grads = segment >= 2
    side = segment - 2 * grads.astype(jnp.int32)
    pick = jnp.where((position == lane - segment * reach) & (row_side == side), named, 0.0)
    pick_in = jnp.where(grads, 0.0, pick).astype(BF16)
    pick_grad = jnp.where(grads, pick, 0.0).astype(BF16)
    ones = jnp.ones((pick.shape[0], META), BF16)
    column = sum(contract(part, ones, 0, 0) for part in gate_parts(pick * gate))
    table = block_rows(blocks, 0, half, tiles).astype(BF16)
    out = contract(pick_in, table, 0, 0)
    table = block_rows(blocks, tiles * half, half, tiles).astype(BF16)
    out = out + contract(pick_grad, table, 0, 0) * column[:, :1]
    for q, send in enumerate(sends):
        send[...] = out[q * fold : (q + 1) * fold].astype(BF16)


def tables_kernel(dims, count, reach, *refs):
    pick_ref, gate_hi_ref, gate_mid_ref, _ = refs[-4:]
    lane, named, gate, position, row_side = routing(refs[:count], 2 * reach, dims)
    side = (lane >= reach).astype(jnp.int32)
    pick = jnp.where((position == lane - side * reach) & (row_side == side), named, 0.0)
    pick_ref[...] = pick.astype(BF16)
    gate_hi_ref[...], gate_mid_ref[...], _ = gate_parts(pick * gate)


def stack_kernel(dims, *refs):
    inner, reach, held = dims
    fold, half = refs[0].shape
    values = stacked(flipped(refs[:inner]))
    rows = inner * held
    row = lax.broadcasted_iota(jnp.int32, (rows, 1), 0)
    step = count_above(row, held, rows)
    item = row - step * held
    column = lax.broadcasted_iota(jnp.int32, (rows, inner * fold), 1)
    wanted = jnp.where(item < reach, step * fold + item, -4 * reach)
    chosen = [(column == wanted + n * reach).astype(F32) for n in range(4)]
    out = jnp.dot(jnp.concatenate(chosen, axis=0).astype(BF16), values, preferred_element_type=F32)
    for segment in range(4):
        array, side = divmod(segment, 2)
        part = out[segment * rows : (segment + 1) * rows].astype(BF16)
        refs[-1][array * rows : (array + 1) * rows, side * half : (side + 1) * half] = part


def turn_kernel(count, *refs):
    for source, target in zip(refs[:count], refs[count + 1 : -1]):
        target[...] = source[0].T


def core_spans(cores, width, move):
    core = lax.axis_index("etp")
    return [pl.ds(pl.multiple_of(move(core, d, cores) * width, width), width) for d in range(cores)]


def array_rows(stacks, sizes, array):
    return jnp.concatenate([s[array * n : (array + 1) * n, :] for s, n in zip(stacks, sizes)], axis=0)


def forward_own_kernel(dims, sizes, *refs):
    gate_w, up_w, gate_ref, up_ref = refs[len(sizes) :]
    rows = array_rows(refs, sizes, 0)
    span = core_spans(*dims, traced_origin)[0]
    gate_ref[...] = jnp.dot(rows, gate_w[0, span, :], preferred_element_type=F32)
    up_ref[...] = jnp.dot(rows, up_w[0, span, :], preferred_element_type=F32)


def forward_kernel(dims, sizes, *refs):
    cores, width = dims
    groups = len(sizes)
    gate_own, up_own, gate_w, up_w, down_w, *stacks = refs[: 5 + groups * (cores - 1)]
    gate_ref, up_ref, act_ref, *parts = refs[-(3 + cores) :]
    spans = core_spans(cores, width, traced_origin)
    gate_pre = gate_own[...]
    up_pre = up_own[...]
    for n, span in enumerate(spans[1:]):
        rows = array_rows(stacks[n * groups : (n + 1) * groups], sizes, 0)
        gate_pre = gate_pre + jnp.dot(rows, gate_w[0, span, :], preferred_element_type=F32)
        up_pre = up_pre + jnp.dot(rows, up_w[0, span, :], preferred_element_type=F32)
    act = (gate_pre * jax.nn.sigmoid(gate_pre) * up_pre).astype(BF16)
    gate_ref[...] = gate_pre
    up_ref[...] = up_pre
    act_ref[...] = act
    spans = core_spans(cores, width, traced_partner)
    for d in reversed(range(cores)):
        parts[d][...] = jnp.dot(act, down_w[0, :, spans[d]], preferred_element_type=F32).astype(BF16)


def backward_own_kernel(dims, sizes, *refs):
    down_t, out_ref = refs[len(sizes)], refs[-1]
    rows = array_rows(refs, sizes, 1)
    span = core_spans(*dims, traced_origin)[0]
    out_ref[...] = jnp.dot(rows, down_t[span, :], preferred_element_type=F32)


def backward_kernel(dims, sizes, *refs):
    cores, width = dims
    groups = len(sizes)
    act_own, gate_t, up_t, down_t, gate_ref, up_ref, *stacks = refs[: 6 + groups * (cores - 1)]
    gate_out, up_out, *parts = refs[-(cores + 1) :]
    spans = core_spans(cores, width, traced_origin)
    act_grad = act_own[...]
    for n, span in enumerate(spans[1:]):
        rows = array_rows(stacks[n * groups : (n + 1) * groups], sizes, 1)
        act_grad = act_grad + jnp.dot(rows, down_t[span, :], preferred_element_type=F32)
    gate_pre = gate_ref[...]
    sigmoid = jax.nn.sigmoid(gate_pre)
    gate_grad = (act_grad * up_ref[...] * sigmoid * (1.0 + gate_pre * (1.0 - sigmoid))).astype(BF16)
    up_grad = (act_grad * (gate_pre * sigmoid)).astype(BF16)
    gate_out[...] = gate_grad
    up_out[...] = up_grad
    spans = core_spans(cores, width, traced_partner)
    for part, span in zip(parts, spans[1:]):
        value = jnp.dot(gate_grad, gate_t[:, span], preferred_element_type=F32)
        value = value + jnp.dot(up_grad, up_t[:, span], preferred_element_type=F32)
        part[...] = value.astype(BF16)


def input_own_kernel(dims, *refs):
    gate_grad, up_grad, gate_t, up_t = refs[:4]
    span = core_spans(*dims, traced_partner)[0]
    value = jnp.dot(gate_grad[...], gate_t[:, span], preferred_element_type=F32)
    value = value + jnp.dot(up_grad[...], up_t[:, span], preferred_element_type=F32)
    refs[-1][...] = value.astype(BF16)


def down_kernel(dims, sizes, chunks, *refs):
    cores, width = dims
    groups = len(sizes)
    act_ref = refs[cores * groups]
    out_hbm, result, out_sems = refs[-3:]
    core = lax.axis_index("etp")
    act = act_ref[...].T
    chunk = width // chunks
    copies = []
    for d in range(cores):
        rows = array_rows(refs[d * groups : (d + 1) * groups], sizes, 1)
        base = traced_origin(core, d, cores) * width
        for n in range(chunks):
            slot = d * chunks + n
            value = jnp.dot(act, rows[:, n * chunk : (n + 1) * chunk], preferred_element_type=F32)
            result[slot] = value.astype(BF16)
            span = pl.ds(pl.multiple_of(base + n * chunk, chunk), chunk)
            copy = pltpu.make_async_copy(result.at[slot], out_hbm.at[0, :, span], out_sems.at[slot])
            copy.start()
            copies.append(copy)
    for copy in copies:
        copy.wait()


def split_kernel(dims, groups, *refs):
    cores, inner, reach = dims
    total = refs[0][...].astype(F32)
    for part in refs[1:cores]:
        total = total + part[...].astype(F32)
    total = total.astype(BF16)
    half = total.shape[1] // 2
    fold = 2 * reach
    row = lax.broadcasted_iota(jnp.int32, (inner * fold, 1), 0)
    step = count_above(row, fold, inner * fold)
    place = row - step * fold
    row_side = (place >= reach).astype(jnp.int32)
    slot = place - row_side * reach
    wanted = jnp.zeros_like(row)
    first = 0
    base = 0
    for size, held in groups:
        wanted = jnp.where(slot >= first, base + step * held + slot - first, wanted)
        first += size
        base += inner * held
    column = lax.broadcasted_iota(jnp.int32, (inner * fold, total.shape[0]), 1)
    out = None
    for side in range(2):
        chosen = ((column == wanted) & (row_side == side)).astype(F32).astype(BF16)
        term = jnp.dot(chosen, total[:, side * half : (side + 1) * half], preferred_element_type=F32)
        out = term if out is None else out + term
    for q in range(inner):
        refs[q - inner][...] = out[q * fold : (q + 1) * fold].astype(BF16)


def combine_kernel(dims, weighted, *refs):
    outer, inner, unit = dims
    tables = refs[inner : inner + weighted]
    outs = refs[-outer:]
    rows = stacked(flipped(refs[:inner]))
    total = None
    for table in tables:
        term = jnp.dot(table[...], rows, preferred_element_type=F32)
        total = term if total is None else total + term
    for b in range(outer):
        outs[b][...] = total[b * unit : (b + 1) * unit].astype(BF16)


def final_kernel(dims, *refs):
    outer, tokens, half = dims
    out_ref = refs[-2]
    total = refs[0][...].astype(F32)
    for part in refs[1:outer]:
        total = total + part[...].astype(F32)
    out_ref[:, :half] = total[:tokens].astype(BF16)
    out_ref[:, half:] = total[tokens:].astype(BF16)


def shape(rows, columns, kind=BF16):
    return jax.ShapeDtypeStruct((rows, columns), kind)


def on_device(hidden_in, expert_ids, gate_weights, out_grad, gate_weight, up_weight, down_weight):
    tokens, top = expert_ids.shape
    experts = lax.axis_size("expert")
    cores = lax.axis_size("etp")
    outer, inner = group_sizes(experts)
    cap = min(tokens, tokens * top // experts + 1)
    width = hidden_in.shape[1]
    half = width // 2
    hidden = gate_weight.shape[2]
    reach = outer * cap
    unit = 2 * tokens
    near = min(2, outer)
    groups = [g for g in (range(near), range(near, outer)) if len(g)]
    sizes = [(len(g) * cap, -(-len(g) * cap // 16) * 16) for g in groups]
    route_dims = (inner, tokens, top, cap, half)

    with jax.named_scope("prepare"):
        packed = pl.pallas_call(
            functools.partial(prepare_kernel, (tokens, top, half)),
            out_shape=shape(SUBLANES, 2 * unit // SUBLANES * half + META),
            in_specs=hbm_specs(4),
            out_specs=pl.BlockSpec(memory_space=pltpu.VMEM),
            scratch_shapes=[
                pltpu.VMEM((top, tokens), jnp.int32),
                pltpu.VMEM((top, tokens), F32),
                pltpu.VMEM((tokens, width), BF16),
                pltpu.VMEM((tokens, width), BF16),
                pltpu.SemaphoreType.DMA((4,)),
            ],
            compiler_params=params(),
            cost_estimate=cost("PREPARE"),
            name="prepare",
        )(in_hbm(expert_ids.T), in_hbm(gate_weights.T), in_hbm(hidden_in), in_hbm(out_grad))

    with jax.named_scope("gather_blocks"):
        blocks = [packed] + [send_outer(packed, s, outer, inner) for s in range(1, outer)]

    piece_shapes = [shape(2 * reach, half)] * inner
    table_shape = shape(outer * unit, inner * 2 * reach)
    token_shape = shape(8, META, F32)
    weights = [pltpu.with_memory_space_constraint(w, pltpu.VMEM) for w in (gate_weight, up_weight, down_weight)]
    dims = (cores, width)

    def route(g, after=()):
        members = [blocks[i] for i in groups[g]]
        size = sizes[g][0]
        return pl.pallas_call(
            functools.partial(route_kernel, route_dims, len(members), size),
            out_shape=[shape(4 * size, half)] * inner,
            in_specs=whole_specs(len(members) + len(after)),
            out_specs=whole_specs(inner),
            compiler_params=params(),
            cost_estimate=cost(f"ROUTE{g}"),
            name=f"route{g}",
        )(*members, *after)

    def spread(sends):
        return [sends[0]] + [send_inner(sends[q], q, outer, inner) for q in range(1, inner)]

    def gather_cores(g, pieces, after=()):
        size, held = sizes[g]
        stack = pl.pallas_call(
            functools.partial(stack_kernel, (inner, size, held)),
            out_shape=shape(2 * inner * held, width),
            in_specs=whole_specs(inner) + any_specs(len(after)),
            out_specs=pl.BlockSpec(memory_space=pltpu.VMEM),
            compiler_params=params(),
            cost_estimate=cost(f"STACK{g}"),
            name=f"stack{g}",
        )(*flipped(pieces), *after)
        return [stack] + [send_core(stack, d, cores) for d in range(1, cores)]

    with jax.named_scope("near_blocks"):
        sends = route(0)
        near_pieces = spread(sends)
    def turn(picked, after, name):
        return pl.pallas_call(
            functools.partial(turn_kernel, len(picked)),
            out_shape=[pltpu.VMEM((w.shape[2], w.shape[1]), BF16) for w in picked] + [token_shape],
            in_specs=whole_specs(len(picked)) + any_specs(1),
            out_specs=whole_specs(len(picked) + 1),
            compiler_params=params(),
            cost_estimate=cost(name.upper()),
            name=name,
        )(*picked, after)

    with jax.named_scope("turn_weights"):
        down_t, ready = turn(weights[2:], sends[0], "turn_down")
    with jax.named_scope("far_blocks"):
        far_pieces = [spread(route(g, (ready,))) for g in range(1, len(groups))]
    with jax.named_scope("turn_weights"):
        gate_t, up_t, turned = turn(weights[:2], (far_pieces or [near_pieces])[0][0], "turn_rest")
    with jax.named_scope("tables"):
        pick, gate_hi, gate_lo, listed = pl.pallas_call(
            functools.partial(tables_kernel, route_dims, outer, reach),
            out_shape=[table_shape] * 3 + [token_shape],
            in_specs=whole_specs(outer) + any_specs(1),
            out_specs=whole_specs(4),
            compiler_params=params(),
            cost_estimate=cost("TABLES"),
            name="tables",
        )(*blocks, sends[0])
    counts = [inner * held for _, held in sizes]
    rows = sum(counts)
    with jax.named_scope("gather_cores"):
        stacks = [gather_cores(0, near_pieces, [pieces[0] for pieces in far_pieces])]
        for g, pieces in enumerate(far_pieces, 1):
            stacks.append(gather_cores(g, pieces, (listed, turned)))
        own_stacks = [stack[0] for stack in stacks]
        other_stacks = [stack[d] for d in range(1, cores) for stack in stacks]

    with jax.named_scope("forward"):
        own = pl.pallas_call(
            functools.partial(forward_own_kernel, dims, counts),
            out_shape=[shape(rows, hidden, F32)] * 2,
            in_specs=whole_specs(len(counts) + 2),
            out_specs=whole_specs(2),
            compiler_params=params(),
            cost_estimate=cost("FORWARD_OWN"),
            name="forward_own",
        )(*own_stacks, *weights[:2])
        gate_pre, up_pre, act, *out_parts = pl.pallas_call(
            functools.partial(forward_kernel, dims, counts),
            out_shape=[shape(rows, hidden, F32)] * 2 + [shape(rows, hidden)] + [shape(rows, width)] * cores,
            in_specs=whole_specs(5 + len(other_stacks)),
            out_specs=whole_specs(3 + cores),
            compiler_params=params(),
            cost_estimate=cost("FORWARD"),
            name="forward",
        )(*own, *weights, *other_stacks)

    def give_back(parts, after=()):
        got = [parts[0]] + [send_core(parts[d], d, cores) for d in range(1, cores)]
        sends = pl.pallas_call(
            functools.partial(split_kernel, (cores, inner, reach), sizes),
            out_shape=piece_shapes,
            in_specs=whole_specs(cores) + any_specs(len(after)),
            out_specs=whole_specs(inner),
            compiler_params=params(),
            name="split",
        )(*got, *after)
        return [sends[0]] + [send_inner(sends[q], q, outer, inner, back=True) for q in range(1, inner)]

    def combine(pieces, tables):
        blocks = pl.pallas_call(
            functools.partial(combine_kernel, (outer, inner, unit), len(tables)),
            out_shape=[shape(unit, half)] * outer,
            in_specs=whole_specs(inner + len(tables)),
            out_specs=whole_specs(outer),
            compiler_params=params(),
            name="combine",
        )(*flipped(pieces), *tables)
        return [blocks[0]] + [send_outer(blocks[s], s, outer, inner, back=True) for s in range(1, outer)]

    def finish(blocks, after=()):
        return pl.pallas_call(
            functools.partial(final_kernel, (outer, tokens, half)),
            out_shape=[shape(tokens, width), shape(8, META, F32)],
            in_specs=whole_specs(outer + len(after)),
            out_specs=whole_specs(2),
            compiler_params=params(),
            name="final",
        )(*flipped(blocks), *after)

    with jax.named_scope("return_out"):
        out_back = give_back(out_parts)
        out_blocks = combine(out_back, (gate_hi, gate_lo))

    with jax.named_scope("backward"):
        act_own = pl.pallas_call(
            functools.partial(backward_own_kernel, dims, counts),
            out_shape=shape(rows, hidden, F32),
            in_specs=whole_specs(len(counts) + 1),
            out_specs=pl.BlockSpec(memory_space=pltpu.VMEM),
            compiler_params=params(),
            cost_estimate=cost("BACKWARD_OWN"),
            name="backward_own",
        )(*own_stacks, down_t)
        gate_grad, up_grad, *grad_parts = pl.pallas_call(
            functools.partial(backward_kernel, dims, counts),
            out_shape=[shape(rows, hidden)] * 2 + [shape(rows, width)] * (cores - 1),
            in_specs=whole_specs(6 + len(other_stacks)),
            out_specs=whole_specs(cores + 1),
            compiler_params=params(),
            cost_estimate=cost("BACKWARD"),
            name="backward",
        )(act_own, gate_t, up_t, down_t, gate_pre, up_pre, *other_stacks)
        own_part = pl.pallas_call(
            functools.partial(input_own_kernel, dims),
            out_shape=shape(rows, width),
            in_specs=whole_specs(4) + any_specs(1),
            out_specs=pl.BlockSpec(memory_space=pltpu.VMEM),
            compiler_params=params(),
            cost_estimate=cost("INPUT_OWN"),
            name="input_own",
        )(gate_grad, up_grad, gate_t, up_t, out_back[0])
        grad_parts = [own_part, *grad_parts]

    with jax.named_scope("return_grad"):
        back_blocks = combine(give_back(grad_parts, out_back[:1]), (pick,))

    with jax.named_scope("down_grad"):
        chunks = max(1, width // 512)
        down_grad = pl.pallas_call(
            functools.partial(down_kernel, dims, counts, chunks),
            out_shape=pltpu.HBM(down_weight.shape, BF16),
            in_specs=whole_specs(cores * len(groups) + 1) + any_specs(1),
            out_specs=pl.BlockSpec(memory_space=pltpu.HBM),
            scratch_shapes=[
                pltpu.VMEM((cores * chunks, hidden, width // chunks), BF16),
                pltpu.SemaphoreType.DMA((cores * chunks,)),
            ],
            compiler_params=params(),
            name="down_grad",
        )(*own_stacks, *other_stacks, act, back_blocks[0])

    mixed_out, done = finish(out_blocks)
    input_grad, done = finish(back_blocks, (done,))
    return (mixed_out, input_grad, down_grad)


def solution(mesh):
    return jax.shard_map(
        on_device,
        mesh=mesh,
        in_specs=(
            P("expert", "etp"),
            P("expert", None),
            P("expert", None),
            P("expert", "etp"),
            P("expert", None, "etp"),
            P("expert", None, "etp"),
            P("expert", "etp", None),
        ),
        out_specs=(P("expert", "etp"), P("expert", "etp"), P("expert", "etp", None)),
        check_vma=False,
    )
```

```python
import functools
import jax
import jax.numpy as jnp
from jax import lax
from jax.experimental import pallas as pl
from jax.experimental.pallas import tpu as pltpu
from jax.sharding import PartitionSpec as P

BF16 = jnp.bfloat16
F32 = jnp.float32
META = 128
COSTS = {"PREPARE": 20, "ROUTE0": 9, "ROUTE1": 9}
SUBLANES = 8
VMEM_LIMIT = 20 * 1024 * 1024


def group_sizes(experts):
    inner = 1
    while inner * inner * 4 <= experts and experts % (inner * 2) == 0:
        inner *= 2
    return experts // inner, inner


def partner(index, step, size):
    return index ^ step if size & (size - 1) == 0 else (index + step) % size


def origin(index, step, size):
    return index ^ step if size & (size - 1) == 0 else (index - step) % size


def traced_partner(index, step, size):
    return index ^ step if size & (size - 1) == 0 else lax.rem(index + step, size)


def traced_origin(index, step, size):
    return index ^ step if size & (size - 1) == 0 else lax.rem(index + size - step, size)


def send_outer(x, step, outer, inner, back=False):
    move = origin if back else partner
    pairs = [
        (a * inner + b, move(a, step, outer) * inner + b) for a in range(outer) for b in range(inner)
    ]
    return lax.ppermute(x, "expert", pairs)


def send_inner(x, step, outer, inner, back=False):
    move = origin if back else partner
    pairs = [
        (a * inner + b, a * inner + move(b, step, inner)) for a in range(outer) for b in range(inner)
    ]
    return lax.ppermute(x, "expert", pairs)


def send_core(x, step, cores, back=False):
    move = origin if back else partner
    return lax.ppermute(x, "etp", [(i, move(i, step, cores)) for i in range(cores)])


def flipped(parts):
    return [parts[0], *parts[:0:-1]]


def contract(left, right, left_dim, right_dim):
    return lax.dot_general(
        left, right, (((left_dim,), (right_dim,)), ((), ())), preferred_element_type=F32
    )


def whole_specs(count):
    return [pl.BlockSpec(memory_space=pltpu.VMEM)] * count


def any_specs(count):
    return [pl.BlockSpec(memory_space=pl.ANY)] * count


def cost(name):
    return pl.CostEstimate(flops=int(COSTS.get(name, 0) * 1e9) + 1, bytes_accessed=1, transcendentals=0)


def params():
    return pltpu.CompilerParams(vmem_limit_bytes=VMEM_LIMIT)


def in_hbm(x):
    return pltpu.with_memory_space_constraint(x, pltpu.HBM)


def hbm_specs(count):
    return [pl.BlockSpec(memory_space=pltpu.HBM)] * count


def prepare_kernel(dims, *refs):
    tokens, top, half = dims
    sources, out_ref, held, sems = refs[:4], refs[4], refs[5:9], refs[9]
    copies = [pltpu.make_async_copy(a, b, sems.at[n]) for n, (a, b) in enumerate(zip(sources, held))]
    for copy in copies:
        copy.start()
    for copy in copies:
        copy.wait()
    ids_ref, gates_ref, hidden_ref, grad_ref = held
    gates = gates_ref[...]
    gate_hi = gates.astype(BF16)
    rest = gates - gate_hi.astype(F32)
    gate_mid = rest.astype(BF16)
    gate_lo = rest - gate_mid.astype(F32)
    values = [ids_ref[...].astype(F32), gate_hi.astype(F32), gate_mid.astype(F32), gate_lo]
    values = jnp.concatenate(values, axis=0).astype(BF16)
    entry = lax.broadcasted_iota(jnp.int32, (4 * top, META), 0)
    lane = lax.broadcasted_iota(jnp.int32, (4 * top, META), 1)
    meta = contract(values, (lane == entry).astype(F32).astype(BF16), 0, 0)
    meta = jnp.concatenate([meta, meta], axis=0)
    tiles = 2 * tokens // SUBLANES
    for n, source in enumerate((hidden_ref, grad_ref)):
        value = source[...].astype(F32)
        value = jnp.concatenate([value[:, :half], value[:, half:]], axis=0)
        for i in range(tiles):
            start = (n * tiles + i) * half
            out_ref[:, start : start + half] = value[i * SUBLANES : (i + 1) * SUBLANES].astype(BF16)
    packed = meta[:SUBLANES]
    for i in range(1, tiles):
        packed = packed + pltpu.roll(meta[i * SUBLANES : (i + 1) * SUBLANES], i * 4 * top, 1)
    out_ref[:, 2 * tiles * half :] = packed.astype(BF16)


def block_rows(blocks, start, width, tiles, shift=0):
    parts = []
    for block in blocks:
        for i in range(tiles):
            if shift:
                part = block[:, start : start + width].astype(F32)
                parts.append(pltpu.roll(part, width - i * shift, 1) if i else part)
            else:
                parts.append(block[:, start + i * width : start + (i + 1) * width].astype(F32))
    return jnp.concatenate(parts, axis=0)


def stacked(refs):
    return jnp.concatenate([r[...].astype(F32) for r in refs], axis=0).astype(BF16)


def count_above(index, unit, total):
    value = jnp.zeros_like(index)
    for m in range(unit, total, unit):
        value = value + (index >= m).astype(jnp.int32)
    return value


def routing(blocks, fold, dims):
    inner, tokens, top, cap, half = dims
    tiles = 2 * tokens // SUBLANES
    rows = len(blocks) * 2 * tokens
    shape = (rows, inner * fold)
    me = lax.axis_index("expert")
    my_inner = lax.rem(me, inner)
    my_base = me - my_inner
    lane = lax.broadcasted_iota(jnp.int32, shape, 1)
    step = count_above(lane, fold, shape[1])
    dest = jnp.zeros(shape, F32)
    for q in range(inner):
        expert = (my_base + traced_partner(my_inner, q, inner)).astype(F32)
        dest = jnp.where(step == q, expert, dest)
    meta = block_rows(blocks, 2 * tiles * half, META, tiles, 4 * top)
    named = jnp.zeros(shape, F32)
    gate = jnp.zeros(shape, F32)
    for k in range(top):
        hit = meta[:, k : k + 1] == dest
        value = sum(meta[:, n * top + k : n * top + k + 1] for n in range(1, 4))
        named = jnp.where(hit, 1.0, named)
        gate = jnp.where(hit, value, gate)
    left = lax.broadcasted_iota(jnp.int32, (rows, rows), 1)
    down = lax.broadcasted_iota(jnp.int32, (rows, rows), 0)
    same = count_above(left, tokens, rows) == count_above(down, tokens, rows)
    before = (same & (left < down)).astype(F32).astype(BF16)
    rank = jnp.dot(before, named.astype(BF16), preferred_element_type=F32)
    row = lax.broadcasted_iota(jnp.int32, (rows, 1), 0)
    block = count_above(row, 2 * tokens, rows)
    row_side = count_above(row, tokens, rows) - 2 * block
    position = block * cap + rank.astype(jnp.int32)
    return lane - step * fold, named, gate, position, row_side


def gate_parts(gate):
    gate_hi = gate.astype(BF16)
    rest = gate - gate_hi.astype(F32)
    gate_mid = rest.astype(BF16)
    return gate_hi, gate_mid, (rest - gate_mid.astype(F32)).astype(BF16)


def route_kernel(dims, count, reach, *refs):
    inner, tokens, top, cap, half = dims
    blocks = refs[:count]
    sends = refs[-inner:]
    fold = 4 * reach
    tiles = 2 * tokens // SUBLANES
    lane, named, gate, position, row_side = routing(blocks, fold, dims)
    segment = count_above(lane, reach, fold)
    grads = segment >= 2
    side = segment - 2 * grads.astype(jnp.int32)
    pick = jnp.where((position == lane - segment * reach) & (row_side == side), named, 0.0)
    pick_in = jnp.where(grads, 0.0, pick).astype(BF16)
    pick_grad = jnp.where(grads, pick, 0.0).astype(BF16)
    ones = jnp.ones((pick.shape[0], META), BF16)
    column = sum(contract(part, ones, 0, 0) for part in gate_parts(pick * gate))
    table = block_rows(blocks, 0, half, tiles).astype(BF16)
    out = contract(pick_in, table, 0, 0)
    table = block_rows(blocks, tiles * half, half, tiles).astype(BF16)
    out = out + contract(pick_grad, table, 0, 0) * column[:, :1]
    for q, send in enumerate(sends):
        send[...] = out[q * fold : (q + 1) * fold].astype(BF16)


def tables_kernel(dims, count, reach, *refs):
    pick_ref, gate_hi_ref, gate_mid_ref, _ = refs[-4:]
    lane, named, gate, position, row_side = routing(refs[:count], 2 * reach, dims)
    side = (lane >= reach).astype(jnp.int32)
    pick = jnp.where((position == lane - side * reach) & (row_side == side), named, 0.0)
    pick_ref[...] = pick.astype(BF16)
    gate_hi_ref[...], gate_mid_ref[...], _ = gate_parts(pick * gate)


def shifted(rows, shift):
    return pltpu.roll(rows, shift % rows.shape[0], 0) if shift else rows


def padded(rows, before, after):
    parts = [rows]
    if before:
        parts.insert(0, jnp.zeros((before, rows.shape[1]), F32))
    if after:
        parts.append(jnp.zeros((after, rows.shape[1]), F32))
    return jnp.concatenate(parts, axis=0) if len(parts) > 1 else rows


def stack_kernel(dims, *refs):
    inner, reach, held = dims
    half = refs[0].shape[1]
    rows = inner * held
    live = lax.broadcasted_iota(jnp.int32, (held, half), 0) < reach
    for q, piece in enumerate(flipped(refs[:inner])):
        values = piece[...].astype(F32)
        for segment in range(4):
            array, side = divmod(segment, 2)
            start = segment * reach // SUBLANES * SUBLANES
            shift = segment * reach - start
            frame = -(-(shift + reach) // SUBLANES) * SUBLANES
            part = shifted(values[start : start + frame], -shift)
            part = part[:held] if frame > held else padded(part, 0, held - frame)
            first = array * rows + q * held
            target = refs[-1].at[first : first + held, side * half : (side + 1) * half]
            target[...] = jnp.where(live, part, 0.0).astype(BF16)


def turn_kernel(count, *refs):
    for source, target in zip(refs[:count], refs[count + 1 : -1]):
        target[...] = source[0].T


def core_spans(cores, width, move):
    core = lax.axis_index("etp")
    return [pl.ds(pl.multiple_of(move(core, d, cores) * width, width), width) for d in range(cores)]


def array_rows(stacks, sizes, array):
    return jnp.concatenate([s[array * n : (array + 1) * n, :] for s, n in zip(stacks, sizes)], axis=0)


def forward_own_kernel(dims, sizes, *refs):
    gate_w, up_w, gate_ref, up_ref = refs[len(sizes) :]
    rows = array_rows(refs, sizes, 0)
    span = core_spans(*dims, traced_origin)[0]
    gate_ref[...] = jnp.dot(rows, gate_w[0, span, :], preferred_element_type=F32)
    up_ref[...] = jnp.dot(rows, up_w[0, span, :], preferred_element_type=F32)


def forward_kernel(dims, sizes, *refs):
    cores, width = dims
    groups = len(sizes)
    gate_own, up_own, gate_w, up_w, down_w, *stacks = refs[: 5 + groups * (cores - 1)]
    gate_ref, up_ref, act_ref, *parts = refs[-(3 + cores) :]
    spans = core_spans(cores, width, traced_origin)
    gate_pre = gate_own[...]
    up_pre = up_own[...]
    for n, span in enumerate(spans[1:]):
        rows = array_rows(stacks[n * groups : (n + 1) * groups], sizes, 0)
        gate_pre = gate_pre + jnp.dot(rows, gate_w[0, span, :], preferred_element_type=F32)
        up_pre = up_pre + jnp.dot(rows, up_w[0, span, :], preferred_element_type=F32)
    act = (gate_pre * jax.nn.sigmoid(gate_pre) * up_pre).astype(BF16)
    gate_ref[...] = gate_pre
    up_ref[...] = up_pre
    act_ref[...] = act
    spans = core_spans(cores, width, traced_partner)
    for d in reversed(range(cores)):
        parts[d][...] = jnp.dot(act, down_w[0, :, spans[d]], preferred_element_type=F32).astype(BF16)


def backward_own_kernel(dims, sizes, *refs):
    down_t, out_ref = refs[len(sizes)], refs[-1]
    rows = array_rows(refs, sizes, 1)
    span = core_spans(*dims, traced_origin)[0]
    out_ref[...] = jnp.dot(rows, down_t[span, :], preferred_element_type=F32)


def backward_kernel(dims, sizes, *refs):
    cores, width = dims
    groups = len(sizes)
    act_own, gate_t, up_t, down_t, gate_ref, up_ref, *stacks = refs[: 6 + groups * (cores - 1)]
    gate_out, up_out, *parts = refs[-(cores + 1) :]
    spans = core_spans(cores, width, traced_origin)
    act_grad = act_own[...]
    for n, span in enumerate(spans[1:]):
        rows = array_rows(stacks[n * groups : (n + 1) * groups], sizes, 1)
        act_grad = act_grad + jnp.dot(rows, down_t[span, :], preferred_element_type=F32)
    gate_pre = gate_ref[...]
    sigmoid = jax.nn.sigmoid(gate_pre)
    gate_grad = (act_grad * up_ref[...] * sigmoid * (1.0 + gate_pre * (1.0 - sigmoid))).astype(BF16)
    up_grad = (act_grad * (gate_pre * sigmoid)).astype(BF16)
    gate_out[...] = gate_grad
    up_out[...] = up_grad
    spans = core_spans(cores, width, traced_partner)
    for part, span in zip(parts, spans[1:]):
        value = jnp.dot(gate_grad, gate_t[:, span], preferred_element_type=F32)
        value = value + jnp.dot(up_grad, up_t[:, span], preferred_element_type=F32)
        part[...] = value.astype(BF16)


def input_own_kernel(dims, *refs):
    gate_grad, up_grad, gate_t, up_t = refs[:4]
    span = core_spans(*dims, traced_partner)[0]
    value = jnp.dot(gate_grad[...], gate_t[:, span], preferred_element_type=F32)
    value = value + jnp.dot(up_grad[...], up_t[:, span], preferred_element_type=F32)
    refs[-1][...] = value.astype(BF16)


def down_kernel(dims, sizes, chunks, *refs):
    cores, width = dims
    groups = len(sizes)
    act_ref = refs[cores * groups]
    out_hbm, result, out_sems = refs[-3:]
    core = lax.axis_index("etp")
    act = act_ref[...].T
    chunk = width // chunks
    copies = []
    for d in range(cores):
        rows = array_rows(refs[d * groups : (d + 1) * groups], sizes, 1)
        base = traced_origin(core, d, cores) * width
        for n in range(chunks):
            slot = d * chunks + n
            value = jnp.dot(act, rows[:, n * chunk : (n + 1) * chunk], preferred_element_type=F32)
            result[slot] = value.astype(BF16)
            span = pl.ds(pl.multiple_of(base + n * chunk, chunk), chunk)
            copy = pltpu.make_async_copy(result.at[slot], out_hbm.at[0, :, span], out_sems.at[slot])
            copy.start()
            copies.append(copy)
    for copy in copies:
        copy.wait()


def split_kernel(dims, groups, *refs):
    cores, inner, reach = dims
    total = refs[0][...].astype(F32)
    for part in refs[1:cores]:
        total = total + part[...].astype(F32)
    half = total.shape[1] // 2
    fold = 2 * reach
    for q in range(inner):
        out = None
        first = 0
        base = 0
        for size, held in groups:
            rows = total[base + q * held : base + (q + 1) * held]
            for side in range(2):
                place = side * reach + first
                start = place // SUBLANES * SUBLANES
                frame = -(-(place - start + size) // SUBLANES) * SUBLANES
                part = rows[:, side * half : (side + 1) * half]
                part = part[:frame] if frame < held else padded(part, 0, frame - held)
                part = shifted(part, place - start)
                part = padded(part, start, fold - start - frame)
                out = part if out is None else out + part
            first += size
            base += inner * held
        refs[q - inner][...] = out.astype(BF16)


def combine_kernel(dims, weighted, *refs):
    outer, inner, unit = dims
    tables = refs[inner : inner + weighted]
    outs = refs[-outer:]
    rows = stacked(refs[:inner])
    total = None
    for table in tables:
        term = jnp.dot(table[...], rows, preferred_element_type=F32)
        total = term if total is None else total + term
    for b in range(outer):
        outs[b][...] = total[b * unit : (b + 1) * unit].astype(BF16)


def final_kernel(dims, *refs):
    outer, tokens, half = dims
    out_ref = refs[-2]
    total = refs[0][...].astype(F32)
    for part in refs[1:outer]:
        total = total + part[...].astype(F32)
    out_ref[:, :half] = total[:tokens].astype(BF16)
    out_ref[:, half:] = total[tokens:].astype(BF16)


def shape(rows, columns, kind=BF16):
    return jax.ShapeDtypeStruct((rows, columns), kind)


def on_device(hidden_in, expert_ids, gate_weights, out_grad, gate_weight, up_weight, down_weight):
    tokens, top = expert_ids.shape
    experts = lax.axis_size("expert")
    cores = lax.axis_size("etp")
    outer, inner = group_sizes(experts)
    cap = min(tokens, tokens * top // experts + 1)
    width = hidden_in.shape[1]
    half = width // 2
    hidden = gate_weight.shape[2]
    reach = outer * cap
    unit = 2 * tokens
    near = min(2, outer)
    groups = [g for g in (range(near), range(near, outer)) if len(g)]
    sizes = [(len(g) * cap, -(-len(g) * cap // 16) * 16) for g in groups]
    route_dims = (inner, tokens, top, cap, half)

    with jax.named_scope("prepare"):
        packed = pl.pallas_call(
            functools.partial(prepare_kernel, (tokens, top, half)),
            out_shape=shape(SUBLANES, 2 * unit // SUBLANES * half + META),
            in_specs=hbm_specs(4),
            out_specs=pl.BlockSpec(memory_space=pltpu.VMEM),
            scratch_shapes=[
                pltpu.VMEM((top, tokens), jnp.int32),
                pltpu.VMEM((top, tokens), F32),
                pltpu.VMEM((tokens, width), BF16),
                pltpu.VMEM((tokens, width), BF16),
                pltpu.SemaphoreType.DMA((4,)),
            ],
            compiler_params=params(),
            cost_estimate=cost("PREPARE"),
            name="prepare",
        )(in_hbm(expert_ids.T), in_hbm(gate_weights.T), in_hbm(hidden_in), in_hbm(out_grad))

    with jax.named_scope("gather_blocks"):
        blocks = [packed] + [send_outer(packed, s, outer, inner) for s in range(1, outer)]

    piece_shapes = [shape(2 * reach, half)] * inner
    table_shape = shape(outer * unit, inner * 2 * reach)
    token_shape = shape(8, META, F32)
    weights = [pltpu.with_memory_space_constraint(w, pltpu.VMEM) for w in (gate_weight, up_weight, down_weight)]
    dims = (cores, width)

    def route(g, after=()):
        members = [blocks[i] for i in groups[g]]
        size = sizes[g][0]
        return pl.pallas_call(
            functools.partial(route_kernel, route_dims, len(members), size),
            out_shape=[shape(4 * size, half)] * inner,
            in_specs=whole_specs(len(members) + len(after)),
            out_specs=whole_specs(inner),
            compiler_params=params(),
            cost_estimate=cost(f"ROUTE{g}"),
            name=f"route{g}",
        )(*members, *after)

    def spread(sends):
        return [sends[0]] + [send_inner(sends[q], q, outer, inner) for q in range(1, inner)]

    def gather_cores(g, pieces, after=()):
        size, held = sizes[g]
        stack = pl.pallas_call(
            functools.partial(stack_kernel, (inner, size, held)),
            out_shape=shape(2 * inner * held, width),
            in_specs=whole_specs(inner) + any_specs(len(after)),
            out_specs=pl.BlockSpec(memory_space=pltpu.VMEM),
            compiler_params=params(),
            cost_estimate=cost(f"STACK{g}"),
            name=f"stack{g}",
        )(*flipped(pieces), *after)
        return [stack] + [send_core(stack, d, cores) for d in range(1, cores)]

    with jax.named_scope("near_blocks"):
        sends = route(0)
        near_pieces = spread(sends)
    def turn(picked, after, name):
        return pl.pallas_call(
            functools.partial(turn_kernel, len(picked)),
            out_shape=[pltpu.VMEM((w.shape[2], w.shape[1]), BF16) for w in picked] + [token_shape],
            in_specs=whole_specs(len(picked)) + any_specs(1),
            out_specs=whole_specs(len(picked) + 1),
            compiler_params=params(),
            cost_estimate=cost(name.upper()),
            name=name,
        )(*picked, after)

    with jax.named_scope("turn_weights"):
        down_t, ready = turn(weights[2:], sends[0], "turn_down")
    with jax.named_scope("far_blocks"):
        far_pieces = [spread(route(g, (ready,))) for g in range(1, len(groups))]
    with jax.named_scope("turn_weights"):
        gate_t, up_t, turned = turn(weights[:2], (far_pieces or [near_pieces])[0][0], "turn_rest")
    with jax.named_scope("tables"):
        pick, gate_hi, gate_lo, listed = pl.pallas_call(
            functools.partial(tables_kernel, route_dims, outer, reach),
            out_shape=[table_shape] * 3 + [token_shape],
            in_specs=whole_specs(outer) + any_specs(1),
            out_specs=whole_specs(4),
            compiler_params=params(),
            cost_estimate=cost("TABLES"),
            name="tables",
        )(*blocks, sends[0])
    counts = [inner * held for _, held in sizes]
    rows = sum(counts)
    with jax.named_scope("gather_cores"):
        stacks = [gather_cores(0, near_pieces, [pieces[0] for pieces in far_pieces])]
        for g, pieces in enumerate(far_pieces, 1):
            stacks.append(gather_cores(g, pieces, (listed, turned)))
        own_stacks = [stack[0] for stack in stacks]
        other_stacks = [stack[d] for d in range(1, cores) for stack in stacks]

    with jax.named_scope("forward"):
        own = pl.pallas_call(
            functools.partial(forward_own_kernel, dims, counts),
            out_shape=[shape(rows, hidden, F32)] * 2,
            in_specs=whole_specs(len(counts) + 2),
            out_specs=whole_specs(2),
            compiler_params=params(),
            cost_estimate=cost("FORWARD_OWN"),
            name="forward_own",
        )(*own_stacks, *weights[:2])
        act_own = pl.pallas_call(
            functools.partial(backward_own_kernel, dims, counts),
            out_shape=shape(rows, hidden, F32),
            in_specs=whole_specs(len(counts) + 1),
            out_specs=pl.BlockSpec(memory_space=pltpu.VMEM),
            compiler_params=params(),
            cost_estimate=cost("BACKWARD_OWN"),
            name="backward_own",
        )(*own_stacks, down_t)
        gate_pre, up_pre, act, *out_parts = pl.pallas_call(
            functools.partial(forward_kernel, dims, counts),
            out_shape=[shape(rows, hidden, F32)] * 2 + [shape(rows, hidden)] + [shape(rows, width)] * cores,
            in_specs=whole_specs(5 + len(other_stacks)) + any_specs(1),
            out_specs=whole_specs(3 + cores),
            compiler_params=params(),
            cost_estimate=cost("FORWARD"),
            name="forward",
        )(*own, *weights, *other_stacks, act_own)

    def give_back(parts, after=()):
        got = [parts[0]] + [send_core(parts[d], d, cores) for d in range(1, cores)]
        sends = pl.pallas_call(
            functools.partial(split_kernel, (cores, inner, reach), sizes),
            out_shape=piece_shapes,
            in_specs=whole_specs(cores) + any_specs(len(after)),
            out_specs=whole_specs(inner),
            compiler_params=params(),
            name="split",
        )(*got, *after)
        return [sends[0]] + [send_inner(sends[q], q, outer, inner, back=True) for q in range(1, inner)]

    def combine(pieces, tables):
        blocks = pl.pallas_call(
            functools.partial(combine_kernel, (outer, inner, unit), len(tables)),
            out_shape=[shape(unit, half)] * outer,
            in_specs=whole_specs(inner + len(tables)),
            out_specs=whole_specs(outer),
            compiler_params=params(),
            name="combine",
        )(*pieces, *tables)
        return [blocks[0]] + [send_outer(blocks[s], s, outer, inner, back=True) for s in range(1, outer)]

    def finish(blocks, after=()):
        return pl.pallas_call(
            functools.partial(final_kernel, (outer, tokens, half)),
            out_shape=[shape(tokens, width), shape(8, META, F32)],
            in_specs=whole_specs(outer + len(after)),
            out_specs=whole_specs(2),
            compiler_params=params(),
            name="final",
        )(*flipped(blocks), *after)

    with jax.named_scope("return_out"):
        out_back = give_back(out_parts)
        out_blocks = combine(out_back, (gate_hi, gate_lo))

    with jax.named_scope("backward"):
        gate_grad, up_grad, *grad_parts = pl.pallas_call(
            functools.partial(backward_kernel, dims, counts),
            out_shape=[shape(rows, hidden)] * 2 + [shape(rows, width)] * (cores - 1),
            in_specs=whole_specs(6 + len(other_stacks)),
            out_specs=whole_specs(cores + 1),
            compiler_params=params(),
            cost_estimate=cost("BACKWARD"),
            name="backward",
        )(act_own, gate_t, up_t, down_t, gate_pre, up_pre, *other_stacks)
        own_part = pl.pallas_call(
            functools.partial(input_own_kernel, dims),
            out_shape=shape(rows, width),
            in_specs=whole_specs(4) + any_specs(1),
            out_specs=pl.BlockSpec(memory_space=pltpu.VMEM),
            compiler_params=params(),
            cost_estimate=cost("INPUT_OWN"),
            name="input_own",
        )(gate_grad, up_grad, gate_t, up_t, out_back[0])
        grad_parts = [own_part, *grad_parts]

    with jax.named_scope("return_grad"):
        back_blocks = combine(give_back(grad_parts, out_back[:1]), (pick,))

    with jax.named_scope("down_grad"):
        chunks = max(1, width // 512)
        down_grad = pl.pallas_call(
            functools.partial(down_kernel, dims, counts, chunks),
            out_shape=pltpu.HBM(down_weight.shape, BF16),
            in_specs=whole_specs(cores * len(groups) + 1) + any_specs(1),
            out_specs=pl.BlockSpec(memory_space=pltpu.HBM),
            scratch_shapes=[
                pltpu.VMEM((cores * chunks, hidden, width // chunks), BF16),
                pltpu.SemaphoreType.DMA((cores * chunks,)),
            ],
            compiler_params=params(),
            name="down_grad",
        )(*own_stacks, *other_stacks, act, back_blocks[0])

    mixed_out, done = finish(out_blocks)
    input_grad, done = finish(back_blocks, (done,))
    return (mixed_out, input_grad, down_grad)


def solution(mesh):
    return jax.shard_map(
        on_device,
        mesh=mesh,
        in_specs=(
            P("expert", "etp"),
            P("expert", None),
            P("expert", None),
            P("expert", "etp"),
            P("expert", None, "etp"),
            P("expert", None, "etp"),
            P("expert", "etp", None),
        ),
        out_specs=(P("expert", "etp"), P("expert", "etp"), P("expert", "etp", None)),
        check_vma=False,
    )
```

```python
import functools
import jax
import jax.numpy as jnp
from jax import lax
from jax.experimental import pallas as pl
from jax.experimental.pallas import tpu as pltpu
from jax.sharding import PartitionSpec as P

BF16 = jnp.bfloat16
F32 = jnp.float32
META = 128
COSTS = {"PREPARE": 20, "ROUTE0": 9, "ROUTE1": 9}
SUBLANES = 8
VMEM_LIMIT = 20 * 1024 * 1024


def group_sizes(experts):
    inner = 1
    while inner * inner * 4 <= experts and experts % (inner * 2) == 0:
        inner *= 2
    return experts // inner, inner


def partner(index, step, size):
    return index ^ step if size & (size - 1) == 0 else (index + step) % size


def origin(index, step, size):
    return index ^ step if size & (size - 1) == 0 else (index - step) % size


def traced_partner(index, step, size):
    return index ^ step if size & (size - 1) == 0 else lax.rem(index + step, size)


def traced_origin(index, step, size):
    return index ^ step if size & (size - 1) == 0 else lax.rem(index + size - step, size)


def send_outer(x, step, outer, inner, back=False):
    move = origin if back else partner
    pairs = [
        (a * inner + b, move(a, step, outer) * inner + b) for a in range(outer) for b in range(inner)
    ]
    return lax.ppermute(x, "expert", pairs)


def send_inner(x, step, outer, inner, back=False):
    move = origin if back else partner
    pairs = [
        (a * inner + b, a * inner + move(b, step, inner)) for a in range(outer) for b in range(inner)
    ]
    return lax.ppermute(x, "expert", pairs)


def send_core(x, step, cores, back=False):
    move = origin if back else partner
    return lax.ppermute(x, "etp", [(i, move(i, step, cores)) for i in range(cores)])


def flipped(parts):
    return [parts[0], *parts[:0:-1]]


def contract(left, right, left_dim, right_dim):
    return lax.dot_general(
        left, right, (((left_dim,), (right_dim,)), ((), ())), preferred_element_type=F32
    )


def whole_specs(count):
    return [pl.BlockSpec(memory_space=pltpu.VMEM)] * count


def any_specs(count):
    return [pl.BlockSpec(memory_space=pl.ANY)] * count


def cost(name):
    return pl.CostEstimate(flops=int(COSTS.get(name, 0) * 1e9) + 1, bytes_accessed=1, transcendentals=0)


def params():
    return pltpu.CompilerParams(vmem_limit_bytes=VMEM_LIMIT)


def in_hbm(x):
    return pltpu.with_memory_space_constraint(x, pltpu.HBM)


def hbm_specs(count):
    return [pl.BlockSpec(memory_space=pltpu.HBM)] * count


def prepare_kernel(dims, *refs):
    tokens, top, half = dims
    sources, out_ref, held, sems = refs[:4], refs[4], refs[5:9], refs[9]
    copies = [pltpu.make_async_copy(a, b, sems.at[n]) for n, (a, b) in enumerate(zip(sources, held))]
    for copy in copies:
        copy.start()
    for copy in copies:
        copy.wait()
    ids_ref, gates_ref, hidden_ref, grad_ref = held
    gates = gates_ref[...]
    gate_hi = gates.astype(BF16)
    rest = gates - gate_hi.astype(F32)
    gate_mid = rest.astype(BF16)
    gate_lo = rest - gate_mid.astype(F32)
    values = [ids_ref[...].astype(F32), gate_hi.astype(F32), gate_mid.astype(F32), gate_lo]
    values = jnp.concatenate(values, axis=0).astype(BF16)
    entry = lax.broadcasted_iota(jnp.int32, (4 * top, META), 0)
    lane = lax.broadcasted_iota(jnp.int32, (4 * top, META), 1)
    meta = contract(values, (lane == entry).astype(F32).astype(BF16), 0, 0)
    meta = jnp.concatenate([meta, meta], axis=0)
    tiles = 2 * tokens // SUBLANES
    for n, source in enumerate((hidden_ref, grad_ref)):
        value = source[...].astype(F32)
        value = jnp.concatenate([value[:, :half], value[:, half:]], axis=0)
        for i in range(tiles):
            start = (n * tiles + i) * half
            out_ref[:, start : start + half] = value[i * SUBLANES : (i + 1) * SUBLANES].astype(BF16)
    packed = meta[:SUBLANES]
    for i in range(1, tiles):
        packed = packed + pltpu.roll(meta[i * SUBLANES : (i + 1) * SUBLANES], i * 4 * top, 1)
    out_ref[:, 2 * tiles * half :] = packed.astype(BF16)


def block_rows(blocks, start, width, tiles, shift=0):
    parts = []
    for block in blocks:
        for i in range(tiles):
            if shift:
                part = block[:, start : start + width].astype(F32)
                parts.append(pltpu.roll(part, width - i * shift, 1) if i else part)
            else:
                parts.append(block[:, start + i * width : start + (i + 1) * width].astype(F32))
    return jnp.concatenate(parts, axis=0)


def stacked(refs):
    return jnp.concatenate([r[...].astype(F32) for r in refs], axis=0).astype(BF16)


def count_above(index, unit, total):
    value = jnp.zeros_like(index)
    for m in range(unit, total, unit):
        value = value + (index >= m).astype(jnp.int32)
    return value


def routing(blocks, fold, dims):
    inner, tokens, top, cap, half = dims
    tiles = 2 * tokens // SUBLANES
    rows = len(blocks) * 2 * tokens
    shape = (rows, inner * fold)
    me = lax.axis_index("expert")
    my_inner = lax.rem(me, inner)
    my_base = me - my_inner
    lane = lax.broadcasted_iota(jnp.int32, (1, shape[1]), 1)
    step = count_above(lane, fold, shape[1])
    dest = jnp.zeros(lane.shape, F32)
    for q in range(inner):
        expert = (my_base + traced_partner(my_inner, q, inner)).astype(F32)
        dest = jnp.where(step == q, expert, dest)
    meta = block_rows(blocks, 2 * tiles * half, META, tiles, 4 * top)
    weights = meta + pltpu.roll(meta, META - top, 1) + pltpu.roll(meta, META - 2 * top, 1)
    named = jnp.zeros(shape, F32)
    gate = jnp.zeros(shape, F32)
    for k in range(top):
        hit = meta[:, k : k + 1] == dest
        value = weights[:, top + k : top + k + 1]
        named = jnp.where(hit, 1.0, named)
        gate = jnp.where(hit, value, gate)
    left = lax.broadcasted_iota(jnp.int32, (rows, rows), 1)
    down = lax.broadcasted_iota(jnp.int32, (rows, rows), 0)
    same = count_above(left, tokens, rows) == count_above(down, tokens, rows)
    before = (same & (left < down)).astype(F32).astype(BF16)
    rank = jnp.dot(before, named.astype(BF16), preferred_element_type=F32)
    row = lax.broadcasted_iota(jnp.int32, (rows, 1), 0)
    block = count_above(row, 2 * tokens, rows)
    row_side = count_above(row, tokens, rows) - 2 * block
    position = block * cap + rank.astype(jnp.int32)
    return lane - step * fold, named, gate, position, row_side


def gate_parts(gate):
    gate_hi = gate.astype(BF16)
    rest = gate - gate_hi.astype(F32)
    gate_mid = rest.astype(BF16)
    return gate_hi, gate_mid, (rest - gate_mid.astype(F32)).astype(BF16)


def route_kernel(dims, count, reach, *refs):
    inner, tokens, top, cap, half = dims
    blocks = refs[:count]
    sends = refs[-inner:]
    fold = 4 * reach
    tiles = 2 * tokens // SUBLANES
    lane, named, gate, position, row_side = routing(blocks, fold, dims)
    segment = count_above(lane, reach, fold)
    grads = segment >= 2
    side = segment - 2 * grads.astype(jnp.int32)
    pick = jnp.where((position == lane - segment * reach) & (row_side == side), named, 0.0)
    ones = jnp.ones((pick.shape[0], META), BF16)
    column = sum(contract(part, ones, 0, 0) for part in gate_parts(pick * jnp.where(grads, gate, 1.0)))
    chosen = jnp.concatenate([jnp.where(grads, 0.0, pick), jnp.where(grads, pick, 0.0)], axis=0).astype(BF16)
    table = [block_rows(blocks, n * tiles * half, half, tiles) for n in range(2)]
    out = contract(chosen, jnp.concatenate(table, axis=0).astype(BF16), 0, 0) * column[:, :1]
    for q, send in enumerate(sends):
        send[...] = out[q * fold : (q + 1) * fold].astype(BF16)


def tables_kernel(dims, count, reach, *refs):
    pick_ref, gate_hi_ref, gate_mid_ref, _ = refs[-4:]
    lane, named, gate, position, row_side = routing(refs[:count], 2 * reach, dims)
    side = (lane >= reach).astype(jnp.int32)
    pick = jnp.where((position == lane - side * reach) & (row_side == side), named, 0.0)
    pick_ref[...] = pick.astype(BF16)
    gate_hi_ref[...], gate_mid_ref[...], _ = gate_parts(pick * gate)


def shifted(rows, shift):
    return pltpu.roll(rows, shift % rows.shape[0], 0) if shift else rows


def padded(rows, before, after):
    parts = [rows]
    if before:
        parts.insert(0, jnp.zeros((before, rows.shape[1]), F32))
    if after:
        parts.append(jnp.zeros((after, rows.shape[1]), F32))
    return jnp.concatenate(parts, axis=0) if len(parts) > 1 else rows


def stack_kernel(dims, *refs):
    inner, reach, held = dims
    half = refs[0].shape[1]
    rows = inner * held
    live = lax.broadcasted_iota(jnp.int32, (held, half), 0) < reach
    for q, piece in enumerate(flipped(refs[:inner])):
        values = piece[...].astype(F32)
        for segment in range(4):
            array, side = divmod(segment, 2)
            start = segment * reach // SUBLANES * SUBLANES
            shift = segment * reach - start
            frame = -(-(shift + reach) // SUBLANES) * SUBLANES
            part = shifted(values[start : start + frame], -shift)
            part = part[:held] if frame > held else padded(part, 0, held - frame)
            first = array * rows + q * held
            target = refs[-1].at[first : first + held, side * half : (side + 1) * half]
            target[...] = jnp.where(live, part, 0.0).astype(BF16)


def turn_kernel(count, *refs):
    for source, target in zip(refs[:count], refs[count + 1 : -1]):
        target[...] = source[0].T


def core_spans(cores, width, move):
    core = lax.axis_index("etp")
    return [pl.ds(pl.multiple_of(move(core, d, cores) * width, width), width) for d in range(cores)]


def array_rows(stacks, sizes, array):
    return jnp.concatenate([s[array * n : (array + 1) * n, :] for s, n in zip(stacks, sizes)], axis=0)


def forward_own_kernel(dims, sizes, *refs):
    gate_w, up_w, gate_ref, up_ref = refs[len(sizes) :]
    rows = array_rows(refs, sizes, 0)
    span = core_spans(*dims, traced_origin)[0]
    gate_ref[...] = jnp.dot(rows, gate_w[0, span, :], preferred_element_type=F32)
    up_ref[...] = jnp.dot(rows, up_w[0, span, :], preferred_element_type=F32)


def forward_kernel(dims, sizes, *refs):
    cores, width = dims
    groups = len(sizes)
    gate_own, up_own, gate_w, up_w, down_w, *stacks = refs[: 5 + groups * (cores - 1)]
    gate_ref, up_ref, act_ref, *parts = refs[-(3 + cores) :]
    spans = core_spans(cores, width, traced_origin)
    gate_pre = gate_own[...]
    up_pre = up_own[...]
    for n, span in enumerate(spans[1:]):
        rows = array_rows(stacks[n * groups : (n + 1) * groups], sizes, 0)
        gate_pre = gate_pre + jnp.dot(rows, gate_w[0, span, :], preferred_element_type=F32)
        up_pre = up_pre + jnp.dot(rows, up_w[0, span, :], preferred_element_type=F32)
    act = (gate_pre * jax.nn.sigmoid(gate_pre) * up_pre).astype(BF16)
    gate_ref[...] = gate_pre
    up_ref[...] = up_pre
    act_ref[...] = act
    spans = core_spans(cores, width, traced_partner)
    for d in reversed(range(cores)):
        parts[d][...] = jnp.dot(act, down_w[0, :, spans[d]], preferred_element_type=F32).astype(BF16)


def backward_own_kernel(dims, sizes, *refs):
    down_t, out_ref = refs[len(sizes)], refs[-1]
    rows = array_rows(refs, sizes, 1)
    span = core_spans(*dims, traced_origin)[0]
    out_ref[...] = jnp.dot(rows, down_t[span, :], preferred_element_type=F32)


def backward_kernel(dims, sizes, *refs):
    cores, width = dims
    groups = len(sizes)
    act_own, gate_t, up_t, down_t, gate_ref, up_ref, *stacks = refs[: 6 + groups * (cores - 1)]
    gate_out, up_out, *parts = refs[-(cores + 1) :]
    spans = core_spans(cores, width, traced_origin)
    act_grad = act_own[...]
    for n, span in enumerate(spans[1:]):
        rows = array_rows(stacks[n * groups : (n + 1) * groups], sizes, 1)
        act_grad = act_grad + jnp.dot(rows, down_t[span, :], preferred_element_type=F32)
    gate_pre = gate_ref[...]
    sigmoid = jax.nn.sigmoid(gate_pre)
    gate_grad = (act_grad * up_ref[...] * sigmoid * (1.0 + gate_pre * (1.0 - sigmoid))).astype(BF16)
    up_grad = (act_grad * (gate_pre * sigmoid)).astype(BF16)
    gate_out[...] = gate_grad
    up_out[...] = up_grad
    spans = core_spans(cores, width, traced_partner)
    for part, span in zip(parts, spans[1:]):
        value = jnp.dot(gate_grad, gate_t[:, span], preferred_element_type=F32)
        value = value + jnp.dot(up_grad, up_t[:, span], preferred_element_type=F32)
        part[...] = value.astype(BF16)


def input_own_kernel(dims, *refs):
    gate_grad, up_grad, gate_t, up_t = refs[:4]
    span = core_spans(*dims, traced_partner)[0]
    value = jnp.dot(gate_grad[...], gate_t[:, span], preferred_element_type=F32)
    value = value + jnp.dot(up_grad[...], up_t[:, span], preferred_element_type=F32)
    refs[-1][...] = value.astype(BF16)


def down_kernel(dims, sizes, chunks, *refs):
    cores, width = dims
    groups = len(sizes)
    act_ref = refs[cores * groups]
    out_hbm, result, out_sems = refs[-3:]
    core = lax.axis_index("etp")
    act = act_ref[...].T
    chunk = width // chunks
    copies = []
    for d in range(cores):
        rows = array_rows(refs[d * groups : (d + 1) * groups], sizes, 1)
        base = traced_origin(core, d, cores) * width
        for n in range(chunks):
            slot = d * chunks + n
            value = jnp.dot(act, rows[:, n * chunk : (n + 1) * chunk], preferred_element_type=F32)
            result[slot] = value.astype(BF16)
            span = pl.ds(pl.multiple_of(base + n * chunk, chunk), chunk)
            copy = pltpu.make_async_copy(result.at[slot], out_hbm.at[0, :, span], out_sems.at[slot])
            copy.start()
            copies.append(copy)
    for copy in copies:
        copy.wait()


def split_kernel(dims, groups, *refs):
    cores, inner, reach = dims
    total = refs[0][...].astype(F32)
    for part in refs[1:cores]:
        total = total + part[...].astype(F32)
    half = total.shape[1] // 2
    fold = 2 * reach
    for q in range(inner):
        out = None
        first = 0
        base = 0
        for size, held in groups:
            rows = total[base + q * held : base + (q + 1) * held]
            for side in range(2):
                place = side * reach + first
                start = place // SUBLANES * SUBLANES
                frame = -(-(place - start + size) // SUBLANES) * SUBLANES
                part = rows[:, side * half : (side + 1) * half]
                part = part[:frame] if frame < held else padded(part, 0, frame - held)
                part = shifted(part, place - start)
                part = padded(part, start, fold - start - frame)
                out = part if out is None else out + part
            first += size
            base += inner * held
        refs[q - inner][...] = out.astype(BF16)


def combine_kernel(dims, weighted, *refs):
    outer, inner, unit = dims
    tables = refs[inner : inner + weighted]
    outs = refs[-outer:]
    rows = stacked(refs[:inner])
    total = None
    for table in tables:
        term = jnp.dot(table[...], rows, preferred_element_type=F32)
        total = term if total is None else total + term
    for b in range(outer):
        outs[b][...] = total[b * unit : (b + 1) * unit].astype(BF16)


def final_kernel(dims, *refs):
    outer, tokens, half = dims
    out_ref = refs[-2]
    total = refs[0][...].astype(F32)
    for part in refs[1:outer]:
        total = total + part[...].astype(F32)
    out_ref[:, :half] = total[:tokens].astype(BF16)
    out_ref[:, half:] = total[tokens:].astype(BF16)


def shape(rows, columns, kind=BF16):
    return jax.ShapeDtypeStruct((rows, columns), kind)


def on_device(hidden_in, expert_ids, gate_weights, out_grad, gate_weight, up_weight, down_weight):
    tokens, top = expert_ids.shape
    experts = lax.axis_size("expert")
    cores = lax.axis_size("etp")
    outer, inner = group_sizes(experts)
    cap = min(tokens, tokens * top // experts + 1)
    width = hidden_in.shape[1]
    half = width // 2
    hidden = gate_weight.shape[2]
    reach = outer * cap
    unit = 2 * tokens
    near = min(2, outer)
    groups = [g for g in (range(near), range(near, outer)) if len(g)]
    sizes = [(len(g) * cap, -(-len(g) * cap // 16) * 16) for g in groups]
    route_dims = (inner, tokens, top, cap, half)

    with jax.named_scope("prepare"):
        packed = pl.pallas_call(
            functools.partial(prepare_kernel, (tokens, top, half)),
            out_shape=shape(SUBLANES, 2 * unit // SUBLANES * half + META),
            in_specs=hbm_specs(4),
            out_specs=pl.BlockSpec(memory_space=pltpu.VMEM),
            scratch_shapes=[
                pltpu.VMEM((top, tokens), jnp.int32),
                pltpu.VMEM((top, tokens), F32),
                pltpu.VMEM((tokens, width), BF16),
                pltpu.VMEM((tokens, width), BF16),
                pltpu.SemaphoreType.DMA((4,)),
            ],
            compiler_params=params(),
            cost_estimate=cost("PREPARE"),
            name="prepare",
        )(in_hbm(expert_ids.T), in_hbm(gate_weights.T), in_hbm(hidden_in), in_hbm(out_grad))

    with jax.named_scope("gather_blocks"):
        blocks = [packed] + [send_outer(packed, s, outer, inner) for s in range(1, outer)]

    piece_shapes = [shape(2 * reach, half)] * inner
    table_shape = shape(outer * unit, inner * 2 * reach)
    token_shape = shape(8, META, F32)
    weights = [pltpu.with_memory_space_constraint(w, pltpu.VMEM) for w in (gate_weight, up_weight, down_weight)]
    dims = (cores, width)

    def route(g, after=()):
        members = [blocks[i] for i in groups[g]]
        size = sizes[g][0]
        return pl.pallas_call(
            functools.partial(route_kernel, route_dims, len(members), size),
            out_shape=[shape(4 * size, half)] * inner,
            in_specs=whole_specs(len(members) + len(after)),
            out_specs=whole_specs(inner),
            compiler_params=params(),
            cost_estimate=cost(f"ROUTE{g}"),
            name=f"route{g}",
        )(*members, *after)

    def spread(sends):
        return [sends[0]] + [send_inner(sends[q], q, outer, inner) for q in range(1, inner)]

    def gather_cores(g, pieces, after=()):
        size, held = sizes[g]
        stack = pl.pallas_call(
            functools.partial(stack_kernel, (inner, size, held)),
            out_shape=shape(2 * inner * held, width),
            in_specs=whole_specs(inner) + any_specs(len(after)),
            out_specs=pl.BlockSpec(memory_space=pltpu.VMEM),
            compiler_params=params(),
            cost_estimate=cost(f"STACK{g}"),
            name=f"stack{g}",
        )(*flipped(pieces), *after)
        return [stack] + [send_core(stack, d, cores) for d in range(1, cores)]

    with jax.named_scope("near_blocks"):
        sends = route(0)
        near_pieces = spread(sends)
    def turn(picked, after, name):
        return pl.pallas_call(
            functools.partial(turn_kernel, len(picked)),
            out_shape=[pltpu.VMEM((w.shape[2], w.shape[1]), BF16) for w in picked] + [token_shape],
            in_specs=whole_specs(len(picked)) + any_specs(1),
            out_specs=whole_specs(len(picked) + 1),
            compiler_params=params(),
            cost_estimate=cost(name.upper()),
            name=name,
        )(*picked, after)

    with jax.named_scope("turn_weights"):
        down_t, ready = turn(weights[2:], sends[0], "turn_down")
    with jax.named_scope("far_blocks"):
        far_pieces = [spread(route(g, (ready,))) for g in range(1, len(groups))]
    with jax.named_scope("turn_weights"):
        gate_t, up_t, turned = turn(weights[:2], (far_pieces or [near_pieces])[0][0], "turn_rest")
    with jax.named_scope("tables"):
        pick, gate_hi, gate_lo, listed = pl.pallas_call(
            functools.partial(tables_kernel, route_dims, outer, reach),
            out_shape=[table_shape] * 3 + [token_shape],
            in_specs=whole_specs(outer) + any_specs(1),
            out_specs=whole_specs(4),
            compiler_params=params(),
            cost_estimate=cost("TABLES"),
            name="tables",
        )(*blocks, sends[0])
    counts = [inner * held for _, held in sizes]
    rows = sum(counts)
    with jax.named_scope("gather_cores"):
        stacks = [gather_cores(0, near_pieces, [pieces[0] for pieces in far_pieces])]
        for g, pieces in enumerate(far_pieces, 1):
            stacks.append(gather_cores(g, pieces, (listed, turned)))
        own_stacks = [stack[0] for stack in stacks]
        other_stacks = [stack[d] for d in range(1, cores) for stack in stacks]

    with jax.named_scope("forward"):
        own = pl.pallas_call(
            functools.partial(forward_own_kernel, dims, counts),
            out_shape=[shape(rows, hidden, F32)] * 2,
            in_specs=whole_specs(len(counts) + 2),
            out_specs=whole_specs(2),
            compiler_params=params(),
            cost_estimate=cost("FORWARD_OWN"),
            name="forward_own",
        )(*own_stacks, *weights[:2])
        act_own = pl.pallas_call(
            functools.partial(backward_own_kernel, dims, counts),
            out_shape=shape(rows, hidden, F32),
            in_specs=whole_specs(len(counts) + 1),
            out_specs=pl.BlockSpec(memory_space=pltpu.VMEM),
            compiler_params=params(),
            cost_estimate=cost("BACKWARD_OWN"),
            name="backward_own",
        )(*own_stacks, down_t)
        gate_pre, up_pre, act, *out_parts = pl.pallas_call(
            functools.partial(forward_kernel, dims, counts),
            out_shape=[shape(rows, hidden, F32)] * 2 + [shape(rows, hidden)] + [shape(rows, width)] * cores,
            in_specs=whole_specs(5 + len(other_stacks)) + any_specs(1),
            out_specs=whole_specs(3 + cores),
            compiler_params=params(),
            cost_estimate=cost("FORWARD"),
            name="forward",
        )(*own, *weights, *other_stacks, act_own)

    def give_back(parts, after=()):
        got = [parts[0]] + [send_core(parts[d], d, cores) for d in range(1, cores)]
        sends = pl.pallas_call(
            functools.partial(split_kernel, (cores, inner, reach), sizes),
            out_shape=piece_shapes,
            in_specs=whole_specs(cores) + any_specs(len(after)),
            out_specs=whole_specs(inner),
            compiler_params=params(),
            name="split",
        )(*got, *after)
        return [sends[0]] + [send_inner(sends[q], q, outer, inner, back=True) for q in range(1, inner)]

    def combine(pieces, tables):
        blocks = pl.pallas_call(
            functools.partial(combine_kernel, (outer, inner, unit), len(tables)),
            out_shape=[shape(unit, half)] * outer,
            in_specs=whole_specs(inner + len(tables)),
            out_specs=whole_specs(outer),
            compiler_params=params(),
            name="combine",
        )(*pieces, *tables)
        return [blocks[0]] + [send_outer(blocks[s], s, outer, inner, back=True) for s in range(1, outer)]

    def finish(blocks, after=()):
        return pl.pallas_call(
            functools.partial(final_kernel, (outer, tokens, half)),
            out_shape=[shape(tokens, width), shape(8, META, F32)],
            in_specs=whole_specs(outer + len(after)),
            out_specs=whole_specs(2),
            compiler_params=params(),
            name="final",
        )(*flipped(blocks), *after)

    with jax.named_scope("return_out"):
        out_back = give_back(out_parts)
        out_blocks = combine(out_back, (gate_hi, gate_lo))

    with jax.named_scope("backward"):
        gate_grad, up_grad, *grad_parts = pl.pallas_call(
            functools.partial(backward_kernel, dims, counts),
            out_shape=[shape(rows, hidden)] * 2 + [shape(rows, width)] * (cores - 1),
            in_specs=whole_specs(6 + len(other_stacks)),
            out_specs=whole_specs(cores + 1),
            compiler_params=params(),
            cost_estimate=cost("BACKWARD"),
            name="backward",
        )(act_own, gate_t, up_t, down_t, gate_pre, up_pre, *other_stacks)
        own_part = pl.pallas_call(
            functools.partial(input_own_kernel, dims),
            out_shape=shape(rows, width),
            in_specs=whole_specs(4) + any_specs(1),
            out_specs=pl.BlockSpec(memory_space=pltpu.VMEM),
            compiler_params=params(),
            cost_estimate=cost("INPUT_OWN"),
            name="input_own",
        )(gate_grad, up_grad, gate_t, up_t, out_back[0])
        grad_parts = [own_part, *grad_parts]

    with jax.named_scope("return_grad"):
        back_blocks = combine(give_back(grad_parts, out_back[:1]), (pick,))

    with jax.named_scope("down_grad"):
        chunks = max(1, width // 512)
        down_grad = pl.pallas_call(
            functools.partial(down_kernel, dims, counts, chunks),
            out_shape=pltpu.HBM(down_weight.shape, BF16),
            in_specs=whole_specs(cores * len(groups) + 1) + any_specs(1),
            out_specs=pl.BlockSpec(memory_space=pltpu.HBM),
            scratch_shapes=[
                pltpu.VMEM((cores * chunks, hidden, width // chunks), BF16),
                pltpu.SemaphoreType.DMA((cores * chunks,)),
            ],
            compiler_params=params(),
            name="down_grad",
        )(*own_stacks, *other_stacks, act, back_blocks[0])

    mixed_out, done = finish(out_blocks)
    input_grad, done = finish(back_blocks, (done,))
    return (mixed_out, input_grad, down_grad)


def solution(mesh):
    return jax.shard_map(
        on_device,
        mesh=mesh,
        in_specs=(
            P("expert", "etp"),
            P("expert", None),
            P("expert", None),
            P("expert", "etp"),
            P("expert", None, "etp"),
            P("expert", None, "etp"),
            P("expert", "etp", None),
        ),
        out_specs=(P("expert", "etp"), P("expert", "etp"), P("expert", "etp", None)),
        check_vma=False,
    )
```

```python
import functools
import jax
import jax.numpy as jnp
from jax import lax
from jax.experimental import pallas as pl
from jax.experimental.pallas import tpu as pltpu
from jax.sharding import PartitionSpec as P

BF16 = jnp.bfloat16
F32 = jnp.float32
META = 128
COSTS = {"PREPARE": 20, "ROUTE0": 9, "ROUTE1": 9, "TURN_REST": 3}
SUBLANES = 8
VMEM_LIMIT = 20 * 1024 * 1024


def group_sizes(experts):
    inner = 1
    while inner * inner * 4 <= experts and experts % (inner * 2) == 0:
        inner *= 2
    return experts // inner, inner


def partner(index, step, size):
    return index ^ step if size & (size - 1) == 0 else (index + step) % size


def origin(index, step, size):
    return index ^ step if size & (size - 1) == 0 else (index - step) % size


def traced_partner(index, step, size):
    return index ^ step if size & (size - 1) == 0 else lax.rem(index + step, size)


def traced_origin(index, step, size):
    return index ^ step if size & (size - 1) == 0 else lax.rem(index + size - step, size)


def send_outer(x, step, outer, inner, back=False):
    move = origin if back else partner
    pairs = [
        (a * inner + b, move(a, step, outer) * inner + b) for a in range(outer) for b in range(inner)
    ]
    return lax.ppermute(x, "expert", pairs)


def send_inner(x, step, outer, inner, back=False):
    move = origin if back else partner
    pairs = [
        (a * inner + b, a * inner + move(b, step, inner)) for a in range(outer) for b in range(inner)
    ]
    return lax.ppermute(x, "expert", pairs)


def send_core(x, step, cores, back=False):
    move = origin if back else partner
    return lax.ppermute(x, "etp", [(i, move(i, step, cores)) for i in range(cores)])


def flipped(parts):
    return [parts[0], *parts[:0:-1]]


def contract(left, right, left_dim, right_dim):
    return lax.dot_general(
        left, right, (((left_dim,), (right_dim,)), ((), ())), preferred_element_type=F32
    )


def whole_specs(count):
    return [pl.BlockSpec(memory_space=pltpu.VMEM)] * count


def any_specs(count):
    return [pl.BlockSpec(memory_space=pl.ANY)] * count


def cost(name):
    return pl.CostEstimate(flops=int(COSTS.get(name, 0) * 1e9) + 1, bytes_accessed=1, transcendentals=0)


def params():
    return pltpu.CompilerParams(vmem_limit_bytes=VMEM_LIMIT)


def in_hbm(x):
    return pltpu.with_memory_space_constraint(x, pltpu.HBM)


def hbm_specs(count):
    return [pl.BlockSpec(memory_space=pltpu.HBM)] * count


def prepare_kernel(dims, *refs):
    tokens, top, half = dims
    sources, out_ref, held, sems = refs[:4], refs[4], refs[5:9], refs[9]
    copies = [pltpu.make_async_copy(a, b, sems.at[n]) for n, (a, b) in enumerate(zip(sources, held))]
    for copy in copies:
        copy.start()
    for copy in copies:
        copy.wait()
    ids_ref, gates_ref, hidden_ref, grad_ref = held
    gates = gates_ref[...]
    gate_hi = gates.astype(BF16)
    rest = gates - gate_hi.astype(F32)
    gate_mid = rest.astype(BF16)
    gate_lo = rest - gate_mid.astype(F32)
    values = [ids_ref[...].astype(F32), gate_hi.astype(F32), gate_mid.astype(F32), gate_lo]
    values = jnp.concatenate(values, axis=0).astype(BF16)
    entry = lax.broadcasted_iota(jnp.int32, (4 * top, META), 0)
    lane = lax.broadcasted_iota(jnp.int32, (4 * top, META), 1)
    meta = contract(values, (lane == entry).astype(F32).astype(BF16), 0, 0)
    meta = jnp.concatenate([meta, meta], axis=0)
    tiles = 2 * tokens // SUBLANES
    for n, source in enumerate((hidden_ref, grad_ref)):
        value = source[...].astype(F32)
        value = jnp.concatenate([value[:, :half], value[:, half:]], axis=0)
        for i in range(tiles):
            start = (n * tiles + i) * half
            out_ref[:, start : start + half] = value[i * SUBLANES : (i + 1) * SUBLANES].astype(BF16)
    packed = meta[:SUBLANES]
    for i in range(1, tiles):
        packed = packed + pltpu.roll(meta[i * SUBLANES : (i + 1) * SUBLANES], i * 4 * top, 1)
    out_ref[:, 2 * tiles * half :] = packed.astype(BF16)


def block_rows(blocks, start, width, tiles, shift=0):
    parts = []
    for block in blocks:
        for i in range(tiles):
            if shift:
                part = block[:, start : start + width].astype(F32)
                parts.append(pltpu.roll(part, width - i * shift, 1) if i else part)
            else:
                parts.append(block[:, start + i * width : start + (i + 1) * width].astype(F32))
    return jnp.concatenate(parts, axis=0)


def stacked(refs):
    return jnp.concatenate([r[...].astype(F32) for r in refs], axis=0).astype(BF16)


def count_above(index, unit, total):
    value = jnp.zeros_like(index)
    for m in range(unit, total, unit):
        value = value + (index >= m).astype(jnp.int32)
    return value


def routing(blocks, fold, dims):
    inner, tokens, top, cap, half = dims
    tiles = 2 * tokens // SUBLANES
    rows = len(blocks) * 2 * tokens
    shape = (rows, inner * fold)
    me = lax.axis_index("expert")
    my_inner = lax.rem(me, inner)
    my_base = me - my_inner
    lane = lax.broadcasted_iota(jnp.int32, (1, shape[1]), 1)
    step = count_above(lane, fold, shape[1])
    dest = jnp.zeros(lane.shape, F32)
    for q in range(inner):
        expert = (my_base + traced_partner(my_inner, q, inner)).astype(F32)
        dest = jnp.where(step == q, expert, dest)
    meta = block_rows(blocks, 2 * tiles * half, META, tiles, 4 * top)
    weights = meta + pltpu.roll(meta, META - top, 1) + pltpu.roll(meta, META - 2 * top, 1)
    named = jnp.zeros(shape, F32)
    gate = jnp.zeros(shape, F32)
    for k in range(top):
        hit = meta[:, k : k + 1] == dest
        value = weights[:, top + k : top + k + 1]
        named = jnp.where(hit, 1.0, named)
        gate = jnp.where(hit, value, gate)
    left = lax.broadcasted_iota(jnp.int32, (rows, rows), 1)
    down = lax.broadcasted_iota(jnp.int32, (rows, rows), 0)
    same = count_above(left, tokens, rows) == count_above(down, tokens, rows)
    before = (same & (left < down)).astype(F32).astype(BF16)
    rank = jnp.dot(before, named.astype(BF16), preferred_element_type=F32)
    row = lax.broadcasted_iota(jnp.int32, (rows, 1), 0)
    block = count_above(row, 2 * tokens, rows)
    row_side = count_above(row, tokens, rows) - 2 * block
    position = block * cap + rank.astype(jnp.int32)
    return lane - step * fold, named, gate, position, row_side


def gate_parts(gate):
    gate_hi = gate.astype(BF16)
    rest = gate - gate_hi.astype(F32)
    gate_mid = rest.astype(BF16)
    return gate_hi, gate_mid, (rest - gate_mid.astype(F32)).astype(BF16)


def route_kernel(dims, count, reach, *refs):
    inner, tokens, top, cap, half = dims
    blocks = refs[:count]
    sends = refs[-inner:]
    fold = 4 * reach
    tiles = 2 * tokens // SUBLANES
    lane, named, gate, position, row_side = routing(blocks, fold, dims)
    segment = count_above(lane, reach, fold)
    grads = segment >= 2
    side = segment - 2 * grads.astype(jnp.int32)
    pick = jnp.where((position == lane - segment * reach) & (row_side == side), named, 0.0)
    ones = jnp.ones((pick.shape[0], META), BF16)
    column = sum(contract(part, ones, 0, 0) for part in gate_parts(pick * jnp.where(grads, gate, 1.0)))
    chosen = jnp.concatenate([jnp.where(grads, 0.0, pick), jnp.where(grads, pick, 0.0)], axis=0).astype(BF16)
    table = [block_rows(blocks, n * tiles * half, half, tiles) for n in range(2)]
    out = contract(chosen, jnp.concatenate(table, axis=0).astype(BF16), 0, 0) * column[:, :1]
    for q, send in enumerate(sends):
        send[...] = out[q * fold : (q + 1) * fold].astype(BF16)


def tables_kernel(dims, count, reach, *refs):
    pick_ref, gate_hi_ref, gate_mid_ref, _ = refs[-4:]
    lane, named, gate, position, row_side = routing(refs[:count], 2 * reach, dims)
    side = (lane >= reach).astype(jnp.int32)
    pick = jnp.where((position == lane - side * reach) & (row_side == side), named, 0.0)
    pick_ref[...] = pick.astype(BF16)
    gate_hi_ref[...], gate_mid_ref[...], _ = gate_parts(pick * gate)


def shifted(rows, shift):
    return pltpu.roll(rows, shift % rows.shape[0], 0) if shift else rows


def padded(rows, before, after):
    parts = [rows]
    if before:
        parts.insert(0, jnp.zeros((before, rows.shape[1]), F32))
    if after:
        parts.append(jnp.zeros((after, rows.shape[1]), F32))
    return jnp.concatenate(parts, axis=0) if len(parts) > 1 else rows


def stack_kernel(dims, *refs):
    inner, reach, held = dims
    half = refs[0].shape[1]
    rows = inner * held
    live = lax.broadcasted_iota(jnp.int32, (held, half), 0) < reach
    for q, piece in enumerate(flipped(refs[:inner])):
        values = piece[...].astype(F32)
        for segment in range(4):
            array, side = divmod(segment, 2)
            start = segment * reach // SUBLANES * SUBLANES
            shift = segment * reach - start
            frame = -(-(shift + reach) // SUBLANES) * SUBLANES
            part = shifted(values[start : start + frame], -shift)
            part = part[:held] if frame > held else padded(part, 0, held - frame)
            first = array * rows + q * held
            target = refs[-1].at[first : first + held, side * half : (side + 1) * half]
            target[...] = jnp.where(live, part, 0.0).astype(BF16)


def turn_kernel(count, *refs):
    for source, target in zip(refs[:count], refs[count + 1 : -1]):
        target[...] = source[0].T


def core_spans(cores, width, move):
    core = lax.axis_index("etp")
    return [pl.ds(pl.multiple_of(move(core, d, cores) * width, width), width) for d in range(cores)]


def array_rows(stacks, sizes, array):
    return jnp.concatenate([s[array * n : (array + 1) * n, :] for s, n in zip(stacks, sizes)], axis=0)


def forward_own_kernel(dims, sizes, *refs):
    gate_w, up_w, gate_ref, up_ref = refs[len(sizes) :]
    rows = array_rows(refs, sizes, 0)
    span = core_spans(*dims, traced_origin)[0]
    gate_ref[...] = jnp.dot(rows, gate_w[0, span, :], preferred_element_type=F32)
    up_ref[...] = jnp.dot(rows, up_w[0, span, :], preferred_element_type=F32)


def forward_kernel(dims, sizes, *refs):
    cores, width = dims
    groups = len(sizes)
    gate_own, up_own, gate_w, up_w, down_w, *stacks = refs[: 5 + groups * (cores - 1)]
    gate_ref, up_ref, act_ref, *parts = refs[-(3 + cores) :]
    spans = core_spans(cores, width, traced_origin)
    gate_pre = gate_own[...]
    up_pre = up_own[...]
    for n, span in enumerate(spans[1:]):
        rows = array_rows(stacks[n * groups : (n + 1) * groups], sizes, 0)
        gate_pre = gate_pre + jnp.dot(rows, gate_w[0, span, :], preferred_element_type=F32)
        up_pre = up_pre + jnp.dot(rows, up_w[0, span, :], preferred_element_type=F32)
    act = (gate_pre * jax.nn.sigmoid(gate_pre) * up_pre).astype(BF16)
    gate_ref[...] = gate_pre
    up_ref[...] = up_pre
    act_ref[...] = act
    spans = core_spans(cores, width, traced_partner)
    for d in reversed(range(cores)):
        parts[d][...] = jnp.dot(act, down_w[0, :, spans[d]], preferred_element_type=F32).astype(BF16)


def backward_own_kernel(dims, sizes, *refs):
    down_t, out_ref = refs[len(sizes)], refs[-1]
    rows = array_rows(refs, sizes, 1)
    span = core_spans(*dims, traced_origin)[0]
    out_ref[...] = jnp.dot(rows, down_t[span, :], preferred_element_type=F32)


def backward_kernel(dims, sizes, *refs):
    cores, width = dims
    groups = len(sizes)
    act_own, gate_t, up_t, down_t, gate_ref, up_ref, *stacks = refs[: 6 + groups * (cores - 1)]
    gate_out, up_out, *parts = refs[-(cores + 1) :]
    spans = core_spans(cores, width, traced_origin)
    act_grad = act_own[...]
    for n, span in enumerate(spans[1:]):
        rows = array_rows(stacks[n * groups : (n + 1) * groups], sizes, 1)
        act_grad = act_grad + jnp.dot(rows, down_t[span, :], preferred_element_type=F32)
    gate_pre = gate_ref[...]
    sigmoid = jax.nn.sigmoid(gate_pre)
    gate_grad = (act_grad * up_ref[...] * sigmoid * (1.0 + gate_pre * (1.0 - sigmoid))).astype(BF16)
    up_grad = (act_grad * (gate_pre * sigmoid)).astype(BF16)
    gate_out[...] = gate_grad
    up_out[...] = up_grad
    spans = core_spans(cores, width, traced_partner)
    for part, span in zip(parts, spans[1:]):
        value = jnp.dot(gate_grad, gate_t[:, span], preferred_element_type=F32)
        value = value + jnp.dot(up_grad, up_t[:, span], preferred_element_type=F32)
        part[...] = value.astype(BF16)


def input_own_kernel(dims, *refs):
    gate_grad, up_grad, gate_t, up_t = refs[:4]
    span = core_spans(*dims, traced_partner)[0]
    value = jnp.dot(gate_grad[...], gate_t[:, span], preferred_element_type=F32)
    value = value + jnp.dot(up_grad[...], up_t[:, span], preferred_element_type=F32)
    refs[-1][...] = value.astype(BF16)


def down_kernel(dims, sizes, chunks, *refs):
    cores, width = dims
    groups = len(sizes)
    act_ref = refs[cores * groups]
    out_hbm, result, out_sems = refs[-3:]
    core = lax.axis_index("etp")
    act = act_ref[...].T
    chunk = width // chunks
    copies = []
    for d in range(cores):
        rows = array_rows(refs[d * groups : (d + 1) * groups], sizes, 1)
        base = traced_origin(core, d, cores) * width
        for n in range(chunks):
            slot = d * chunks + n
            value = jnp.dot(act, rows[:, n * chunk : (n + 1) * chunk], preferred_element_type=F32)
            result[slot] = value.astype(BF16)
            span = pl.ds(pl.multiple_of(base + n * chunk, chunk), chunk)
            copy = pltpu.make_async_copy(result.at[slot], out_hbm.at[0, :, span], out_sems.at[slot])
            copy.start()
            copies.append(copy)
    for copy in copies:
        copy.wait()


def split_kernel(dims, groups, *refs):
    cores, inner, reach = dims
    total = refs[0][...].astype(F32)
    for part in refs[1:cores]:
        total = total + part[...].astype(F32)
    half = total.shape[1] // 2
    fold = 2 * reach
    for q in range(inner):
        out = None
        first = 0
        base = 0
        for size, held in groups:
            rows = total[base + q * held : base + (q + 1) * held]
            for side in range(2):
                place = side * reach + first
                start = place // SUBLANES * SUBLANES
                frame = -(-(place - start + size) // SUBLANES) * SUBLANES
                part = rows[:, side * half : (side + 1) * half]
                part = part[:frame] if frame < held else padded(part, 0, frame - held)
                part = shifted(part, place - start)
                part = padded(part, start, fold - start - frame)
                out = part if out is None else out + part
            first += size
            base += inner * held
        refs[q - inner][...] = out.astype(BF16)


def combine_kernel(dims, weighted, *refs):
    outer, inner, unit = dims
    tables = refs[inner : inner + weighted]
    outs = refs[-outer:]
    rows = stacked(refs[:inner])
    total = None
    for table in tables:
        term = jnp.dot(table[...], rows, preferred_element_type=F32)
        total = term if total is None else total + term
    for b in range(outer):
        outs[b][...] = total[b * unit : (b + 1) * unit].astype(BF16)


def final_kernel(dims, *refs):
    outer, tokens, half, place = dims
    out_ref = refs[place]
    total = refs[0][...].astype(F32)
    for part in refs[1:outer]:
        total = total + part[...].astype(F32)
    out_ref[:, :half] = total[:tokens].astype(BF16)
    out_ref[:, half:] = total[tokens:].astype(BF16)


def shape(rows, columns, kind=BF16):
    return jax.ShapeDtypeStruct((rows, columns), kind)


def on_device(hidden_in, expert_ids, gate_weights, out_grad, gate_weight, up_weight, down_weight):
    tokens, top = expert_ids.shape
    experts = lax.axis_size("expert")
    cores = lax.axis_size("etp")
    outer, inner = group_sizes(experts)
    cap = min(tokens, tokens * top // experts + 1)
    width = hidden_in.shape[1]
    half = width // 2
    hidden = gate_weight.shape[2]
    reach = outer * cap
    unit = 2 * tokens
    near = min(2, outer)
    groups = [g for g in (range(near), range(near, outer)) if len(g)]
    sizes = [(len(g) * cap, -(-len(g) * cap // 16) * 16) for g in groups]
    route_dims = (inner, tokens, top, cap, half)

    with jax.named_scope("prepare"):
        packed = pl.pallas_call(
            functools.partial(prepare_kernel, (tokens, top, half)),
            out_shape=shape(SUBLANES, 2 * unit // SUBLANES * half + META),
            in_specs=hbm_specs(4),
            out_specs=pl.BlockSpec(memory_space=pltpu.VMEM),
            scratch_shapes=[
                pltpu.VMEM((top, tokens), jnp.int32),
                pltpu.VMEM((top, tokens), F32),
                pltpu.VMEM((tokens, width), BF16),
                pltpu.VMEM((tokens, width), BF16),
                pltpu.SemaphoreType.DMA((4,)),
            ],
            compiler_params=params(),
            cost_estimate=cost("PREPARE"),
            name="prepare",
        )(in_hbm(expert_ids.T), in_hbm(gate_weights.T), in_hbm(hidden_in), in_hbm(out_grad))

    with jax.named_scope("gather_blocks"):
        blocks = [packed] + [send_outer(packed, s, outer, inner) for s in range(1, outer)]

    piece_shapes = [shape(2 * reach, half)] * inner
    table_shape = shape(outer * unit, inner * 2 * reach)
    token_shape = shape(8, META, F32)
    weights = [pltpu.with_memory_space_constraint(w, pltpu.VMEM) for w in (gate_weight, up_weight, down_weight)]
    dims = (cores, width)

    def route(g, after=()):
        members = [blocks[i] for i in groups[g]]
        size = sizes[g][0]
        return pl.pallas_call(
            functools.partial(route_kernel, route_dims, len(members), size),
            out_shape=[shape(4 * size, half)] * inner,
            in_specs=whole_specs(len(members) + len(after)),
            out_specs=whole_specs(inner),
            compiler_params=params(),
            cost_estimate=cost(f"ROUTE{g}"),
            name=f"route{g}",
        )(*members, *after)

    def spread(sends):
        return [sends[0]] + [send_inner(sends[q], q, outer, inner) for q in range(1, inner)]

    def gather_cores(g, pieces, after=()):
        size, held = sizes[g]
        stack = pl.pallas_call(
            functools.partial(stack_kernel, (inner, size, held)),
            out_shape=shape(2 * inner * held, width),
            in_specs=whole_specs(inner) + any_specs(len(after)),
            out_specs=pl.BlockSpec(memory_space=pltpu.VMEM),
            compiler_params=params(),
            cost_estimate=cost(f"STACK{g}"),
            name=f"stack{g}",
        )(*flipped(pieces), *after)
        return [stack] + [send_core(stack, d, cores) for d in range(1, cores)]

    with jax.named_scope("near_blocks"):
        sends = route(0)
        near_pieces = spread(sends)
    def turn(picked, after, name):
        return pl.pallas_call(
            functools.partial(turn_kernel, len(picked)),
            out_shape=[pltpu.VMEM((w.shape[2], w.shape[1]), BF16) for w in picked] + [token_shape],
            in_specs=whole_specs(len(picked)) + any_specs(1),
            out_specs=whole_specs(len(picked) + 1),
            compiler_params=params(),
            cost_estimate=cost(name.upper()),
            name=name,
        )(*picked, after)

    with jax.named_scope("turn_weights"):
        down_t, ready = turn(weights[2:], sends[0], "turn_down")
    with jax.named_scope("far_blocks"):
        far_pieces = [spread(route(g, (ready,))) for g in range(1, len(groups))]
    with jax.named_scope("turn_weights"):
        gate_t, up_t, turned = turn(weights[:2], (far_pieces or [near_pieces])[0][0], "turn_rest")
    with jax.named_scope("tables"):
        pick, gate_hi, gate_lo, listed = pl.pallas_call(
            functools.partial(tables_kernel, route_dims, outer, reach),
            out_shape=[table_shape] * 3 + [token_shape],
            in_specs=whole_specs(outer) + any_specs(1),
            out_specs=whole_specs(4),
            compiler_params=params(),
            cost_estimate=cost("TABLES"),
            name="tables",
        )(*blocks, sends[0])
    counts = [inner * held for _, held in sizes]
    rows = sum(counts)
    with jax.named_scope("gather_cores"):
        stacks = [gather_cores(0, near_pieces, [pieces[0] for pieces in far_pieces])]
        for g, pieces in enumerate(far_pieces, 1):
            stacks.append(gather_cores(g, pieces, (listed, turned)))
        own_stacks = [stack[0] for stack in stacks]
        other_stacks = [stack[d] for d in range(1, cores) for stack in stacks]

    with jax.named_scope("forward"):
        own = pl.pallas_call(
            functools.partial(forward_own_kernel, dims, counts),
            out_shape=[shape(rows, hidden, F32)] * 2,
            in_specs=whole_specs(len(counts) + 2),
            out_specs=whole_specs(2),
            compiler_params=params(),
            cost_estimate=cost("FORWARD_OWN"),
            name="forward_own",
        )(*own_stacks, *weights[:2])
        act_own = pl.pallas_call(
            functools.partial(backward_own_kernel, dims, counts),
            out_shape=shape(rows, hidden, F32),
            in_specs=whole_specs(len(counts) + 1),
            out_specs=pl.BlockSpec(memory_space=pltpu.VMEM),
            compiler_params=params(),
            cost_estimate=cost("BACKWARD_OWN"),
            name="backward_own",
        )(*own_stacks, down_t)
        gate_pre, up_pre, act, *out_parts = pl.pallas_call(
            functools.partial(forward_kernel, dims, counts),
            out_shape=[shape(rows, hidden, F32)] * 2 + [shape(rows, hidden)] + [shape(rows, width)] * cores,
            in_specs=whole_specs(5 + len(other_stacks)) + any_specs(1),
            out_specs=whole_specs(3 + cores),
            compiler_params=params(),
            cost_estimate=cost("FORWARD"),
            name="forward",
        )(*own, *weights, *other_stacks, act_own)

    def give_back(parts, after=()):
        got = [parts[0]] + [send_core(parts[d], d, cores) for d in range(1, cores)]
        sends = pl.pallas_call(
            functools.partial(split_kernel, (cores, inner, reach), sizes),
            out_shape=piece_shapes,
            in_specs=whole_specs(cores) + any_specs(len(after)),
            out_specs=whole_specs(inner),
            compiler_params=params(),
            name="split",
        )(*got, *after)
        return [sends[0]] + [send_inner(sends[q], q, outer, inner, back=True) for q in range(1, inner)]

    def combine(pieces, tables):
        blocks = pl.pallas_call(
            functools.partial(combine_kernel, (outer, inner, unit), len(tables)),
            out_shape=[shape(unit, half)] * outer,
            in_specs=whole_specs(inner + len(tables)),
            out_specs=whole_specs(outer),
            compiler_params=params(),
            name="combine",
        )(*pieces, *tables)
        return [blocks[0]] + [send_outer(blocks[s], s, outer, inner, back=True) for s in range(1, outer)]

    def finish(blocks, after=()):
        return pl.pallas_call(
            functools.partial(final_kernel, (outer, tokens, half, -1 if after else -2)),
            out_shape=[shape(tokens, width)] + ([] if after else [shape(8, META, F32)]),
            in_specs=whole_specs(outer + len(after)),
            out_specs=whole_specs(1 if after else 2),
            compiler_params=params(),
            name="final",
        )(*flipped(blocks), *after)

    with jax.named_scope("return_out"):
        out_back = give_back(out_parts)
        out_blocks = combine(out_back, (gate_hi, gate_lo))

    with jax.named_scope("backward"):
        gate_grad, up_grad, *grad_parts = pl.pallas_call(
            functools.partial(backward_kernel, dims, counts),
            out_shape=[shape(rows, hidden)] * 2 + [shape(rows, width)] * (cores - 1),
            in_specs=whole_specs(6 + len(other_stacks)),
            out_specs=whole_specs(cores + 1),
            compiler_params=params(),
            cost_estimate=cost("BACKWARD"),
            name="backward",
        )(act_own, gate_t, up_t, down_t, gate_pre, up_pre, *other_stacks)
        own_part = pl.pallas_call(
            functools.partial(input_own_kernel, dims),
            out_shape=shape(rows, width),
            in_specs=whole_specs(4) + any_specs(1),
            out_specs=pl.BlockSpec(memory_space=pltpu.VMEM),
            compiler_params=params(),
            cost_estimate=cost("INPUT_OWN"),
            name="input_own",
        )(gate_grad, up_grad, gate_t, up_t, out_back[0])
        grad_parts = [own_part, *grad_parts]

    with jax.named_scope("return_grad"):
        back_blocks = combine(give_back(grad_parts, out_back[:1]), (pick,))

    with jax.named_scope("down_grad"):
        chunks = max(1, width // 512)
        down_grad = pl.pallas_call(
            functools.partial(down_kernel, dims, counts, chunks),
            out_shape=pltpu.HBM(down_weight.shape, BF16),
            in_specs=whole_specs(cores * len(groups) + 1) + any_specs(1),
            out_specs=pl.BlockSpec(memory_space=pltpu.HBM),
            scratch_shapes=[
                pltpu.VMEM((cores * chunks, hidden, width // chunks), BF16),
                pltpu.SemaphoreType.DMA((cores * chunks,)),
            ],
            compiler_params=params(),
            name="down_grad",
        )(*own_stacks, *other_stacks, act, back_blocks[0])

    mixed_out, done = finish(out_blocks)
    (input_grad,) = finish(back_blocks, (done,))
    return (mixed_out, input_grad, down_grad)


def solution(mesh):
    return jax.shard_map(
        on_device,
        mesh=mesh,
        in_specs=(
            P("expert", "etp"),
            P("expert", None),
            P("expert", None),
            P("expert", "etp"),
            P("expert", None, "etp"),
            P("expert", None, "etp"),
            P("expert", "etp", None),
        ),
        out_specs=(P("expert", "etp"), P("expert", "etp"), P("expert", "etp", None)),
        check_vma=False,
    )
```
